32 devices in a mesh: frame: 4 (over x, core), height: 4 (over z), width: 2 (over y).
Axes of the slice: x: 2, y: 2, z: 4, core: 2. Of those that a mesh axis runs over, the one named last changes fastest.
Arguments:
- queries: bfloat16 [16, 24, 16, 128], P('frame', 'height', 'width'), may hold values from -8 to 8
- key_vectors: bfloat16 [16, 24, 16, 128], P('frame', 'height', 'width'), may hold values from -8 to 8
- value_vectors: bfloat16 [16, 24, 16, 128], P('frame', 'height', 'width'), may hold values from -24 to 24
- out_weight: bfloat16 [128, 3072], replicated, may hold values from -0.5 to 0.5
- projected_grad: bfloat16 [16, 24, 16, 3072], P('frame', 'height', 'width'), may hold values from -6 to 6
Outputs:
- projected: bfloat16 [16, 24, 16, 3072], P('frame', 'height', 'width')
- grad_query: bfloat16 [16, 24, 16, 128], P('frame', 'height', 'width')
- grad_key: bfloat16 [16, 24, 16, 128], P('frame', 'height', 'width')
- grad_value: bfloat16 [16, 24, 16, 128], P('frame', 'height', 'width')
- grad_out_weight: float32 [128, 3072], replicated
The draws below stay inside these ranges and needn't reach their ends.
All inputs are finite; a program needn't handle non-finite values.
Results may differ from the reference program's by a relative error of at most 0.023.
Values may be sent and summed in bfloat16 or wider, within the bound.
No kernel may reach another device: no remote copies, remote signals or barrier semaphores. Data moves between devices by JAX's collectives and lax.ppermute only.
A program may use at most 128 MiB of HBM per device.

```python
import math
import jax
import jax.numpy as jnp
from jax import lax

TILE_F = 4
TILE_H = 6
TILE_W = 8
HEAD_DIM = 128
MODEL_DIM = 3072
FRAMES = 16
HEIGHT = 24
WIDTH = 16
N_FRAME = 4
N_HEIGHT = 4
N_WIDTH = 2


def draw_queries(key, part):
    own_key = jax.random.fold_in(key, 11)
    return jnp.clip(1.5 * jax.random.normal(own_key, (FRAMES, HEIGHT, WIDTH, HEAD_DIM), jnp.float32), -8.0, 8.0).astype(jnp.bfloat16)


def draw_key_vectors(key, part):
    own_key = jax.random.fold_in(key, 23)
    return jnp.clip(1.5 * jax.random.normal(own_key, (FRAMES, HEIGHT, WIDTH, HEAD_DIM), jnp.float32), -8.0, 8.0).astype(jnp.bfloat16)


def block_levels(stream_key, dims, cuts, smallest, high):
    def one(dim, shards_of):
        steps = jax.random.uniform(jax.random.fold_in(jax.random.fold_in(stream_key, 6), dim), (shards_of,), jnp.float32, smallest / len(cuts), high / len(cuts))
        return jnp.repeat(jnp.exp(steps), dims[dim] // shards_of).reshape((-1,) + (1,) * (len(dims) - dim - 1))

    factor_of = one(*cuts[0])
    for cut in cuts[1:]:
        factor_of = factor_of * one(*cut)
    return factor_of


def scatter_about(stream_key, dims, scale, reach, cuts=(), kind=jnp.bfloat16):
    level = block_levels(stream_key, dims, cuts, -0.22, 0.18) if cuts else 1.0
    drawn = jax.random.normal(stream_key, dims, jnp.float32) * scale * level
    return jnp.minimum(jnp.maximum(drawn, -reach), reach).astype(kind)


def setup_inputs(seed: int = 0) -> dict:
    seeds = jax.random.split(jax.random.key(seed), 6)
    queries = draw_queries(jax.random.fold_in(seeds[5], 71), 0)
    key_vectors = draw_key_vectors(jax.random.fold_in(seeds[5], 71), 0)
    value_vectors = scatter_about(seeds[2], (FRAMES, HEIGHT, WIDTH, HEAD_DIM), 4.0, 24.0, ((0, 4), (1, 4), (2, 2)))
    out_weight = scatter_about(seeds[3], (HEAD_DIM, MODEL_DIM), HEAD_DIM ** -0.5, 0.5)
    projected_grad = scatter_about(seeds[4], (FRAMES, HEIGHT, WIDTH, MODEL_DIM), 1.0, 6.0, ((0, 4), (1, 4), (2, 2)))
    return dict(queries=queries, key_vectors=key_vectors, value_vectors=value_vectors, out_weight=out_weight, projected_grad=projected_grad)


def window_start(position, extent):
    return jnp.maximum(jnp.minimum(position - 1, extent - 3), 0)

def to_bfloat(value):
    return lax.optimization_barrier(value.astype(jnp.bfloat16)).astype(jnp.float32)

def product(left, right):
    return jnp.dot(left, right, precision=lax.Precision.HIGHEST, preferred_element_type=jnp.float32)

def tiles_to_grid(tiled, last_dim):
    shaped = tiled.reshape(N_FRAME, N_HEIGHT, N_WIDTH, TILE_F, TILE_H, TILE_W, last_dim)
    return shaped.transpose(0, 3, 1, 4, 2, 5, 6).reshape(FRAMES, HEIGHT, WIDTH, last_dim)

def reference(queries, key_vectors, value_vectors, out_weight, projected_grad):
    inv_root = 1.0 / math.sqrt(HEAD_DIM)
    frame_span = min(3, N_FRAME)
    height_span = min(3, N_HEIGHT)
    width_span = min(3, N_WIDTH)
    key_shape = (frame_span * TILE_F, height_span * TILE_H, width_span * TILE_W, HEAD_DIM)
    tile_shape = (TILE_F, TILE_H, TILE_W)
    weight_full = out_weight.astype(jnp.float32)
    anchor = jnp.zeros((), jnp.int32)

    def one_tile(accumulators, tile_flat):
        key_acc, value_acc, weight_acc = accumulators
        frame_tile = tile_flat // (N_HEIGHT * N_WIDTH)
        height_tile = tile_flat // N_WIDTH % N_HEIGHT
        width_tile = tile_flat % N_WIDTH
        corner = (frame_tile * TILE_F, height_tile * TILE_H, width_tile * TILE_W, anchor)
        window_corner = (window_start(frame_tile, N_FRAME) * TILE_F, window_start(height_tile, N_HEIGHT) * TILE_H, window_start(width_tile, N_WIDTH) * TILE_W, anchor)
        query_rows = lax.dynamic_slice(queries, corner, tile_shape + (HEAD_DIM,)).reshape(-1, HEAD_DIM).astype(jnp.float32)
        key_rows = lax.dynamic_slice(key_vectors, window_corner, key_shape).reshape(-1, HEAD_DIM).astype(jnp.float32)
        value_rows = lax.dynamic_slice(value_vectors, window_corner, key_shape).reshape(-1, HEAD_DIM).astype(jnp.float32)
        grad_rows = lax.dynamic_slice(projected_grad, corner, tile_shape + (MODEL_DIM,)).reshape(-1, MODEL_DIM).astype(jnp.float32)
        scores = product(query_rows, key_rows.T) * inv_root
        row_max = lax.optimization_barrier(jnp.max(scores, axis=1, keepdims=True))
        row_sum = lax.optimization_barrier(jnp.sum(jnp.exp(scores - row_max), axis=1, keepdims=True))
        probability = jnp.exp(scores - row_max) / row_sum
        prob_bf = to_bfloat(probability)
        attended = to_bfloat(product(prob_bf, value_rows))
        projected_tile = product(attended, weight_full).astype(jnp.bfloat16).reshape(tile_shape + (MODEL_DIM,))
        attended_grad = to_bfloat(product(grad_rows, weight_full.T))
        weight_acc = weight_acc + product(attended.T, grad_rows)
        row_dot = lax.optimization_barrier(jnp.sum(attended_grad * attended, axis=1, keepdims=True))
        prob_grad = product(attended_grad, value_rows.T)
        score_grad = to_bfloat(probability * (prob_grad - row_dot))
        query_tile = (product(score_grad, key_rows) * inv_root).astype(jnp.bfloat16).reshape(tile_shape + (HEAD_DIM,))
        key_part = product(score_grad.T, query_rows) * inv_root
        value_part = product(prob_bf.T, attended_grad)
        key_acc = lax.dynamic_update_slice(key_acc, lax.dynamic_slice(key_acc, window_corner, key_shape) + key_part.reshape(key_shape), window_corner)
        value_acc = lax.dynamic_update_slice(value_acc, lax.dynamic_slice(value_acc, window_corner, key_shape) + value_part.reshape(key_shape), window_corner)
        return ((key_acc, value_acc, weight_acc), (projected_tile, query_tile))
    initial = (jnp.zeros((FRAMES, HEIGHT, WIDTH, HEAD_DIM), jnp.float32), jnp.zeros((FRAMES, HEIGHT, WIDTH, HEAD_DIM), jnp.float32), jnp.zeros((HEAD_DIM, MODEL_DIM), jnp.float32))
    tile_total = N_FRAME * N_HEIGHT * N_WIDTH
    finals, outputs = lax.scan(one_tile, initial, jnp.arange(tile_total, dtype=jnp.int32))
    projected = tiles_to_grid(outputs[0], MODEL_DIM)
    grad_query = tiles_to_grid(outputs[1], HEAD_DIM)
    grad_out_weight = finals[2] / float(tile_total)
    return (projected, grad_query, finals[0].astype(jnp.bfloat16), finals[1].astype(jnp.bfloat16), grad_out_weight)
```

```python
import math

import jax
import jax.numpy as jnp
from jax import lax
from jax.sharding import PartitionSpec as P

AXES = ("frame", "height", "width")


def window_of(position, extent):
    span = min(3, extent)
    start = max(0, min(position - 1, extent - 3))
    return range(start, start + span)


def routes_of(extent):
    first = [(p ^ 1, p) for p in range(extent) if (p ^ 1) in window_of(p, extent)]
    if extent > 4:
        first = [(p + 1, p) for p in range(extent - 1)]
    wanted = [(s, p) for p in range(extent) for s in window_of(p, extent) if s != p]
    routes = [first]
    for pair in wanted:
        if pair in first:
            continue
        for route in routes[1:]:
            if all(pair[0] != s and pair[1] != p for s, p in route):
                route.append(pair)
                break
        else:
            routes.append([pair])
    return [route for route in routes if route]


def slots_of(extent):
    routes = routes_of(extent)
    arrivals = [[c for c, r in enumerate(routes) if any(q == p for _, q in r)] for p in range(extent)]
    return [[arrivals[p][k] for p in range(extent)] for k in range(min(3, extent) - 1)]


def chosen(options, choice, axis):
    value = options[choice[0]]
    for option in sorted(set(choice)):
        if option != choice[0]:
            here = jnp.array([c == option for c in choice])[lax.axis_index(axis)]
            value = jnp.where(here, options[option], value)
    return value


def give_back(pieces, axis):
    extent = lax.axis_size(axis)
    slots = slots_of(extent)
    summed = pieces[0]
    for c, route in enumerate(routes_of(extent)):
        holders = [next((k for k in range(len(slots)) if slots[k][p] == c), None) for p in range(extent)]
        used = sorted({k for k in holders if k is not None})
        choice = [k if k is not None else used[0] for k in holders]
        outgoing = chosen({k: pieces[k + 1] for k in used}, choice, axis).astype(jnp.bfloat16)
        back = lax.ppermute(outgoing, axis, [(p, s) for s, p in route])
        summed = summed + back.astype(jnp.float32)
    return summed


def sum_everywhere(term):
    rows, columns = term.shape
    plane = lax.axis_size("frame") * lax.axis_size("width")
    column = lax.axis_size("height")
    part = term.astype(jnp.bfloat16).reshape(plane, rows // plane, columns)
    part = lax.all_to_all(part, ("frame", "width"), 0, 0)
    part = jnp.sum(part.astype(jnp.float32), axis=0).astype(jnp.bfloat16)
    part = part.reshape(rows // plane, column, columns // column).transpose(1, 0, 2)
    part = lax.all_to_all(part, "height", 0, 0)
    part = jnp.sum(part.astype(jnp.float32), axis=0).astype(jnp.bfloat16)
    whole = lax.all_gather(part, ("frame", "width", "height"))
    whole = whole.reshape(plane, column, rows // plane, columns // column)
    return whole.transpose(0, 2, 1, 3).reshape(rows, columns).astype(jnp.float32)


def body(queries, key_vectors, value_vectors, out_weight, projected_grad):
    head_dim = queries.shape[-1]
    model_dim = out_weight.shape[1]
    inv_root = 1.0 / math.sqrt(head_dim)
    extents = tuple(lax.axis_size(axis) for axis in AXES)
    spans = tuple(min(3, extent) for extent in extents)
    query_rows = queries.reshape(-1, head_dim)
    grad_rows = projected_grad.reshape(-1, model_dim)
    tile = query_rows.shape[0]
    own = jnp.stack((key_vectors.reshape(tile, head_dim), value_vectors.reshape(tile, head_dim)))
    everything = lax.all_gather(own, AXES).reshape(extents + (2, tile, head_dim))
    starts = [
        jnp.maximum(jnp.minimum(lax.axis_index(axis) - 1, lax.axis_size(axis) - 3), 0) for axis in AXES
    ]
    window = lax.dynamic_slice(everything, (*starts, 0, 0, 0), spans + (2, tile, head_dim))
    key_rows = window[:, :, :, 0].reshape(-1, head_dim)
    value_rows = window[:, :, :, 1].reshape(-1, head_dim)
    attended_grad = jnp.einsum(
        "tm,dm->td", grad_rows, out_weight, preferred_element_type=jnp.float32
    ).astype(jnp.bfloat16)
    scores = (
        jnp.einsum("qd,kd->qk", query_rows, key_rows, preferred_element_type=jnp.float32) * inv_root
    )
    row_max = jnp.max(scores, axis=1, keepdims=True)
    weights = jnp.exp(scores - row_max)
    probability = weights / jnp.sum(weights, axis=1, keepdims=True)
    prob_bf = probability.astype(jnp.bfloat16)
    attended = jnp.dot(prob_bf, value_rows, preferred_element_type=jnp.float32).astype(jnp.bfloat16)
    weight_term = jnp.einsum("td,tm->dm", attended, grad_rows, preferred_element_type=jnp.float32)
    tile_count = math.prod(extents)
    grad_out_weight = sum_everywhere(weight_term * (1.0 / float(tile_count)))
    projected = (
        jnp.dot(attended, out_weight, preferred_element_type=jnp.float32)
        .astype(jnp.bfloat16)
        .reshape(projected_grad.shape)
    )
    row_dot = jnp.sum(
        attended_grad.astype(jnp.float32) * attended.astype(jnp.float32), axis=1, keepdims=True
    )
    prob_grad = jnp.einsum(
        "qd,kd->qk", attended_grad, value_rows, preferred_element_type=jnp.float32
    )
    score_grad = (probability * (prob_grad - row_dot)).astype(jnp.bfloat16)
    query_grad = jnp.dot(score_grad, key_rows, preferred_element_type=jnp.float32)
    grad_query = (query_grad * inv_root).astype(jnp.bfloat16).reshape(queries.shape)
    key_grad = (
        jnp.einsum("qk,qd->kd", score_grad, query_rows, preferred_element_type=jnp.float32)
        * inv_root
    )
    value_grad = jnp.einsum("qk,qd->kd", prob_bf, attended_grad, preferred_element_type=jnp.float32)
    grads = jnp.stack((key_grad, value_grad)).reshape((2,) + spans + (tile, head_dim))
    for dim, axis in ((3, "width"), (2, "height"), (1, "frame")):
        extent = lax.axis_size(axis)
        position = lax.axis_index(axis)
        slots = slots_of(extent)
        routes = routes_of(extent)
        orders = [[list(window_of(p, extent)).index(p) for p in range(extent)]]
        for slot in slots:
            senders = [next(s for s, q in routes[slot[p]] if q == p) for p in range(extent)]
            orders.append([list(window_of(p, extent)).index(senders[p]) for p in range(extent)])
        pieces = [
            lax.dynamic_index_in_dim(grads, jnp.array(order)[position], dim, keepdims=False)
            for order in orders
        ]
        grads = give_back(pieces, axis)
    grad_key = grads[0].astype(jnp.bfloat16).reshape(key_vectors.shape)
    grad_value = grads[1].astype(jnp.bfloat16).reshape(value_vectors.shape)
    return (projected, grad_query, grad_key, grad_value, grad_out_weight)


def solution(mesh):
    tokens = P("frame", "height", "width", None)
    return jax.shard_map(
        body,
        mesh=mesh,
        in_specs=(tokens, tokens, tokens, P(), tokens),
        out_specs=(tokens, tokens, tokens, tokens, P()),
        check_vma=False,
    )
```

```python
import functools
import math

import jax
import jax.numpy as jnp
from jax import lax
from jax.experimental import pallas as pl
from jax.experimental.pallas import tpu as pltpu
from jax.sharding import PartitionSpec as P

AXES = ("frame", "height", "width")
VMEM = pl.BlockSpec(memory_space=pltpu.VMEM)
SMEM = pl.BlockSpec(memory_space=pltpu.SMEM)
PARAMS = pltpu.CompilerParams(vmem_limit_bytes=24 * 1024 * 1024)
STAT_ROWS = 8


def window_of(position, extent):
    span = min(3, extent)
    start = max(0, min(position - 1, extent - 3))
    return range(start, start + span)


def routes_of(extent):
    first = [(p ^ 1, p) for p in range(extent) if (p ^ 1) in window_of(p, extent)]
    if extent > 4:
        first = [(p + 1, p) for p in range(extent - 1)]
    wanted = [(s, p) for p in range(extent) for s in window_of(p, extent) if s != p]
    wanted.sort(key=lambda pair: (pair[0] ^ pair[1], pair))
    routes = [first]
    for pair in wanted:
        if pair in first:
            continue
        for route in routes[1:]:
            if all(pair[0] != s and pair[1] != p for s, p in route):
                route.append(pair)
                break
        else:
            routes.append([pair])
    return [route for route in routes if route]


def slots_of(extent):
    routes = routes_of(extent)
    arrivals = [[c for c, r in enumerate(routes) if any(q == p for _, q in r)] for p in range(extent)]
    return [[arrivals[p][k] for p in range(extent)] for k in range(min(3, extent) - 1)]


def chosen(options, choice, axis):
    value = options[choice[0]]
    position = lax.axis_index(axis)
    for option in sorted(set(choice)):
        if option != choice[0]:
            here = functools.reduce(
                jnp.logical_or, [position == p for p, c in enumerate(choice) if c == option]
            )
            value = jnp.where(here, options[option], value)
    return value


def fetch(block, axis):
    extent = lax.axis_size(axis)
    routes = routes_of(extent)
    arrived = [lax.ppermute(block, axis, route) for route in routes]
    tiles = []
    for slot in slots_of(extent):
        used = sorted(set(slot))
        reached = sum(len(routes[c]) for c in used)
        if reached == extent:
            tiles.append(functools.reduce(jnp.add, [arrived[c] for c in used]))
        else:
            tiles.append(chosen(arrived, slot, axis))
    return tiles


def give_back(pieces, axis):
    extent = lax.axis_size(axis)
    slots = slots_of(extent)
    summed = pieces[0]
    for c, route in enumerate(routes_of(extent)):
        holders = [next((k for k in range(len(slots)) if slots[k][p] == c), None) for p in range(extent)]
        used = sorted({k for k in holders if k is not None})
        choice = [k if k is not None else used[0] for k in holders]
        outgoing = chosen({k: pieces[k + 1] for k in used}, choice, axis).astype(jnp.bfloat16)
        back = lax.ppermute(outgoing, axis, [(p, s) for s, p in route])
        summed = summed + back.astype(jnp.float32)
    return summed


def flip(block, axes, bits):
    sizes = [lax.axis_size(axis) for axis in axes]
    route = []
    for flat in range(math.prod(sizes)):
        rest, target, scale = flat, 0, 1
        for size, bit in zip(reversed(sizes), reversed(bits)):
            target += ((rest % size) ^ bit) * scale
            rest //= size
            scale *= size
        route.append((flat, target))
    return lax.ppermute(block, axes, route)


def rows_of(refs, part):
    block = refs[0][:, part]
    for ref in refs[1:]:
        block = block + ref[:, part]
    return block.reshape(-1, block.shape[-1])


def token_kernel(
    place, queries, queries_other, grads, weight, payload, grads_half, grad_rows, both_queries
):
    half = grads_half.shape[1]
    product = lax.dot_general(
        grads[...], weight[...], (((1,), (1,)), ((), ())), preferred_element_type=jnp.float32
    ).astype(jnp.bfloat16)
    grad_rows[...] = product
    payload[:, half:] = product
    payload[:, :half] = grads[:, pl.ds(pl.multiple_of((1 - place[0]) * half, half), half)]
    grads_half[...] = grads[:, pl.ds(pl.multiple_of(place[0] * half, half), half)]
    both_tiles(place, queries[...], queries_other[...], both_queries)


def both_tiles(place, mine, theirs, both):
    tile = mine.shape[0]
    both[pl.ds(pl.multiple_of(place[0] * tile, tile), tile), :] = mine
    both[pl.ds(pl.multiple_of((1 - place[0]) * tile, tile), tile), :] = theirs


def forward_kernel(inv_root, layout, place, both_queries, *refs):
    groups, rest = split_groups(layout, refs)
    partial, scores = rest
    dim = both_queries.shape[1]
    query_rows = both_queries[...]
    top = None
    start = 0
    spans = []
    for group in groups:
        keys = rows_of(group, 0)
        piece = lax.dot_general(
            keys, query_rows, (((1,), (1,)), ((), ())), preferred_element_type=jnp.float32
        )
        scores[start : start + keys.shape[0], :] = piece
        spans.append((start, keys.shape[0]))
        start += keys.shape[0]
        piece_top = jnp.max(piece, axis=0, keepdims=True)
        top = piece_top if top is None else jnp.maximum(top, piece_top)
    total = jnp.zeros_like(top)
    mixed = jnp.zeros((dim, query_rows.shape[0]), jnp.float32)
    for group, (start, count) in zip(groups, spans):
        weights = jnp.exp((scores[start : start + count, :] - top) * inv_root)
        total = total + jnp.sum(weights, axis=0, keepdims=True)
        mixed = mixed + lax.dot_general(
            rows_of(group, 1),
            weights.astype(jnp.bfloat16),
            (((0,), (0,)), ((), ())),
            preferred_element_type=jnp.float32,
        )
    partial[:dim, :] = mixed
    row = lax.broadcasted_iota(jnp.int32, (STAT_ROWS, query_rows.shape[0]), 0)
    partial[dim:, :] = jnp.where(row == 0, top * inv_root, total)


def merge_kernel(scale, plane, place, mine, theirs, payload, grads_half, grad_rows, *refs):
    stats, attended_own, terms, both_grads, both_attended, term_rows = (
        refs[0],
        refs[1],
        refs[2:-3],
        refs[-3],
        refs[-2],
        refs[-1],
    )
    tile, dim = grad_rows.shape
    half = grads_half.shape[1]
    top_a, top_b = mine[dim : dim + 1, :], theirs[dim : dim + 1, :]
    sum_a, sum_b = mine[dim + 1 : dim + 2, :], theirs[dim + 1 : dim + 2, :]
    top = jnp.maximum(top_a, top_b)
    share_a, share_b = jnp.exp(top_a - top), jnp.exp(top_b - top)
    total = share_a * sum_a + share_b * sum_b
    mixed = mine[:dim, :] * (share_a / total) + theirs[:dim, :] * (share_b / total)
    attended_t = mixed.astype(jnp.bfloat16).astype(jnp.float32)
    both_tiles(place, grad_rows[...], payload[:, half:], both_grads)
    row_dot = jnp.sum(both_grads[...].astype(jnp.float32).T * attended_t, axis=0, keepdims=True)
    row = lax.broadcasted_iota(jnp.int32, (STAT_ROWS, mixed.shape[1]), 0)
    stats[...] = jnp.where(row == 0, top + jnp.log(total), row_dot)
    both_attended[...] = attended_t.T.astype(jnp.bfloat16)
    rows_mine = both_attended[pl.ds(pl.multiple_of(place[0] * tile, tile), tile), :]
    rows_theirs = both_attended[pl.ds(pl.multiple_of((1 - place[0]) * tile, tile), tile), :]
    attended_own[...] = rows_mine
    if not terms:
        return
    contract = (((0,), (0,)), ((), ()))
    term = lax.dot_general(
        rows_mine, grads_half[...], contract, preferred_element_type=jnp.float32
    )
    term = term + lax.dot_general(
        rows_theirs, payload[:, :half], contract, preferred_element_type=jnp.float32
    )
    term_rows[...] = term * scale
    count = dim // plane
    for order, out in enumerate(terms):
        chunk = place[1] ^ order
        out[...] = term_rows[pl.ds(pl.multiple_of(chunk * count, count), count), :].astype(jnp.bfloat16)


def split_groups(layout, refs):
    groups, start = [], 0
    for count in layout:
        groups.append(refs[start : start + count])
        start += count
    return groups, refs[start:]


def backward_kernel(
    inv_root, layout, targets, place, stats, both_queries, payload, grad_rows, *refs
):
    groups, rest = split_groups(layout, refs)
    count = 1 + max(out for out, _ in targets)
    outs, (query_own, query_other, both_grads, both_out) = rest[:count], rest[count:]
    tile, dim = grad_rows.shape
    columns = payload.shape[1]
    both_tiles(place, grad_rows[...], payload[:, columns - dim :], both_grads)
    query_rows, out_grads = both_queries[...], both_grads[...]
    level, row_dot = stats[0:1, :], stats[1:2, :]
    along = (((1,), (1,)), ((), ()))
    query_grad = jnp.zeros((dim, 2 * tile), jnp.float32)
    for group, (target, first) in zip(groups, targets):
        out, tiles = outs[target], group[0].shape[0]
        keys, values = rows_of(group, 0), rows_of(group, 1)
        scores = lax.dot_general(keys, query_rows, along, preferred_element_type=jnp.float32)
        probability = jnp.exp(scores * inv_root - level)
        prob_grad = lax.dot_general(values, out_grads, along, preferred_element_type=jnp.float32)
        score_grad = (probability * (prob_grad - row_dot)).astype(jnp.bfloat16)
        shape = (tiles,) + out.shape[2:]
        key_grad = jnp.dot(score_grad, query_rows, preferred_element_type=jnp.float32) * inv_root
        value_grad = jnp.dot(
            probability.astype(jnp.bfloat16), out_grads, preferred_element_type=jnp.float32
        )
        out[first : first + tiles, 0] = key_grad.reshape(shape).astype(out.dtype)
        out[first : first + tiles, 1] = value_grad.reshape(shape).astype(out.dtype)
        query_grad = query_grad + lax.dot_general(
            keys, score_grad, (((0,), (0,)), ((), ())), preferred_element_type=jnp.float32
        )
    both_out[...] = query_grad.T * inv_root
    query_own[...] = both_out[pl.ds(pl.multiple_of(place[0] * tile, tile), tile), :]
    other = both_out[pl.ds(pl.multiple_of((1 - place[0]) * tile, tile), tile), :]
    other = other.astype(jnp.bfloat16)
    rows = query_other.shape[0]
    for block in range(tile // rows):
        query_other[:, block * dim : (block + 1) * dim] = other[block * rows : (block + 1) * rows]


def assemble_kernel(flipped, rows, place, part, *refs):
    whole, rows_ref, done = refs[-3 - flipped], refs[-2], refs[-1]
    count, width = rows_ref.shape
    for order in range(count // rows):
        row = pl.multiple_of((place[1] ^ order) * rows, rows)
        rows_ref[pl.ds(row, rows), :] = part[order * rows : (order + 1) * rows, :].astype(jnp.float32)
    core = 1 - place[0] if flipped else place[0]
    columns = pl.ds(pl.multiple_of(core * width, width), width)
    copy = pltpu.make_async_copy(rows_ref, whole.at[:, columns], done)
    copy.start()
    if flipped:
        query_own, grad_query = refs[0], refs[-3]
        dim, step = grad_query.shape[1], part.shape[0] - count
        for block in range(width // dim):
            piece = part[count:, block * dim : (block + 1) * dim].astype(jnp.float32)
            span = slice(block * step, (block + 1) * step)
            grad_query[span, :] = (query_own[span, :] + piece).astype(jnp.bfloat16)
    copy.wait()


def assemble(flipped, place, part, rows, shape, whole=None, query_own=None):
    anywhere = pl.BlockSpec(memory_space=pl.ANY)
    outs, out_specs, operands, in_specs = shape, anywhere, (place, part), [SMEM, VMEM]
    if flipped:
        outs, out_specs = (shape, shaped(*query_own.shape)), (anywhere, VMEM)
        operands, in_specs = operands + (query_own, whole), in_specs + [VMEM, anywhere]
    return pl.pallas_call(
        functools.partial(assemble_kernel, flipped, rows),
        out_shape=outs,
        in_specs=in_specs,
        out_specs=out_specs,
        scratch_shapes=[
            pltpu.VMEM((shape.shape[0], part.shape[1]), jnp.float32),
            pltpu.SemaphoreType.DMA,
        ],
        input_output_aliases={3: 0} if flipped else {},
        compiler_params=PARAMS,
    )(*operands)


def pack_kernel(*refs):
    start = 0
    for piece in refs[:-1]:
        refs[-1][start : start + piece.shape[0], :] = piece[...]
        start += piece.shape[0]


def combine_kernel(column, *refs):
    arrived, pieces = refs[: -column.shape[0]], refs[-column.shape[0] :]
    for k, piece in enumerate(pieces):
        total = column[k]
        for block in arrived:
            total = total + block[k].astype(jnp.float32)
        piece[...] = total.astype(piece.dtype)


def shaped(*shape, kind=jnp.bfloat16):
    return jax.ShapeDtypeStruct(shape, kind)


def kernel_call(kernel, operands, outs, scratch=(), cost=None):
    many = isinstance(outs, (list, tuple))
    return pl.pallas_call(
        kernel,
        out_shape=outs,
        in_specs=[SMEM] + [VMEM] * (len(operands) - 1),
        out_specs=[VMEM] * len(outs) if many else VMEM,
        scratch_shapes=list(scratch),
        compiler_params=PARAMS,
        cost_estimate=cost,
    )(*operands)


def cost_of(flops, moved):
    return pl.CostEstimate(flops=int(flops), bytes_accessed=int(moved), transcendentals=0)


PLANE_BITS = ((0, 0), (0, 1), (2, 0), (2, 1))


def sum_over_plane(terms):
    summed = terms[0].astype(jnp.float32)
    for term, bit in zip(terms[1:], PLANE_BITS[1:]):
        summed = summed + flip(term, ("frame", "width"), bit).astype(jnp.float32)
    return summed.astype(jnp.bfloat16)


def join_sum(part, query_own, query_other, place):
    plane = len(part)
    pieces = part + [query_other]
    part = pl.pallas_call(
        pack_kernel,
        out_shape=shaped(sum(p.shape[0] for p in pieces), pieces[0].shape[1]),
        in_specs=[VMEM] * len(pieces),
        out_specs=VMEM,
        compiler_params=PARAMS,
    )(*pieces)
    other = flip(part, ("frame",), (1,))
    rows = (part.shape[0] - query_other.shape[0]) // plane
    shape = shaped(plane * rows, 2 * part.shape[1], kind=jnp.float32)
    whole = assemble(False, place, part, rows, shape)
    return assemble(True, place, other, rows, shape, whole, query_own)


def body(queries, key_vectors, value_vectors, out_weight, projected_grad):
    head_dim = queries.shape[-1]
    model_dim = out_weight.shape[1]
    half = model_dim // 2
    inv_root = 1.0 / math.sqrt(head_dim)
    extents = tuple(lax.axis_size(axis) for axis in AXES)
    assert extents[0] == 4
    small = extents[1:] == (4, 2)
    frame, height, width = (lax.axis_index(axis) for axis in AXES)
    core = frame % 2
    place = jnp.stack([core, (frame // 2) * 2 + width, height]).astype(jnp.int32)
    query_rows = queries.reshape(-1, head_dim)
    grads = projected_grad.reshape(-1, model_dim)
    tile = query_rows.shape[0]

    own = jnp.stack((key_vectors.reshape(tile, head_dim), value_vectors.reshape(tile, head_dim)))
    cross = [(2 * s + y, 2 * p + 1 - y) for s, p in ((2, 1), (1, 2)) for y in (0, 1)]

    if small:
        swap = [(0, 1), (1, 0)]
        tiles = fetch(own, "height")
        own_beside = lax.ppermute(own[None], "width", swap)
        others = jnp.stack(tiles)
        column = jnp.stack([own] + tiles)
        others, column, own_beside, query_rows_late = lax.optimization_barrier(
            (others, column, own_beside, query_rows)
        )
        others_beside = lax.ppermute(others, "width", swap)
        far = [
            lax.ppermute(column, "frame", [(2, 0), (1, 3)]),
            lax.ppermute(column, ("frame", "width"), cross),
        ]
        blocks = [column, own_beside, others_beside, *far]
        layout = (1, 1, 1, 2)
        targets = ((0, 0), (1, 0), (1, 1), (2, 0))
        column_tiles, kinds = 1 + others.shape[0], 3
    else:
        query_rows_late = query_rows
        column = jnp.stack([own] + fetch(own, "height"))
        beside = fetch(column, "width")
        everything = jnp.concatenate([column] + beside, axis=0)
        far = [
            lax.ppermute(everything[:, :, : tile // 2], "frame", [(2, 0), (1, 3)]),
            lax.ppermute(everything[:, :, tile // 2 :], "frame", [(2, 1), (1, 2)]),
        ]
        blocks = [column] + beside + far
        layout = (1,) * (1 + len(beside)) + (2,)
        targets = tuple((k, 0) for k in range(len(layout)))
        column_tiles, kinds = column.shape[0], len(layout)
    queries_other = flip(query_rows_late, ("frame",), (1,))
    payload, grads_half, grad_rows, both_queries = kernel_call(
        token_kernel,
        (place, query_rows, queries_other, grads, out_weight),
        (
            shaped(tile, half + head_dim),
            shaped(tile, half),
            shaped(tile, head_dim),
            shaped(2 * tile, head_dim),
        ),
        cost=cost_of(2 * tile * head_dim * model_dim, 4 * tile * model_dim),
    )
    payload, grad_rows, *blocks = lax.optimization_barrier((payload, grad_rows, *blocks))
    payload = flip(payload, ("frame",), (1,))
    grad_shapes = [(column_tiles, 2, tile, head_dim)] * (kinds - 1)
    grad_shapes.append((column_tiles, 2, tile, head_dim) if small else far[0].shape)
    key_count = sum(shape[0] * shape[2] for shape in grad_shapes)
    product = 2 * key_count * 2 * tile * head_dim
    moved = sum(b.size * 2 for b in blocks)

    partial = kernel_call(
        functools.partial(forward_kernel, inv_root, layout),
        (place, both_queries, *blocks),
        shaped(head_dim + STAT_ROWS, 2 * tile, kind=jnp.float32),
        scratch=(pltpu.VMEM((key_count, 2 * tile), jnp.float32),),
        cost=cost_of(2 * product, moved),
    )
    partial_other = flip(partial, ("frame",), (1,))
    plane = 4
    chunks = plane if small else 0
    merged = kernel_call(
        functools.partial(merge_kernel, 1.0 / float(math.prod(extents)), plane),
        (place, partial, partial_other, payload, grads_half, grad_rows),
        (
            shaped(STAT_ROWS, 2 * tile, kind=jnp.float32),
            shaped(tile, head_dim),
            *[shaped(head_dim // plane, half)] * chunks,
        ),
        scratch=(
            pltpu.VMEM((2 * tile, head_dim), jnp.bfloat16),
            pltpu.VMEM((2 * tile, head_dim), jnp.bfloat16),
            pltpu.VMEM((head_dim, half), jnp.float32),
        ),
        cost=cost_of(4 * tile * head_dim * half, 4 * tile * model_dim),
    )
    stats, attended, *terms = merged
    back = kernel_call(
        functools.partial(backward_kernel, inv_root, layout, targets),
        (place, stats, both_queries, payload, grad_rows, *blocks),
        (
            shaped(*grad_shapes[0], kind=jnp.float32),
            *[shaped(*shape) for shape in grad_shapes[1:]],
            shaped(tile, head_dim, kind=jnp.float32),
            shaped(tile * head_dim // half, half),
        ),
        scratch=(
            pltpu.VMEM((2 * tile, head_dim), jnp.bfloat16),
            pltpu.VMEM((2 * tile, head_dim), jnp.float32),
        ),
        cost=cost_of(5 * product, 2 * moved),
    )
    if small:
        terms[0], *back = lax.optimization_barrier((terms[0], *back))
        part = sum_over_plane(terms)
        other = flip(part, ("height",), (1,))
        part = (part.astype(jnp.float32) + other.astype(jnp.float32)).astype(jnp.bfloat16)
        part, attended = lax.optimization_barrier((part, attended))
        other = flip(part, ("height",), (2,))
    else:
        weight_term = jnp.einsum("td,tm->dm", attended, grads, preferred_element_type=jnp.float32)
        grad_out_weight = lax.psum(weight_term, AXES) / float(math.prod(extents))
    projected = (
        jnp.dot(attended, out_weight, preferred_element_type=jnp.float32)
        .astype(jnp.bfloat16)
        .reshape(projected_grad.shape)
    )
    column_grad, *beside_grads, far_grad, query_own, query_other = back
    if small:
        arrived = [
            lax.ppermute(beside_grads[0], "width", [(0, 1), (1, 0)]),
            lax.ppermute(far_grad, "frame", [(0, 2), (3, 1)]),
            lax.ppermute(far_grad, ("frame", "width"), [(p, s) for s, p in cross]),
        ]
        other, projected = lax.optimization_barrier((other, projected))
        part = (part.astype(jnp.float32) + other.astype(jnp.float32)).astype(jnp.bfloat16)
        part, column_grad = lax.optimization_barrier((part, column_grad))
        part = [part] + [flip(part, ("frame", "width"), bit) for bit in PLANE_BITS[1:]]
        shape = column_grad.shape[1:]
        pieces = pl.pallas_call(
            combine_kernel,
            out_shape=[shaped(*shape, kind=jnp.float32)] + [shaped(*shape)] * (column_tiles - 1),
            in_specs=[VMEM] * 4,
            out_specs=[VMEM] * column_tiles,
            compiler_params=PARAMS,
        )(column_grad, *arrived)
    else:
        arrived = jnp.concatenate(
            (
                lax.ppermute(far_grad, "frame", [(0, 2), (3, 1)]),
                lax.ppermute(far_grad, "frame", [(1, 2), (2, 1)]),
            ),
            axis=2,
        ).astype(jnp.float32)
        pieces = [column_grad] + [b.astype(jnp.float32) for b in beside_grads]
        span = column_tiles
        pieces = [p + arrived[i * span : (i + 1) * span] for i, p in enumerate(pieces)]
        column_grad = give_back(pieces, "width")
        pieces = [column_grad[k] for k in range(column_tiles)]
    if small:
        grad_out_weight, grad_query = join_sum(part, query_own, query_other, place)
    else:
        query_other = flip(query_other, ("frame",), (1,)).reshape(-1, half // head_dim, head_dim)
        query_other = query_other.transpose(1, 0, 2).reshape(tile, head_dim)
        grad_query = (query_own + query_other.astype(jnp.float32)).astype(jnp.bfloat16)
    own_grad = give_back(pieces, "height")
    grad_key = own_grad[0].astype(jnp.bfloat16).reshape(key_vectors.shape)
    grad_value = own_grad[1].astype(jnp.bfloat16).reshape(value_vectors.shape)
    grad_query = grad_query.reshape(queries.shape)
    return (projected, grad_query, grad_key, grad_value, grad_out_weight)


def solution(mesh):
    tokens = P("frame", "height", "width", None)
    return jax.shard_map(
        body,
        mesh=mesh,
        in_specs=(tokens, tokens, tokens, P(), tokens),
        out_specs=(tokens, tokens, tokens, tokens, P()),
        check_vma=False,
    )
```

```python
import functools
import math

import jax
import jax.numpy as jnp
from jax import lax
from jax.experimental import pallas as pl
from jax.experimental.pallas import tpu as pltpu
from jax.sharding import PartitionSpec as P

AXES = ("frame", "height", "width")
VMEM = pl.BlockSpec(memory_space=pltpu.VMEM)
SMEM = pl.BlockSpec(memory_space=pltpu.SMEM)
PARAMS = pltpu.CompilerParams(vmem_limit_bytes=24 * 1024 * 1024)
STAT_ROWS = 8


def window_of(position, extent):
    span = min(3, extent)
    start = max(0, min(position - 1, extent - 3))
    return range(start, start + span)


def routes_of(extent):
    first = [(p ^ 1, p) for p in range(extent) if (p ^ 1) in window_of(p, extent)]
    if extent > 4:
        first = [(p + 1, p) for p in range(extent - 1)]
    wanted = [(s, p) for p in range(extent) for s in window_of(p, extent) if s != p]
    wanted.sort(key=lambda pair: (pair[0] ^ pair[1], pair))
    routes = [first]
    for pair in wanted:
        if pair in first:
            continue
        for route in routes[1:]:
            if all(pair[0] != s and pair[1] != p for s, p in route):
                route.append(pair)
                break
        else:
            routes.append([pair])
    return [route for route in routes if route]


def slots_of(extent):
    routes = routes_of(extent)
    arrivals = [[c for c, r in enumerate(routes) if any(q == p for _, q in r)] for p in range(extent)]
    return [[arrivals[p][k] for p in range(extent)] for k in range(min(3, extent) - 1)]


def chosen(options, choice, axis):
    value = options[choice[0]]
    position = lax.axis_index(axis)
    for option in sorted(set(choice)):
        if option != choice[0]:
            here = functools.reduce(
                jnp.logical_or, [position == p for p, c in enumerate(choice) if c == option]
            )
            value = jnp.where(here, options[option], value)
    return value


def fetch(block, axis):
    extent = lax.axis_size(axis)
    routes = routes_of(extent)
    arrived = [lax.ppermute(block, axis, route) for route in routes]
    tiles = []
    for slot in slots_of(extent):
        used = sorted(set(slot))
        reached = sum(len(routes[c]) for c in used)
        if reached == extent:
            tiles.append(functools.reduce(jnp.add, [arrived[c] for c in used]))
        else:
            tiles.append(chosen(arrived, slot, axis))
    return tiles


def give_back(pieces, axis):
    extent = lax.axis_size(axis)
    slots = slots_of(extent)
    summed = pieces[0]
    for c, route in reversed(list(enumerate(routes_of(extent)))):
        holders = [next((k for k in range(len(slots)) if slots[k][p] == c), None) for p in range(extent)]
        used = sorted({k for k in holders if k is not None})
        choice = [k if k is not None else used[0] for k in holders]
        outgoing = chosen({k: pieces[k + 1] for k in used}, choice, axis).astype(jnp.bfloat16)
        back = lax.ppermute(outgoing, axis, [(p, s) for s, p in route])
        summed = summed + back.astype(jnp.float32)
    return summed


def flip(block, axes, bits):
    sizes = [lax.axis_size(axis) for axis in axes]
    route = []
    for flat in range(math.prod(sizes)):
        rest, target, scale = flat, 0, 1
        for size, bit in zip(reversed(sizes), reversed(bits)):
            target += ((rest % size) ^ bit) * scale
            rest //= size
            scale *= size
        route.append((flat, target))
    return lax.ppermute(block, axes, route)


def rows_of(refs, part):
    block = refs[0][:, part]
    for ref in refs[1:]:
        block = block + ref[:, part]
    return block.reshape(-1, block.shape[-1])


def token_kernel(
    place, queries, queries_other, grads, weight, payload, grads_half, grad_rows, both_queries
):
    half = grads_half.shape[1]
    product = lax.dot_general(
        grads[...], weight[...], (((1,), (1,)), ((), ())), preferred_element_type=jnp.float32
    ).astype(jnp.bfloat16)
    grad_rows[...] = product
    payload[:, half:] = product
    payload[:, :half] = grads[:, pl.ds(pl.multiple_of((1 - place[0]) * half, half), half)]
    grads_half[...] = grads[:, pl.ds(pl.multiple_of(place[0] * half, half), half)]
    both_tiles(place, queries[...], queries_other[...], both_queries)


def both_tiles(place, mine, theirs, both):
    tile = mine.shape[0]
    both[pl.ds(pl.multiple_of(place[0] * tile, tile), tile), :] = mine
    both[pl.ds(pl.multiple_of((1 - place[0]) * tile, tile), tile), :] = theirs


def forward_kernel(inv_root, layout, carried, both_queries, *refs):
    groups, rest = split_groups(layout, refs)
    partial, scores = rest[-2:]
    dim = both_queries.shape[1]
    query_rows = both_queries[...]
    top, start, spans = None, 0, []
    if carried:
        top = rest[0][dim : dim + 1, :]
    for group in groups:
        keys = rows_of(group, 0)
        piece = lax.dot_general(
            keys, query_rows, (((1,), (1,)), ((), ())), preferred_element_type=jnp.float32
        )
        scores[start : start + keys.shape[0], :] = piece
        spans.append((start, keys.shape[0]))
        start += keys.shape[0]
        piece_top = jnp.max(piece, axis=0, keepdims=True) * inv_root
        top = piece_top if top is None else jnp.maximum(top, piece_top)
    if carried:
        share = jnp.exp(rest[0][dim : dim + 1, :] - top)
        total = rest[0][dim + 1 : dim + 2, :] * share
        mixed = rest[0][:dim, :] * share
    else:
        total = jnp.zeros_like(top)
        mixed = jnp.zeros((dim, query_rows.shape[0]), jnp.float32)
    for group, (start, count) in zip(groups, spans):
        weights = jnp.exp(scores[start : start + count, :] * inv_root - top)
        total = total + jnp.sum(weights, axis=0, keepdims=True)
        mixed = mixed + lax.dot_general(
            rows_of(group, 1),
            weights.astype(jnp.bfloat16),
            (((0,), (0,)), ((), ())),
            preferred_element_type=jnp.float32,
        )
    partial[:dim, :] = mixed
    row = lax.broadcasted_iota(jnp.int32, (STAT_ROWS, query_rows.shape[0]), 0)
    partial[dim:, :] = jnp.where(row == 0, top, total)


def merge_kernel(scale, plane, place, mine, theirs, payload, grads_half, grad_rows, *refs):
    stats, attended_own, terms, both_grads, both_attended, term_rows = (
        refs[0],
        refs[1],
        refs[2:-3],
        refs[-3],
        refs[-2],
        refs[-1],
    )
    tile, dim = grad_rows.shape
    half = grads_half.shape[1]
    top_a, top_b = mine[dim : dim + 1, :], theirs[dim : dim + 1, :]
    sum_a, sum_b = mine[dim + 1 : dim + 2, :], theirs[dim + 1 : dim + 2, :]
    top = jnp.maximum(top_a, top_b)
    share_a, share_b = jnp.exp(top_a - top), jnp.exp(top_b - top)
    total = share_a * sum_a + share_b * sum_b
    mixed = mine[:dim, :] * (share_a / total) + theirs[:dim, :] * (share_b / total)
    attended_t = mixed.astype(jnp.bfloat16).astype(jnp.float32)
    both_tiles(place, grad_rows[...], payload[:, half:], both_grads)
    row_dot = jnp.sum(both_grads[...].astype(jnp.float32).T * attended_t, axis=0, keepdims=True)
    row = lax.broadcasted_iota(jnp.int32, (STAT_ROWS, mixed.shape[1]), 0)
    stats[...] = jnp.where(row == 0, top + jnp.log(total), row_dot)
    both_attended[...] = attended_t.T.astype(jnp.bfloat16)
    rows_mine = both_attended[pl.ds(pl.multiple_of(place[0] * tile, tile), tile), :]
    rows_theirs = both_attended[pl.ds(pl.multiple_of((1 - place[0]) * tile, tile), tile), :]
    attended_own[...] = rows_mine
    if not terms:
        return
    contract = (((0,), (0,)), ((), ()))
    term = lax.dot_general(
        rows_mine, grads_half[...], contract, preferred_element_type=jnp.float32
    )
    term = term + lax.dot_general(
        rows_theirs, payload[:, :half], contract, preferred_element_type=jnp.float32
    )
    term_rows[...] = term * scale
    count = dim // plane
    for order, out in enumerate(terms):
        chunk = place[1] ^ order
        out[...] = term_rows[pl.ds(pl.multiple_of(chunk * count, count), count), :].astype(jnp.bfloat16)


def split_groups(layout, refs):
    groups, start = [], 0
    for count in layout:
        groups.append(refs[start : start + count])
        start += count
    return groups, refs[start:]


def backward_kernel(
    inv_root, layout, targets, place, stats, both_queries, payload, grad_rows, *refs
):
    groups, rest = split_groups(layout, refs)
    count = 1 + max(out for out, _ in targets)
    outs, (query_own, query_other, both_grads, both_out) = rest[:count], rest[count:]
    tile, dim = grad_rows.shape
    columns = payload.shape[1]
    both_tiles(place, grad_rows[...], payload[:, columns - dim :], both_grads)
    query_rows, out_grads = both_queries[...], both_grads[...]
    level, row_dot = stats[0:1, :], stats[1:2, :]
    along = (((1,), (1,)), ((), ()))
    query_grad = jnp.zeros((dim, 2 * tile), jnp.float32)
    for group, (target, first) in zip(groups, targets):
        out, tiles = outs[target], group[0].shape[0]
        keys, values = rows_of(group, 0), rows_of(group, 1)
        scores = lax.dot_general(keys, query_rows, along, preferred_element_type=jnp.float32)
        probability = jnp.exp(scores * inv_root - level)
        prob_grad = lax.dot_general(values, out_grads, along, preferred_element_type=jnp.float32)
        score_grad = (probability * (prob_grad - row_dot)).astype(jnp.bfloat16)
        shape = (tiles,) + out.shape[2:]
        key_grad = jnp.dot(score_grad, query_rows, preferred_element_type=jnp.float32) * inv_root
        value_grad = jnp.dot(
            probability.astype(jnp.bfloat16), out_grads, preferred_element_type=jnp.float32
        )
        out[first : first + tiles, 0] = key_grad.reshape(shape).astype(out.dtype)
        out[first : first + tiles, 1] = value_grad.reshape(shape).astype(out.dtype)
        query_grad = query_grad + lax.dot_general(
            keys, score_grad, (((0,), (0,)), ((), ())), preferred_element_type=jnp.float32
        )
    both_out[...] = query_grad.T * inv_root
    query_own[...] = both_out[pl.ds(pl.multiple_of(place[0] * tile, tile), tile), :]
    other = both_out[pl.ds(pl.multiple_of((1 - place[0]) * tile, tile), tile), :]
    other = other.astype(jnp.bfloat16)
    rows = query_other.shape[0]
    for block in range(tile // rows):
        query_other[:, block * dim : (block + 1) * dim] = other[block * rows : (block + 1) * rows]


def assemble_kernel(flipped, rows, place, part, *refs):
    whole, rows_ref, done = refs[-3 - flipped], refs[-2], refs[-1]
    count, width = rows_ref.shape
    core = 1 - place[0] if flipped else place[0]
    columns = pl.ds(pl.multiple_of(core * width, width), width)
    copies = []
    for order in range(count // rows):
        span = pl.ds(pl.multiple_of((place[1] ^ order) * rows, rows), rows)
        rows_ref[span, :] = part[order * rows : (order + 1) * rows, :].astype(jnp.float32)
        copies.append(
            pltpu.make_async_copy(rows_ref.at[span, :], whole.at[span, columns], done.at[order])
        )
        copies[-1].start()
    if flipped:
        query_own, grad_query = refs[0], refs[-3]
        dim, step = grad_query.shape[1], part.shape[0] - count
        for block in range(width // dim):
            piece = part[count:, block * dim : (block + 1) * dim].astype(jnp.float32)
            span = slice(block * step, (block + 1) * step)
            grad_query[span, :] = (query_own[span, :] + piece).astype(jnp.bfloat16)
    for copy in copies:
        copy.wait()


def assemble(flipped, place, part, rows, shape, whole=None, query_own=None):
    anywhere = pl.BlockSpec(memory_space=pl.ANY)
    outs, out_specs, operands, in_specs = shape, anywhere, (place, part), [SMEM, VMEM]
    if flipped:
        outs, out_specs = (shape, shaped(*query_own.shape)), (anywhere, VMEM)
        operands, in_specs = operands + (query_own, whole), in_specs + [VMEM, anywhere]
    return pl.pallas_call(
        functools.partial(assemble_kernel, flipped, rows),
        out_shape=outs,
        in_specs=in_specs,
        out_specs=out_specs,
        scratch_shapes=[
            pltpu.VMEM((shape.shape[0], part.shape[1]), jnp.float32),
            pltpu.SemaphoreType.DMA((shape.shape[0] // rows,)),
        ],
        input_output_aliases={3: 0} if flipped else {},
        compiler_params=PARAMS,
    )(*operands)


def pack_kernel(*refs):
    start = 0
    for piece in refs[:-1]:
        refs[-1][start : start + piece.shape[0], :] = piece[...]
        start += piece.shape[0]


def combine_kernel(column, *refs):
    arrived, pieces = refs[: -column.shape[0]], refs[-column.shape[0] :]
    for k, piece in enumerate(pieces):
        total = column[k]
        for block in arrived:
            total = total + block[k].astype(jnp.float32)
        piece[...] = total.astype(piece.dtype)


def shaped(*shape, kind=jnp.bfloat16):
    return jax.ShapeDtypeStruct(shape, kind)


def kernel_call(kernel, operands, outs, scratch=(), cost=None):
    many = isinstance(outs, (list, tuple))
    return pl.pallas_call(
        kernel,
        out_shape=outs,
        in_specs=[SMEM] + [VMEM] * (len(operands) - 1),
        out_specs=[VMEM] * len(outs) if many else VMEM,
        scratch_shapes=list(scratch),
        compiler_params=PARAMS,
        cost_estimate=cost,
    )(*operands)


def cost_of(flops, moved):
    return pl.CostEstimate(flops=int(flops), bytes_accessed=int(moved), transcendentals=0)


PLANE_BITS = ((0, 0), (0, 1), (2, 0), (2, 1))


def sum_over_plane(terms):
    summed = terms[0].astype(jnp.float32)
    for term, bit in zip(terms[1:], PLANE_BITS[1:]):
        summed = summed + flip(term, ("frame", "width"), bit).astype(jnp.float32)
    return summed.astype(jnp.bfloat16)


def join_sum(part, query_own, query_other, place):
    plane = len(part)
    pieces = part + [query_other]
    part = pl.pallas_call(
        pack_kernel,
        out_shape=shaped(sum(p.shape[0] for p in pieces), pieces[0].shape[1]),
        in_specs=[VMEM] * len(pieces),
        out_specs=VMEM,
        compiler_params=PARAMS,
    )(*pieces)
    other = flip(part, ("frame",), (1,))
    rows = (part.shape[0] - query_other.shape[0]) // plane
    shape = shaped(plane * rows, 2 * part.shape[1], kind=jnp.float32)
    whole = assemble(False, place, part, rows, shape)
    return assemble(True, place, other, rows, shape, whole, query_own)


def body(queries, key_vectors, value_vectors, out_weight, projected_grad):
    head_dim = queries.shape[-1]
    model_dim = out_weight.shape[1]
    half = model_dim // 2
    inv_root = 1.0 / math.sqrt(head_dim)
    extents = tuple(lax.axis_size(axis) for axis in AXES)
    assert extents[0] == 4
    small = extents[1:] == (4, 2)
    frame, height, width = (lax.axis_index(axis) for axis in AXES)
    core = frame % 2
    place = jnp.stack([core, (frame // 2) * 2 + width, height]).astype(jnp.int32)
    query_rows = queries.reshape(-1, head_dim)
    grads = projected_grad.reshape(-1, model_dim)
    tile = query_rows.shape[0]

    own = jnp.stack((key_vectors.reshape(tile, head_dim), value_vectors.reshape(tile, head_dim)))
    cross = [(2 * s + y, 2 * p + 1 - y) for s, p in ((2, 1), (1, 2)) for y in (0, 1)]

    if small:
        swap = [(0, 1), (1, 0)]
        tiles = fetch(own, "height")
        own_beside = lax.ppermute(own[None], "width", swap)
        others = jnp.stack(tiles)
        column = jnp.stack([own] + tiles)
        others, column, own_beside, query_rows_late = lax.optimization_barrier(
            (others, column, own_beside, query_rows)
        )
        others_beside = lax.ppermute(others, "width", swap)
        far = [
            lax.ppermute(column, "frame", [(2, 0), (1, 3)]),
            lax.ppermute(column, ("frame", "width"), cross),
        ]
        blocks = [column, own_beside, others_beside, *far]
        layout = (1, 1, 1, 2)
        targets = ((0, 0), (1, 0), (1, 1), (2, 0))
        column_tiles, kinds = 1 + others.shape[0], 3
    else:
        query_rows_late = query_rows
        column = jnp.stack([own] + fetch(own, "height"))
        beside = fetch(column, "width")
        everything = jnp.concatenate([column] + beside, axis=0)
        far = [
            lax.ppermute(everything[:, :, : tile // 2], "frame", [(2, 0), (1, 3)]),
            lax.ppermute(everything[:, :, tile // 2 :], "frame", [(2, 1), (1, 2)]),
        ]
        blocks = [column] + beside + far
        layout = (1,) * (1 + len(beside)) + (2,)
        targets = tuple((k, 0) for k in range(len(layout)))
        column_tiles, kinds = column.shape[0], len(layout)
    queries_other = flip(query_rows_late, ("frame",), (1,))
    payload, grads_half, grad_rows, both_queries = kernel_call(
        token_kernel,
        (place, query_rows, queries_other, grads, out_weight),
        (
            shaped(tile, half + head_dim),
            shaped(tile, half),
            shaped(tile, head_dim),
            shaped(2 * tile, head_dim),
        ),
        cost=cost_of(2 * tile * head_dim * model_dim, 4 * tile * model_dim),
    )
    grad_shapes = [(column_tiles, 2, tile, head_dim)] * (kinds - 1)
    grad_shapes.append((column_tiles, 2, tile, head_dim) if small else far[0].shape)
    key_count = sum(shape[0] * shape[2] for shape in grad_shapes)
    product = 2 * key_count * 2 * tile * head_dim
    moved = sum(b.size * 2 for b in blocks)

    def forward(operands, groups, carried):
        keys, start = 0, 0
        for count in groups:
            keys += operands[start].shape[0] * operands[start].shape[2]
            start += count
        return pl.pallas_call(
            functools.partial(forward_kernel, inv_root, groups, bool(carried)),
            out_shape=shaped(head_dim + STAT_ROWS, 2 * tile, kind=jnp.float32),
            in_specs=[VMEM] * (1 + len(operands) + len(carried)),
            out_specs=VMEM,
            scratch_shapes=[pltpu.VMEM((keys, 2 * tile), jnp.float32)],
            compiler_params=PARAMS,
            cost_estimate=cost_of(8 * keys * tile * head_dim, moved * keys // key_count),
        )(both_queries, *operands, *carried)

    partial = forward([blocks[0]] + far, (1, 2), ())
    beside = blocks[1 : -len(far)]
    payload, partial, *beside = lax.optimization_barrier((payload, partial, *beside))
    payload = flip(payload, ("frame",), (1,))
    partial = forward(beside, (1,) * len(beside), (partial,))
    blocks = [blocks[0]] + beside + far
    partial_other = flip(partial, ("frame",), (1,))
    plane = 4
    chunks = plane if small else 0
    merged = kernel_call(
        functools.partial(merge_kernel, 1.0 / float(math.prod(extents)), plane),
        (place, partial, partial_other, payload, grads_half, grad_rows),
        (
            shaped(STAT_ROWS, 2 * tile, kind=jnp.float32),
            shaped(tile, head_dim),
            *[shaped(head_dim // plane, half)] * chunks,
        ),
        scratch=(
            pltpu.VMEM((2 * tile, head_dim), jnp.bfloat16),
            pltpu.VMEM((2 * tile, head_dim), jnp.bfloat16),
            pltpu.VMEM((head_dim, half), jnp.float32),
        ),
        cost=cost_of(4 * tile * head_dim * half, 4 * tile * model_dim),
    )
    stats, attended, *terms = merged
    back = kernel_call(
        functools.partial(backward_kernel, inv_root, layout, targets),
        (place, stats, both_queries, payload, grad_rows, *blocks),
        (
            shaped(*grad_shapes[0], kind=jnp.float32),
            *[shaped(*shape) for shape in grad_shapes[1:]],
            shaped(tile, head_dim, kind=jnp.float32),
            shaped(tile * head_dim // half, half),
        ),
        scratch=(
            pltpu.VMEM((2 * tile, head_dim), jnp.bfloat16),
            pltpu.VMEM((2 * tile, head_dim), jnp.float32),
        ),
        cost=cost_of(5 * product, 2 * moved),
    )
    if small:
        terms[0], *back = lax.optimization_barrier((terms[0], *back))
        part = sum_over_plane(terms)
        other = flip(part, ("height",), (1,))
        part = (part.astype(jnp.float32) + other.astype(jnp.float32)).astype(jnp.bfloat16)
        part, attended = lax.optimization_barrier((part, attended))
        other = flip(part, ("height",), (2,))
    else:
        weight_term = jnp.einsum("td,tm->dm", attended, grads, preferred_element_type=jnp.float32)
        grad_out_weight = lax.psum(weight_term, AXES) / float(math.prod(extents))
    projected = (
        jnp.dot(attended, out_weight, preferred_element_type=jnp.float32)
        .astype(jnp.bfloat16)
        .reshape(projected_grad.shape)
    )
    column_grad, *beside_grads, far_grad, query_own, query_other = back
    if small:
        arrived = [
            lax.ppermute(beside_grads[0], "width", [(0, 1), (1, 0)]),
            lax.ppermute(far_grad, "frame", [(0, 2), (3, 1)]),
            lax.ppermute(far_grad, ("frame", "width"), [(p, s) for s, p in cross]),
        ]
        other, projected = lax.optimization_barrier((other, projected))
        part = (part.astype(jnp.float32) + other.astype(jnp.float32)).astype(jnp.bfloat16)
        part, column_grad = lax.optimization_barrier((part, column_grad))
        part = [part] + [flip(part, ("frame", "width"), bit) for bit in PLANE_BITS[1:]]
        shape = column_grad.shape[1:]
        pieces = pl.pallas_call(
            combine_kernel,
            out_shape=[shaped(*shape, kind=jnp.float32)] + [shaped(*shape)] * (column_tiles - 1),
            in_specs=[VMEM] * 4,
            out_specs=[VMEM] * column_tiles,
            compiler_params=PARAMS,
        )(column_grad, *arrived)
    else:
        arrived = jnp.concatenate(
            (
                lax.ppermute(far_grad, "frame", [(0, 2), (3, 1)]),
                lax.ppermute(far_grad, "frame", [(1, 2), (2, 1)]),
            ),
            axis=2,
        ).astype(jnp.float32)
        pieces = [column_grad] + [b.astype(jnp.float32) for b in beside_grads]
        span = column_tiles
        pieces = [p + arrived[i * span : (i + 1) * span] for i, p in enumerate(pieces)]
        column_grad = give_back(pieces, "width")
        pieces = [column_grad[k] for k in range(column_tiles)]
    if small:
        grad_out_weight, grad_query = join_sum(part, query_own, query_other, place)
    else:
        query_other = flip(query_other, ("frame",), (1,)).reshape(-1, half // head_dim, head_dim)
        query_other = query_other.transpose(1, 0, 2).reshape(tile, head_dim)
        grad_query = (query_own + query_other.astype(jnp.float32)).astype(jnp.bfloat16)
    own_grad = give_back(pieces, "height")
    grad_key = own_grad[0].astype(jnp.bfloat16).reshape(key_vectors.shape)
    grad_value = own_grad[1].astype(jnp.bfloat16).reshape(value_vectors.shape)
    grad_query = grad_query.reshape(queries.shape)
    return (projected, grad_query, grad_key, grad_value, grad_out_weight)


def solution(mesh):
    tokens = P("frame", "height", "width", None)
    return jax.shard_map(
        body,
        mesh=mesh,
        in_specs=(tokens, tokens, tokens, P(), tokens),
        out_specs=(tokens, tokens, tokens, tokens, P()),
        check_vma=False,
    )
```

```python
import functools
import math

import jax
import jax.numpy as jnp
from jax import lax
from jax.experimental import pallas as pl
from jax.experimental.pallas import tpu as pltpu
from jax.sharding import PartitionSpec as P

AXES = ("frame", "height", "width")
VMEM = pl.BlockSpec(memory_space=pltpu.VMEM)
SMEM = pl.BlockSpec(memory_space=pltpu.SMEM)
PARAMS = pltpu.CompilerParams(vmem_limit_bytes=24 * 1024 * 1024)
STAT_ROWS = 8


def window_of(position, extent):
    span = min(3, extent)
    start = max(0, min(position - 1, extent - 3))
    return range(start, start + span)


def routes_of(extent):
    first = [(p ^ 1, p) for p in range(extent) if (p ^ 1) in window_of(p, extent)]
    if extent > 4:
        first = [(p + 1, p) for p in range(extent - 1)]
    wanted = [(s, p) for p in range(extent) for s in window_of(p, extent) if s != p]
    wanted.sort(key=lambda pair: (pair[0] ^ pair[1], pair))
    routes = [first]
    for pair in wanted:
        if pair in first:
            continue
        for route in routes[1:]:
            if all(pair[0] != s and pair[1] != p for s, p in route):
                route.append(pair)
                break
        else:
            routes.append([pair])
    return [route for route in routes if route]


def slots_of(extent):
    routes = routes_of(extent)
    arrivals = [[c for c, r in enumerate(routes) if any(q == p for _, q in r)] for p in range(extent)]
    return [[arrivals[p][k] for p in range(extent)] for k in range(min(3, extent) - 1)]


def chosen(options, choice, axis):
    value = options[choice[0]]
    position = lax.axis_index(axis)
    for option in sorted(set(choice)):
        if option != choice[0]:
            here = functools.reduce(
                jnp.logical_or, [position == p for p, c in enumerate(choice) if c == option]
            )
            value = jnp.where(here, options[option], value)
    return value


def fetch(block, axis):
    extent = lax.axis_size(axis)
    routes = routes_of(extent)
    arrived = [lax.ppermute(block, axis, route) for route in routes]
    tiles = []
    for slot in slots_of(extent):
        used = sorted(set(slot))
        reached = sum(len(routes[c]) for c in used)
        if reached == extent:
            tiles.append(functools.reduce(jnp.add, [arrived[c] for c in used]))
        else:
            tiles.append(chosen(arrived, slot, axis))
    return tiles


def give_back(pieces, axis):
    extent = lax.axis_size(axis)
    slots = slots_of(extent)
    summed = pieces[0]
    for c, route in reversed(list(enumerate(routes_of(extent)))):
        holders = [next((k for k in range(len(slots)) if slots[k][p] == c), None) for p in range(extent)]
        used = sorted({k for k in holders if k is not None})
        choice = [k if k is not None else used[0] for k in holders]
        outgoing = chosen({k: pieces[k + 1] for k in used}, choice, axis).astype(jnp.bfloat16)
        back = lax.ppermute(outgoing, axis, [(p, s) for s, p in route])
        summed = summed + back.astype(jnp.float32)
    return summed


def flip(block, axes, bits):
    sizes = [lax.axis_size(axis) for axis in axes]
    route = []
    for flat in range(math.prod(sizes)):
        rest, target, scale = flat, 0, 1
        for size, bit in zip(reversed(sizes), reversed(bits)):
            target += ((rest % size) ^ bit) * scale
            rest //= size
            scale *= size
        route.append((flat, target))
    return lax.ppermute(block, axes, route)


def rows_of(refs, part):
    block = refs[0][:, part]
    for ref in refs[1:]:
        block = block + ref[:, part]
    return block.reshape(-1, block.shape[-1])


def token_kernel(
    place, queries, queries_other, grads, weight, payload, grads_half, grad_rows, both_queries
):
    half = grads_half.shape[1]
    product = lax.dot_general(
        grads[...], weight[...], (((1,), (1,)), ((), ())), preferred_element_type=jnp.float32
    ).astype(jnp.bfloat16)
    grad_rows[...] = product
    payload[:, half:] = product
    payload[:, :half] = grads[:, pl.ds(pl.multiple_of((1 - place[0]) * half, half), half)]
    grads_half[...] = grads[:, pl.ds(pl.multiple_of(place[0] * half, half), half)]
    both_tiles(place, queries[...], queries_other[...], both_queries)


def both_tiles(place, mine, theirs, both):
    tile = mine.shape[0]
    both[pl.ds(pl.multiple_of(place[0] * tile, tile), tile), :] = mine
    both[pl.ds(pl.multiple_of((1 - place[0]) * tile, tile), tile), :] = theirs


def forward_kernel(inv_root, layout, carried, both_queries, *refs):
    groups, rest = split_groups(layout, refs)
    partial, scores = rest[-2:]
    dim = both_queries.shape[1]
    query_rows = both_queries[...]
    top, start, spans = None, 0, []
    if carried:
        top = rest[0][dim : dim + 1, :]
    for group in groups:
        keys = rows_of(group, 0)
        piece = lax.dot_general(
            keys, query_rows, (((1,), (1,)), ((), ())), preferred_element_type=jnp.float32
        )
        scores[start : start + keys.shape[0], :] = piece
        spans.append((start, keys.shape[0]))
        start += keys.shape[0]
        piece_top = jnp.max(piece, axis=0, keepdims=True) * inv_root
        top = piece_top if top is None else jnp.maximum(top, piece_top)
    if carried:
        share = jnp.exp(rest[0][dim : dim + 1, :] - top)
        total = rest[0][dim + 1 : dim + 2, :] * share
        mixed = rest[0][:dim, :] * share
    else:
        total = jnp.zeros_like(top)
        mixed = jnp.zeros((dim, query_rows.shape[0]), jnp.float32)
    for group, (start, count) in zip(groups, spans):
        weights = jnp.exp(scores[start : start + count, :] * inv_root - top)
        total = total + jnp.sum(weights, axis=0, keepdims=True)
        mixed = mixed + lax.dot_general(
            rows_of(group, 1),
            weights.astype(jnp.bfloat16),
            (((0,), (0,)), ((), ())),
            preferred_element_type=jnp.float32,
        )
    partial[:dim, :] = mixed
    row = lax.broadcasted_iota(jnp.int32, (STAT_ROWS, query_rows.shape[0]), 0)
    partial[dim:, :] = jnp.where(row == 0, top, total)


def merge_kernel(scale, plane, place, mine, theirs, payload, grads_half, grad_rows, *refs):
    stats, attended_own, terms, both_grads, both_attended, term_rows = (
        refs[0],
        refs[1],
        refs[2:-3],
        refs[-3],
        refs[-2],
        refs[-1],
    )
    tile, dim = grad_rows.shape
    half = grads_half.shape[1]
    top_a, top_b = mine[dim : dim + 1, :], theirs[dim : dim + 1, :]
    sum_a, sum_b = mine[dim + 1 : dim + 2, :], theirs[dim + 1 : dim + 2, :]
    top = jnp.maximum(top_a, top_b)
    share_a, share_b = jnp.exp(top_a - top), jnp.exp(top_b - top)
    total = share_a * sum_a + share_b * sum_b
    mixed = mine[:dim, :] * (share_a / total) + theirs[:dim, :] * (share_b / total)
    attended_t = mixed.astype(jnp.bfloat16).astype(jnp.float32)
    both_tiles(place, grad_rows[...], payload[:, half:], both_grads)
    row_dot = jnp.sum(both_grads[...].astype(jnp.float32).T * attended_t, axis=0, keepdims=True)
    row = lax.broadcasted_iota(jnp.int32, (STAT_ROWS, mixed.shape[1]), 0)
    stats[...] = jnp.where(row == 0, top + jnp.log(total), row_dot)
    both_attended[...] = attended_t.T.astype(jnp.bfloat16)
    rows_mine = both_attended[pl.ds(pl.multiple_of(place[0] * tile, tile), tile), :]
    rows_theirs = both_attended[pl.ds(pl.multiple_of((1 - place[0]) * tile, tile), tile), :]
    attended_own[...] = rows_mine
    if not terms:
        return
    contract = (((0,), (0,)), ((), ()))
    term = lax.dot_general(
        rows_mine, grads_half[...], contract, preferred_element_type=jnp.float32
    )
    term = term + lax.dot_general(
        rows_theirs, payload[:, :half], contract, preferred_element_type=jnp.float32
    )
    term_rows[...] = term * scale
    count = dim // plane
    for order, out in enumerate(terms):
        chunk = place[1] ^ order
        out[...] = term_rows[pl.ds(pl.multiple_of(chunk * count, count), count), :].astype(jnp.bfloat16)


def split_groups(layout, refs):
    groups, start = [], 0
    for count in layout:
        groups.append(refs[start : start + count])
        start += count
    return groups, refs[start:]


def backward_kernel(
    inv_root, layout, targets, place, stats, both_queries, payload, grad_rows, *refs
):
    groups, rest = split_groups(layout, refs)
    count = 1 + max(out for out, _ in targets)
    outs, (query_own, query_other, both_grads, both_out) = rest[:count], rest[count:]
    tile, dim = grad_rows.shape
    columns = payload.shape[1]
    both_tiles(place, grad_rows[...], payload[:, columns - dim :], both_grads)
    query_rows, out_grads = both_queries[...], both_grads[...]
    level, row_dot = stats[0:1, :], stats[1:2, :]
    along = (((1,), (1,)), ((), ()))
    query_grad = jnp.zeros((dim, 2 * tile), jnp.float32)
    for group, (target, first) in zip(groups, targets):
        out, tiles = outs[target], group[0].shape[0]
        keys, values = rows_of(group, 0), rows_of(group, 1)
        scores = lax.dot_general(keys, query_rows, along, preferred_element_type=jnp.float32)
        probability = jnp.exp(scores * inv_root - level)
        prob_grad = lax.dot_general(values, out_grads, along, preferred_element_type=jnp.float32)
        score_grad = (probability * (prob_grad - row_dot)).astype(jnp.bfloat16)
        shape = (tiles,) + out.shape[2:]
        key_grad = jnp.dot(score_grad, query_rows, preferred_element_type=jnp.float32) * inv_root
        value_grad = jnp.dot(
            probability.astype(jnp.bfloat16), out_grads, preferred_element_type=jnp.float32
        )
        out[first : first + tiles, 0] = key_grad.reshape(shape).astype(out.dtype)
        out[first : first + tiles, 1] = value_grad.reshape(shape).astype(out.dtype)
        query_grad = query_grad + lax.dot_general(
            keys, score_grad, (((0,), (0,)), ((), ())), preferred_element_type=jnp.float32
        )
    both_out[...] = query_grad.T * inv_root
    query_own[...] = both_out[pl.ds(pl.multiple_of(place[0] * tile, tile), tile), :]
    other = both_out[pl.ds(pl.multiple_of((1 - place[0]) * tile, tile), tile), :]
    other = other.astype(jnp.bfloat16)
    rows = query_other.shape[0]
    for block in range(tile // rows):
        query_other[:, block * dim : (block + 1) * dim] = other[block * rows : (block + 1) * rows]


def assemble_kernel(flipped, rows, place, part, *refs):
    whole, rows_ref, done = refs[-3 - flipped], refs[-2], refs[-1]
    count, width = rows_ref.shape
    core = 1 - place[0] if flipped else place[0]
    columns = pl.ds(pl.multiple_of(core * width, width), width)
    copies = []
    for order in range(count // rows):
        span = pl.ds(pl.multiple_of((place[1] ^ order) * rows, rows), rows)
        rows_ref[span, :] = part[order * rows : (order + 1) * rows, :].astype(jnp.float32)
        copies.append(
            pltpu.make_async_copy(rows_ref.at[span, :], whole.at[span, columns], done.at[order])
        )
        copies[-1].start()
    if flipped:
        query_own, grad_query = refs[0], refs[-3]
        dim, step = grad_query.shape[1], part.shape[0] - count
        for block in range(width // dim):
            piece = part[count:, block * dim : (block + 1) * dim].astype(jnp.float32)
            span = slice(block * step, (block + 1) * step)
            grad_query[span, :] = (query_own[span, :] + piece).astype(jnp.bfloat16)
    for copy in copies:
        copy.wait()


def assemble(flipped, place, part, rows, shape, whole=None, query_own=None):
    anywhere = pl.BlockSpec(memory_space=pl.ANY)
    outs, out_specs, operands, in_specs = shape, anywhere, (place, part), [SMEM, VMEM]
    if flipped:
        outs, out_specs = (shape, shaped(*query_own.shape)), (anywhere, VMEM)
        operands, in_specs = operands + (query_own, whole), in_specs + [VMEM, anywhere]
    return pl.pallas_call(
        functools.partial(assemble_kernel, flipped, rows),
        out_shape=outs,
        in_specs=in_specs,
        out_specs=out_specs,
        scratch_shapes=[
            pltpu.VMEM((shape.shape[0], part.shape[1]), jnp.float32),
            pltpu.SemaphoreType.DMA((shape.shape[0] // rows,)),
        ],
        input_output_aliases={3: 0} if flipped else {},
        compiler_params=PARAMS,
    )(*operands)


def pack_kernel(*refs):
    start = 0
    for piece in refs[:-1]:
        refs[-1][start : start + piece.shape[0], :] = piece[...]
        start += piece.shape[0]


def combine_kernel(column, *refs):
    arrived, pieces = refs[: -column.shape[0]], refs[-column.shape[0] :]
    for k, piece in enumerate(pieces):
        total = column[k]
        for block in arrived:
            total = total + block[k].astype(jnp.float32)
        piece[...] = total.astype(piece.dtype)


def shaped(*shape, kind=jnp.bfloat16):
    return jax.ShapeDtypeStruct(shape, kind)


def kernel_call(kernel, operands, outs, scratch=(), cost=None):
    many = isinstance(outs, (list, tuple))
    return pl.pallas_call(
        kernel,
        out_shape=outs,
        in_specs=[SMEM] + [VMEM] * (len(operands) - 1),
        out_specs=[VMEM] * len(outs) if many else VMEM,
        scratch_shapes=list(scratch),
        compiler_params=PARAMS,
        cost_estimate=cost,
    )(*operands)


def cost_of(flops, moved):
    return pl.CostEstimate(flops=int(flops), bytes_accessed=int(moved), transcendentals=0)


PLANE_BITS = ((0, 0), (0, 1), (2, 0), (2, 1))


def sum_over_plane(terms):
    summed = terms[0].astype(jnp.float32)
    for term, bit in zip(terms[1:], PLANE_BITS[1:]):
        summed = summed + flip(term, ("frame", "width"), bit).astype(jnp.float32)
    return summed.astype(jnp.bfloat16)


def join_sum(part, query_own, query_other, place):
    plane = len(part)
    pieces = part + [query_other]
    part = pl.pallas_call(
        pack_kernel,
        out_shape=shaped(sum(p.shape[0] for p in pieces), pieces[0].shape[1]),
        in_specs=[VMEM] * len(pieces),
        out_specs=VMEM,
        compiler_params=PARAMS,
    )(*pieces)
    other = flip(part, ("frame",), (1,))
    rows = (part.shape[0] - query_other.shape[0]) // plane
    shape = shaped(plane * rows, 2 * part.shape[1], kind=jnp.float32)
    whole = assemble(False, place, part, rows, shape)
    return assemble(True, place, other, rows, shape, whole, query_own)


def body(queries, key_vectors, value_vectors, out_weight, projected_grad):
    head_dim = queries.shape[-1]
    model_dim = out_weight.shape[1]
    half = model_dim // 2
    inv_root = 1.0 / math.sqrt(head_dim)
    extents = tuple(lax.axis_size(axis) for axis in AXES)
    assert extents[0] == 4
    small = extents[1:] == (4, 2)
    frame, height, width = (lax.axis_index(axis) for axis in AXES)
    core = frame % 2
    place = jnp.stack([core, (frame // 2) * 2 + width, height]).astype(jnp.int32)
    query_rows = queries.reshape(-1, head_dim)
    grads = projected_grad.reshape(-1, model_dim)
    tile = query_rows.shape[0]

    own = jnp.stack((key_vectors.reshape(tile, head_dim), value_vectors.reshape(tile, head_dim)))
    cross = [(2 * s + y, 2 * p + 1 - y) for s, p in ((2, 1), (1, 2)) for y in (0, 1)]

    if small:
        swap = [(0, 1), (1, 0)]
        tiles = fetch(own, "height")
        own_beside = lax.ppermute(own[None], "width", swap)
        others = jnp.stack(tiles)
        column = jnp.stack([own] + tiles)
        others, column, own_beside, query_rows_late = lax.optimization_barrier(
            (others, column, own_beside, query_rows)
        )
        others_beside = lax.ppermute(others, "width", swap)
        far = [
            lax.ppermute(column, ("frame", "width"), cross),
            lax.ppermute(column, "frame", [(2, 0), (1, 3)]),
        ]
        blocks = [column, own_beside, others_beside, *far]
        layout = (1, 1, 1, 2)
        targets = ((0, 0), (1, 0), (1, 1), (2, 0))
        column_tiles, kinds = 1 + others.shape[0], 3
    else:
        query_rows_late = query_rows
        column = jnp.stack([own] + fetch(own, "height"))
        beside = fetch(column, "width")
        everything = jnp.concatenate([column] + beside, axis=0)
        far = [
            lax.ppermute(everything[:, :, : tile // 2], "frame", [(2, 0), (1, 3)]),
            lax.ppermute(everything[:, :, tile // 2 :], "frame", [(2, 1), (1, 2)]),
        ]
        blocks = [column] + beside + far
        layout = (1,) * (1 + len(beside)) + (2,)
        targets = tuple((k, 0) for k in range(len(layout)))
        column_tiles, kinds = column.shape[0], len(layout)
    queries_other = flip(query_rows_late, ("frame",), (1,))
    payload, grads_half, grad_rows, both_queries = kernel_call(
        token_kernel,
        (place, query_rows, queries_other, grads, out_weight),
        (
            shaped(tile, half + head_dim),
            shaped(tile, half),
            shaped(tile, head_dim),
            shaped(2 * tile, head_dim),
        ),
        cost=cost_of(2 * tile * head_dim * model_dim, 4 * tile * model_dim),
    )
    grad_shapes = [(column_tiles, 2, tile, head_dim)] * (kinds - 1)
    grad_shapes.append((column_tiles, 2, tile, head_dim) if small else far[0].shape)
    key_count = sum(shape[0] * shape[2] for shape in grad_shapes)
    product = 2 * key_count * 2 * tile * head_dim
    moved = sum(b.size * 2 for b in blocks)

    def forward(operands, groups, carried):
        keys, start = 0, 0
        for count in groups:
            keys += operands[start].shape[0] * operands[start].shape[2]
            start += count
        return pl.pallas_call(
            functools.partial(forward_kernel, inv_root, groups, bool(carried)),
            out_shape=shaped(head_dim + STAT_ROWS, 2 * tile, kind=jnp.float32),
            in_specs=[VMEM] * (1 + len(operands) + len(carried)),
            out_specs=VMEM,
            scratch_shapes=[pltpu.VMEM((keys, 2 * tile), jnp.float32)],
            compiler_params=PARAMS,
            cost_estimate=cost_of(8 * keys * tile * head_dim, moved * keys // key_count),
        )(both_queries, *operands, *carried)

    partial = forward([blocks[0]] + far, (1, 2), ())
    beside = blocks[1 : -len(far)]
    payload, partial, *beside = lax.optimization_barrier((payload, partial, *beside))
    payload = flip(payload, ("frame",), (1,))
    partial = forward(beside, (1,) * len(beside), (partial,))
    blocks = [blocks[0]] + beside + far
    partial_other = flip(partial, ("frame",), (1,))
    plane = 4
    chunks = plane if small else 0
    merged = kernel_call(
        functools.partial(merge_kernel, 1.0 / float(math.prod(extents)), plane),
        (place, partial, partial_other, payload, grads_half, grad_rows),
        (
            shaped(STAT_ROWS, 2 * tile, kind=jnp.float32),
            shaped(tile, head_dim),
            *[shaped(head_dim // plane, half)] * chunks,
        ),
        scratch=(
            pltpu.VMEM((2 * tile, head_dim), jnp.bfloat16),
            pltpu.VMEM((2 * tile, head_dim), jnp.bfloat16),
            pltpu.VMEM((head_dim, half), jnp.float32),
        ),
        cost=cost_of(4 * tile * head_dim * half, 4 * tile * model_dim),
    )
    stats, attended, *terms = merged
    back = kernel_call(
        functools.partial(backward_kernel, inv_root, layout, targets),
        (place, stats, both_queries, payload, grad_rows, *blocks),
        (
            shaped(*grad_shapes[0], kind=jnp.float32),
            *[shaped(*shape) for shape in grad_shapes[1:]],
            shaped(tile, head_dim, kind=jnp.float32),
            shaped(tile * head_dim // half, half),
        ),
        scratch=(
            pltpu.VMEM((2 * tile, head_dim), jnp.bfloat16),
            pltpu.VMEM((2 * tile, head_dim), jnp.float32),
        ),
        cost=cost_of(5 * product, 2 * moved),
    )
    if small:
        terms[0], *back = lax.optimization_barrier((terms[0], *back))
        part = sum_over_plane(terms)
        other = flip(part, ("height",), (1,))
        part = (part.astype(jnp.float32) + other.astype(jnp.float32)).astype(jnp.bfloat16)
        part, attended = lax.optimization_barrier((part, attended))
        other = flip(part, ("height",), (2,))
    else:
        weight_term = jnp.einsum("td,tm->dm", attended, grads, preferred_element_type=jnp.float32)
        grad_out_weight = lax.psum(weight_term, AXES) / float(math.prod(extents))
    projected = (
        jnp.dot(attended, out_weight, preferred_element_type=jnp.float32)
        .astype(jnp.bfloat16)
        .reshape(projected_grad.shape)
    )
    column_grad, *beside_grads, far_grad, query_own, query_other = back
    if small:
        arrived = [
            lax.ppermute(beside_grads[0], "width", [(0, 1), (1, 0)]),
            lax.ppermute(far_grad, ("frame", "width"), [(p, s) for s, p in cross]),
            lax.ppermute(far_grad, "frame", [(0, 2), (3, 1)]),
        ]
        other, projected = lax.optimization_barrier((other, projected))
        part = (part.astype(jnp.float32) + other.astype(jnp.float32)).astype(jnp.bfloat16)
        part, column_grad = lax.optimization_barrier((part, column_grad))
        part = [part] + [flip(part, ("frame", "width"), bit) for bit in PLANE_BITS[1:]]
        shape = column_grad.shape[1:]
        pieces = pl.pallas_call(
            combine_kernel,
            out_shape=[shaped(*shape, kind=jnp.float32)] + [shaped(*shape)] * (column_tiles - 1),
            in_specs=[VMEM] * 4,
            out_specs=[VMEM] * column_tiles,
            compiler_params=PARAMS,
        )(column_grad, *arrived)
    else:
        arrived = jnp.concatenate(
            (
                lax.ppermute(far_grad, "frame", [(0, 2), (3, 1)]),
                lax.ppermute(far_grad, "frame", [(1, 2), (2, 1)]),
            ),
            axis=2,
        ).astype(jnp.float32)
        pieces = [column_grad] + [b.astype(jnp.float32) for b in beside_grads]
        span = column_tiles
        pieces = [p + arrived[i * span : (i + 1) * span] for i, p in enumerate(pieces)]
        column_grad = give_back(pieces, "width")
        pieces = [column_grad[k] for k in range(column_tiles)]
    if small:
        grad_out_weight, grad_query = join_sum(part, query_own, query_other, place)
    else:
        query_other = flip(query_other, ("frame",), (1,)).reshape(-1, half // head_dim, head_dim)
        query_other = query_other.transpose(1, 0, 2).reshape(tile, head_dim)
        grad_query = (query_own + query_other.astype(jnp.float32)).astype(jnp.bfloat16)
    own_grad = give_back(pieces, "height")
    grad_key = own_grad[0].astype(jnp.bfloat16).reshape(key_vectors.shape)
    grad_value = own_grad[1].astype(jnp.bfloat16).reshape(value_vectors.shape)
    grad_query = grad_query.reshape(queries.shape)
    return (projected, grad_query, grad_key, grad_value, grad_out_weight)


def solution(mesh):
    tokens = P("frame", "height", "width", None)
    return jax.shard_map(
        body,
        mesh=mesh,
        in_specs=(tokens, tokens, tokens, P(), tokens),
        out_specs=(tokens, tokens, tokens, tokens, P()),
        check_vma=False,
    )
```

```python
import functools
import math

import jax
import jax.numpy as jnp
from jax import lax
from jax.experimental import pallas as pl
from jax.experimental.pallas import tpu as pltpu
from jax.sharding import PartitionSpec as P

AXES = ("frame", "height", "width")
VMEM = pl.BlockSpec(memory_space=pltpu.VMEM)
SMEM = pl.BlockSpec(memory_space=pltpu.SMEM)
PARAMS = pltpu.CompilerParams(vmem_limit_bytes=24 * 1024 * 1024)
STAT_ROWS = 8


def window_of(position, extent):
    span = min(3, extent)
    start = max(0, min(position - 1, extent - 3))
    return range(start, start + span)


def routes_of(extent):
    first = [(p ^ 1, p) for p in range(extent) if (p ^ 1) in window_of(p, extent)]
    if extent > 4:
        first = [(p + 1, p) for p in range(extent - 1)]
    wanted = [(s, p) for p in range(extent) for s in window_of(p, extent) if s != p]
    wanted.sort(key=lambda pair: (pair[0] ^ pair[1], pair))
    routes = [first]
    for pair in wanted:
        if pair in first:
            continue
        for route in routes[1:]:
            if all(pair[0] != s and pair[1] != p for s, p in route):
                route.append(pair)
                break
        else:
            routes.append([pair])
    return [route for route in routes if route]


def slots_of(extent):
    routes = routes_of(extent)
    arrivals = [[c for c, r in enumerate(routes) if any(q == p for _, q in r)] for p in range(extent)]
    return [[arrivals[p][k] for p in range(extent)] for k in range(min(3, extent) - 1)]


def chosen(options, choice, axis):
    value = options[choice[0]]
    position = lax.axis_index(axis)
    for option in sorted(set(choice)):
        if option != choice[0]:
            here = functools.reduce(
                jnp.logical_or, [position == p for p, c in enumerate(choice) if c == option]
            )
            value = jnp.where(here, options[option], value)
    return value


def fetch(block, axis):
    extent = lax.axis_size(axis)
    routes = routes_of(extent)
    arrived = [lax.ppermute(block, axis, route) for route in routes]
    tiles = []
    for slot in slots_of(extent):
        used = sorted(set(slot))
        reached = sum(len(routes[c]) for c in used)
        if reached == extent:
            tiles.append(functools.reduce(jnp.add, [arrived[c] for c in used]))
        else:
            tiles.append(chosen(arrived, slot, axis))
    return tiles


def give_back(pieces, axis):
    extent = lax.axis_size(axis)
    slots = slots_of(extent)
    summed = pieces[0]
    for c, route in reversed(list(enumerate(routes_of(extent)))):
        holders = [next((k for k in range(len(slots)) if slots[k][p] == c), None) for p in range(extent)]
        used = sorted({k for k in holders if k is not None})
        choice = [k if k is not None else used[0] for k in holders]
        outgoing = chosen({k: pieces[k + 1] for k in used}, choice, axis).astype(jnp.bfloat16)
        back = lax.ppermute(outgoing, axis, [(p, s) for s, p in route])
        summed = summed + back.astype(jnp.float32)
    return summed


def flip(block, axes, bits):
    sizes = [lax.axis_size(axis) for axis in axes]
    route = []
    for flat in range(math.prod(sizes)):
        rest, target, scale = flat, 0, 1
        for size, bit in zip(reversed(sizes), reversed(bits)):
            target += ((rest % size) ^ bit) * scale
            rest //= size
            scale *= size
        route.append((flat, target))
    return lax.ppermute(block, axes, route)


def rows_of(refs, part):
    block = refs[0][:, part]
    for ref in refs[1:]:
        block = block + ref[:, part]
    return block.reshape(-1, block.shape[-1])


def token_kernel(
    place, queries, queries_other, grads, weight, payload, grads_half, grad_rows, both_queries
):
    half = grads_half.shape[1]
    product = lax.dot_general(
        grads[...], weight[...], (((1,), (1,)), ((), ())), preferred_element_type=jnp.float32
    ).astype(jnp.bfloat16)
    grad_rows[...] = product
    payload[:, half:] = product
    payload[:, :half] = grads[:, pl.ds(pl.multiple_of((1 - place[0]) * half, half), half)]
    grads_half[...] = grads[:, pl.ds(pl.multiple_of(place[0] * half, half), half)]
    both_tiles(place, queries[...], queries_other[...], both_queries)


def both_tiles(place, mine, theirs, both):
    tile = mine.shape[0]
    both[pl.ds(pl.multiple_of(place[0] * tile, tile), tile), :] = mine
    both[pl.ds(pl.multiple_of((1 - place[0]) * tile, tile), tile), :] = theirs


def forward_kernel(inv_root, layout, carried, both_queries, *refs):
    groups, rest = split_groups(layout, refs)
    partial, scores = rest[-2:]
    dim = both_queries.shape[1]
    query_rows = both_queries[...]
    top, start, spans = None, 0, []
    if carried:
        top = rest[0][dim : dim + 1, :]
    for group in groups:
        keys = rows_of(group, 0)
        piece = lax.dot_general(
            keys, query_rows, (((1,), (1,)), ((), ())), preferred_element_type=jnp.float32
        )
        scores[start : start + keys.shape[0], :] = piece
        spans.append((start, keys.shape[0]))
        start += keys.shape[0]
        piece_top = jnp.max(piece, axis=0, keepdims=True) * inv_root
        top = piece_top if top is None else jnp.maximum(top, piece_top)
    if carried:
        share = jnp.exp(rest[0][dim : dim + 1, :] - top)
        total = rest[0][dim + 1 : dim + 2, :] * share
        mixed = rest[0][:dim, :] * share
    else:
        total = jnp.zeros_like(top)
        mixed = jnp.zeros((dim, query_rows.shape[0]), jnp.float32)
    for group, (start, count) in zip(groups, spans):
        weights = jnp.exp(scores[start : start + count, :] * inv_root - top)
        total = total + jnp.sum(weights, axis=0, keepdims=True)
        mixed = mixed + lax.dot_general(
            rows_of(group, 1),
            weights.astype(jnp.bfloat16),
            (((0,), (0,)), ((), ())),
            preferred_element_type=jnp.float32,
        )
    partial[:dim, :] = mixed
    row = lax.broadcasted_iota(jnp.int32, (STAT_ROWS, query_rows.shape[0]), 0)
    partial[dim:, :] = jnp.where(row == 0, top, total)


def merge_kernel(scale, plane, place, mine, theirs, payload, grads_half, grad_rows, *refs):
    stats, attended_own, terms, both_grads, both_attended, term_rows = (
        refs[0],
        refs[1],
        refs[2:-3],
        refs[-3],
        refs[-2],
        refs[-1],
    )
    tile, dim = grad_rows.shape
    half = grads_half.shape[1]
    top_a, top_b = mine[dim : dim + 1, :], theirs[dim : dim + 1, :]
    sum_a, sum_b = mine[dim + 1 : dim + 2, :], theirs[dim + 1 : dim + 2, :]
    top = jnp.maximum(top_a, top_b)
    share_a, share_b = jnp.exp(top_a - top), jnp.exp(top_b - top)
    total = share_a * sum_a + share_b * sum_b
    mixed = mine[:dim, :] * (share_a / total) + theirs[:dim, :] * (share_b / total)
    attended_t = mixed.astype(jnp.bfloat16).astype(jnp.float32)
    both_tiles(place, grad_rows[...], payload[:, half:], both_grads)
    row_dot = jnp.sum(both_grads[...].astype(jnp.float32).T * attended_t, axis=0, keepdims=True)
    row = lax.broadcasted_iota(jnp.int32, (STAT_ROWS, mixed.shape[1]), 0)
    stats[...] = jnp.where(row == 0, top + jnp.log(total), row_dot)
    both_attended[...] = attended_t.T.astype(jnp.bfloat16)
    rows_mine = both_attended[pl.ds(pl.multiple_of(place[0] * tile, tile), tile), :]
    rows_theirs = both_attended[pl.ds(pl.multiple_of((1 - place[0]) * tile, tile), tile), :]
    attended_own[...] = rows_mine
    if not terms:
        return
    contract = (((0,), (0,)), ((), ()))
    term = lax.dot_general(
        rows_mine, grads_half[...], contract, preferred_element_type=jnp.float32
    )
    term = term + lax.dot_general(
        rows_theirs, payload[:, :half], contract, preferred_element_type=jnp.float32
    )
    term_rows[...] = term * scale
    count = dim // plane
    for order, out in enumerate(terms):
        chunk = place[1] ^ order
        out[...] = term_rows[pl.ds(pl.multiple_of(chunk * count, count), count), :].astype(jnp.bfloat16)


def split_groups(layout, refs):
    groups, start = [], 0
    for count in layout:
        groups.append(refs[start : start + count])
        start += count
    return groups, refs[start:]


def backward_kernel(
    inv_root, layout, targets, place, stats, both_queries, payload, grad_rows, *refs
):
    groups, rest = split_groups(layout, refs)
    count = 1 + max(out for out, _ in targets)
    outs, (query_own, query_other, both_grads, both_out) = rest[:count], rest[count:]
    tile, dim = grad_rows.shape
    columns = payload.shape[1]
    both_tiles(place, grad_rows[...], payload[:, columns - dim :], both_grads)
    query_rows, out_grads = both_queries[...], both_grads[...]
    level, row_dot = stats[0:1, :], stats[1:2, :]
    along = (((1,), (1,)), ((), ()))
    query_grad = jnp.zeros((dim, 2 * tile), jnp.float32)
    for group, (target, first) in zip(groups, targets):
        out, tiles = outs[target], group[0].shape[0]
        keys, values = rows_of(group, 0), rows_of(group, 1)
        scores = lax.dot_general(keys, query_rows, along, preferred_element_type=jnp.float32)
        probability = jnp.exp(scores * inv_root - level)
        prob_grad = lax.dot_general(values, out_grads, along, preferred_element_type=jnp.float32)
        score_grad = (probability * (prob_grad - row_dot)).astype(jnp.bfloat16)
        shape = (tiles,) + out.shape[2:]
        key_grad = jnp.dot(score_grad, query_rows, preferred_element_type=jnp.float32) * inv_root
        value_grad = jnp.dot(
            probability.astype(jnp.bfloat16), out_grads, preferred_element_type=jnp.float32
        )
        out[first : first + tiles, 0] = key_grad.reshape(shape).astype(out.dtype)
        out[first : first + tiles, 1] = value_grad.reshape(shape).astype(out.dtype)
        query_grad = query_grad + lax.dot_general(
            keys, score_grad, (((0,), (0,)), ((), ())), preferred_element_type=jnp.float32
        )
    both_out[...] = query_grad.T * inv_root
    query_own[...] = both_out[pl.ds(pl.multiple_of(place[0] * tile, tile), tile), :]
    other = both_out[pl.ds(pl.multiple_of((1 - place[0]) * tile, tile), tile), :]
    other = other.astype(jnp.bfloat16)
    rows = query_other.shape[0]
    for block in range(tile // rows):
        query_other[:, block * dim : (block + 1) * dim] = other[block * rows : (block + 1) * rows]


def assemble_kernel(flipped, rows, place, part, *refs):
    whole, rows_ref, done = refs[-3 - flipped], refs[-2], refs[-1]
    count, width = rows_ref.shape
    core = 1 - place[0] if flipped else place[0]
    columns = pl.ds(pl.multiple_of(core * width, width), width)
    copies = []
    for order in range(count // rows):
        span = pl.ds(pl.multiple_of((place[1] ^ order) * rows, rows), rows)
        rows_ref[span, :] = part[order * rows : (order + 1) * rows, :].astype(jnp.float32)
        copies.append(
            pltpu.make_async_copy(rows_ref.at[span, :], whole.at[span, columns], done.at[order])
        )
        copies[-1].start()
    if flipped:
        query_own, grad_query = refs[0], refs[-3]
        dim, step = grad_query.shape[1], part.shape[0] - count
        for block in range(width // dim):
            piece = part[count:, block * dim : (block + 1) * dim].astype(jnp.float32)
            span = slice(block * step, (block + 1) * step)
            grad_query[span, :] = (query_own[span, :] + piece).astype(jnp.bfloat16)
    for copy in copies:
        copy.wait()


def assemble(flipped, place, part, rows, shape, whole=None, query_own=None):
    anywhere = pl.BlockSpec(memory_space=pl.ANY)
    outs, out_specs, operands, in_specs = shape, anywhere, (place, part), [SMEM, VMEM]
    if flipped:
        outs, out_specs = (shape, shaped(*query_own.shape)), (anywhere, VMEM)
        operands, in_specs = operands + (query_own, whole), in_specs + [VMEM, anywhere]
    return pl.pallas_call(
        functools.partial(assemble_kernel, flipped, rows),
        out_shape=outs,
        in_specs=in_specs,
        out_specs=out_specs,
        scratch_shapes=[
            pltpu.VMEM((shape.shape[0], part.shape[1]), jnp.float32),
            pltpu.SemaphoreType.DMA((shape.shape[0] // rows,)),
        ],
        input_output_aliases={3: 0} if flipped else {},
        compiler_params=PARAMS,
    )(*operands)


def pack_kernel(*refs):
    start = 0
    for piece in refs[:-1]:
        refs[-1][start : start + piece.shape[0], :] = piece[...]
        start += piece.shape[0]


def combine_kernel(column, *refs):
    arrived, pieces = refs[: -column.shape[0]], refs[-column.shape[0] :]
    for k, piece in enumerate(pieces):
        total = column[k]
        for block in arrived:
            total = total + block[k].astype(jnp.float32)
        piece[...] = total.astype(piece.dtype)


def shaped(*shape, kind=jnp.bfloat16):
    return jax.ShapeDtypeStruct(shape, kind)


def kernel_call(kernel, operands, outs, scratch=(), cost=None):
    many = isinstance(outs, (list, tuple))
    return pl.pallas_call(
        kernel,
        out_shape=outs,
        in_specs=[SMEM] + [VMEM] * (len(operands) - 1),
        out_specs=[VMEM] * len(outs) if many else VMEM,
        scratch_shapes=list(scratch),
        compiler_params=PARAMS,
        cost_estimate=cost,
    )(*operands)


def cost_of(flops, moved):
    return pl.CostEstimate(flops=int(flops), bytes_accessed=int(moved), transcendentals=0)


PLANE_BITS = ((0, 0), (0, 1), (2, 0), (2, 1))


def sum_over_plane(terms):
    summed = terms[0].astype(jnp.float32)
    for term, bit in zip(terms[1:], PLANE_BITS[1:]):
        summed = summed + flip(term, ("frame", "width"), bit).astype(jnp.float32)
    return summed.astype(jnp.bfloat16)


def join_sum(part, query_own, query_other, place):
    plane = len(part)
    pieces = part + [query_other]
    part = pl.pallas_call(
        pack_kernel,
        out_shape=shaped(sum(p.shape[0] for p in pieces), pieces[0].shape[1]),
        in_specs=[VMEM] * len(pieces),
        out_specs=VMEM,
        compiler_params=PARAMS,
    )(*pieces)
    other = flip(part, ("frame",), (1,))
    rows = (part.shape[0] - query_other.shape[0]) // plane
    shape = shaped(plane * rows, 2 * part.shape[1], kind=jnp.float32)
    whole = assemble(False, place, part, rows, shape)
    return assemble(True, place, other, rows, shape, whole, query_own)


def body(queries, key_vectors, value_vectors, out_weight, projected_grad):
    head_dim = queries.shape[-1]
    model_dim = out_weight.shape[1]
    half = model_dim // 2
    inv_root = 1.0 / math.sqrt(head_dim)
    extents = tuple(lax.axis_size(axis) for axis in AXES)
    assert extents[0] == 4
    small = extents[1:] == (4, 2)
    frame, height, width = (lax.axis_index(axis) for axis in AXES)
    core = frame % 2
    place = jnp.stack([core, (frame // 2) * 2 + width, height]).astype(jnp.int32)
    query_rows = queries.reshape(-1, head_dim)
    grads = projected_grad.reshape(-1, model_dim)
    tile = query_rows.shape[0]

    own = jnp.stack((key_vectors.reshape(tile, head_dim), value_vectors.reshape(tile, head_dim)))
    cross = [(2 * s + y, 2 * p + 1 - y) for s, p in ((2, 1), (1, 2)) for y in (0, 1)]

    if small:
        swap = [(0, 1), (1, 0)]
        tiles = fetch(own, "height")
        own_beside = lax.ppermute(own[None], "width", swap)
        others = jnp.stack(tiles)
        column = jnp.stack([own] + tiles)
        others, column, own_beside, query_rows_late = lax.optimization_barrier(
            (others, column, own_beside, query_rows)
        )
        others_beside = lax.ppermute(others, "width", swap)
        far = [
            lax.ppermute(column, "frame", [(2, 0), (1, 3)]),
            lax.ppermute(column, ("frame", "width"), cross),
        ]
        blocks = [column, own_beside, others_beside, *far]
        layout = (1, 1, 1, 2)
        targets = ((0, 0), (1, 0), (1, 1), (2, 0))
        column_tiles, kinds = 1 + others.shape[0], 3
    else:
        query_rows_late = query_rows
        column = jnp.stack([own] + fetch(own, "height"))
        beside = fetch(column, "width")
        everything = jnp.concatenate([column] + beside, axis=0)
        far = [
            lax.ppermute(everything[:, :, : tile // 2], "frame", [(2, 0), (1, 3)]),
            lax.ppermute(everything[:, :, tile // 2 :], "frame", [(2, 1), (1, 2)]),
        ]
        blocks = [column] + beside + far
        layout = (1,) * (1 + len(beside)) + (2,)
        targets = tuple((k, 0) for k in range(len(layout)))
        column_tiles, kinds = column.shape[0], len(layout)
    queries_other = flip(query_rows_late, ("frame",), (1,))
    payload, grads_half, grad_rows, both_queries = kernel_call(
        token_kernel,
        (place, query_rows, queries_other, grads, out_weight),
        (
            shaped(tile, half + head_dim),
            shaped(tile, half),
            shaped(tile, head_dim),
            shaped(2 * tile, head_dim),
        ),
        cost=cost_of(2 * tile * head_dim * model_dim, 4 * tile * model_dim),
    )
    grad_shapes = [(column_tiles, 2, tile, head_dim)] * (kinds - 1)
    grad_shapes.append((column_tiles, 2, tile, head_dim) if small else far[0].shape)
    key_count = sum(shape[0] * shape[2] for shape in grad_shapes)
    product = 2 * key_count * 2 * tile * head_dim
    moved = sum(b.size * 2 for b in blocks)

    def forward(operands, groups, carried):
        keys, start = 0, 0
        for count in groups:
            keys += operands[start].shape[0] * operands[start].shape[2]
            start += count
        return pl.pallas_call(
            functools.partial(forward_kernel, inv_root, groups, bool(carried)),
            out_shape=shaped(head_dim + STAT_ROWS, 2 * tile, kind=jnp.float32),
            in_specs=[VMEM] * (1 + len(operands) + len(carried)),
            out_specs=VMEM,
            scratch_shapes=[pltpu.VMEM((keys, 2 * tile), jnp.float32)],
            compiler_params=PARAMS,
            cost_estimate=cost_of(8 * keys * tile * head_dim, moved * keys // key_count),
        )(both_queries, *operands, *carried)

    partial = forward([blocks[0]] + far, (1, 2), ())
    beside = blocks[1 : -len(far)]
    payload, partial, *beside = lax.optimization_barrier((payload, partial, *beside))
    payload = flip(payload, ("frame",), (1,))
    partial = forward(beside, (1,) * len(beside), (partial,))
    blocks = [blocks[0]] + beside + far
    partial_other = flip(partial, ("frame",), (1,))
    plane = 4
    chunks = plane if small else 0
    merged = kernel_call(
        functools.partial(merge_kernel, 1.0 / float(math.prod(extents)), plane),
        (place, partial, partial_other, payload, grads_half, grad_rows),
        (
            shaped(STAT_ROWS, 2 * tile, kind=jnp.float32),
            shaped(tile, head_dim),
            *[shaped(head_dim // plane, half)] * chunks,
        ),
        scratch=(
            pltpu.VMEM((2 * tile, head_dim), jnp.bfloat16),
            pltpu.VMEM((2 * tile, head_dim), jnp.bfloat16),
            pltpu.VMEM((head_dim, half), jnp.float32),
        ),
        cost=cost_of(4 * tile * head_dim * half, 4 * tile * model_dim),
    )
    stats, attended, *terms = merged
    back = kernel_call(
        functools.partial(backward_kernel, inv_root, layout, targets),
        (place, stats, both_queries, payload, grad_rows, *blocks),
        (
            shaped(*grad_shapes[0], kind=jnp.float32),
            *[shaped(*shape) for shape in grad_shapes[1:]],
            shaped(tile, head_dim, kind=jnp.float32),
            shaped(tile * head_dim // half, half),
        ),
        scratch=(
            pltpu.VMEM((2 * tile, head_dim), jnp.bfloat16),
            pltpu.VMEM((2 * tile, head_dim), jnp.float32),
        ),
        cost=cost_of(5 * product, 2 * moved),
    )
    if small:
        terms[0], *back = lax.optimization_barrier((terms[0], *back))
        part = sum_over_plane(terms)
        other = flip(part, ("height",), (1,))
        part = (part.astype(jnp.float32) + other.astype(jnp.float32)).astype(jnp.bfloat16)
        part, attended = lax.optimization_barrier((part, attended))
        other = flip(part, ("height",), (2,))
    else:
        weight_term = jnp.einsum("td,tm->dm", attended, grads, preferred_element_type=jnp.float32)
        grad_out_weight = lax.psum(weight_term, AXES) / float(math.prod(extents))
    projected = (
        jnp.dot(attended, out_weight, preferred_element_type=jnp.float32)
        .astype(jnp.bfloat16)
        .reshape(projected_grad.shape)
    )
    column_grad, *beside_grads, far_grad, query_own, query_other = back
    if small:
        far_grad, projected = lax.optimization_barrier((far_grad, projected))
        arrived = [
            lax.ppermute(beside_grads[0], "width", [(0, 1), (1, 0)]),
            lax.ppermute(far_grad, "frame", [(0, 2), (3, 1)]),
            lax.ppermute(far_grad, ("frame", "width"), [(p, s) for s, p in cross]),
        ]
        other, projected = lax.optimization_barrier((other, projected))
        part = (part.astype(jnp.float32) + other.astype(jnp.float32)).astype(jnp.bfloat16)
        part, column_grad = lax.optimization_barrier((part, column_grad))
        part = [part] + [flip(part, ("frame", "width"), bit) for bit in PLANE_BITS[1:]]
        shape = column_grad.shape[1:]
        pieces = pl.pallas_call(
            combine_kernel,
            out_shape=[shaped(*shape, kind=jnp.float32)] + [shaped(*shape)] * (column_tiles - 1),
            in_specs=[VMEM] * 4,
            out_specs=[VMEM] * column_tiles,
            compiler_params=PARAMS,
        )(column_grad, *arrived)
    else:
        arrived = jnp.concatenate(
            (
                lax.ppermute(far_grad, "frame", [(0, 2), (3, 1)]),
                lax.ppermute(far_grad, "frame", [(1, 2), (2, 1)]),
            ),
            axis=2,
        ).astype(jnp.float32)
        pieces = [column_grad] + [b.astype(jnp.float32) for b in beside_grads]
        span = column_tiles
        pieces = [p + arrived[i * span : (i + 1) * span] for i, p in enumerate(pieces)]
        column_grad = give_back(pieces, "width")
        pieces = [column_grad[k] for k in range(column_tiles)]
    if small:
        grad_out_weight, grad_query = join_sum(part, query_own, query_other, place)
    else:
        query_other = flip(query_other, ("frame",), (1,)).reshape(-1, half // head_dim, head_dim)
        query_other = query_other.transpose(1, 0, 2).reshape(tile, head_dim)
        grad_query = (query_own + query_other.astype(jnp.float32)).astype(jnp.bfloat16)
    own_grad = give_back(pieces, "height")
    grad_key = own_grad[0].astype(jnp.bfloat16).reshape(key_vectors.shape)
    grad_value = own_grad[1].astype(jnp.bfloat16).reshape(value_vectors.shape)
    grad_query = grad_query.reshape(queries.shape)
    return (projected, grad_query, grad_key, grad_value, grad_out_weight)


def solution(mesh):
    tokens = P("frame", "height", "width", None)
    return jax.shard_map(
        body,
        mesh=mesh,
        in_specs=(tokens, tokens, tokens, P(), tokens),
        out_specs=(tokens, tokens, tokens, tokens, P()),
        check_vma=False,
    )
```

```python
import functools
import math

import jax
import jax.numpy as jnp
from jax import lax
from jax.experimental import pallas as pl
from jax.experimental.pallas import tpu as pltpu
from jax.sharding import PartitionSpec as P

AXES = ("frame", "height", "width")
VMEM = pl.BlockSpec(memory_space=pltpu.VMEM)
SMEM = pl.BlockSpec(memory_space=pltpu.SMEM)
PARAMS = pltpu.CompilerParams(vmem_limit_bytes=24 * 1024 * 1024)
STAT_ROWS = 8


def window_of(position, extent):
    span = min(3, extent)
    start = max(0, min(position - 1, extent - 3))
    return range(start, start + span)


def routes_of(extent):
    first = [(p ^ 1, p) for p in range(extent) if (p ^ 1) in window_of(p, extent)]
    if extent > 4:
        first = [(p + 1, p) for p in range(extent - 1)]
    wanted = [(s, p) for p in range(extent) for s in window_of(p, extent) if s != p]
    wanted.sort(key=lambda pair: (pair[0] ^ pair[1], pair))
    routes = [first]
    for pair in wanted:
        if pair in first:
            continue
        for route in routes[1:]:
            if all(pair[0] != s and pair[1] != p for s, p in route):
                route.append(pair)
                break
        else:
            routes.append([pair])
    return [route for route in routes if route]


def slots_of(extent):
    routes = routes_of(extent)
    arrivals = [[c for c, r in enumerate(routes) if any(q == p for _, q in r)] for p in range(extent)]
    return [[arrivals[p][k] for p in range(extent)] for k in range(min(3, extent) - 1)]


def chosen(options, choice, axis):
    value = options[choice[0]]
    position = lax.axis_index(axis)
    for option in sorted(set(choice)):
        if option != choice[0]:
            here = functools.reduce(
                jnp.logical_or, [position == p for p, c in enumerate(choice) if c == option]
            )
            value = jnp.where(here, options[option], value)
    return value


def fetch(block, axis):
    extent = lax.axis_size(axis)
    routes = routes_of(extent)
    arrived = [lax.ppermute(block, axis, route) for route in routes]
    tiles = []
    for slot in slots_of(extent):
        used = sorted(set(slot))
        reached = sum(len(routes[c]) for c in used)
        if reached == extent:
            tiles.append(functools.reduce(jnp.add, [arrived[c] for c in used]))
        else:
            tiles.append(chosen(arrived, slot, axis))
    return tiles


def returned(pieces, axis):
    extent = lax.axis_size(axis)
    slots = slots_of(extent)
    arrived = []
    for c, route in reversed(list(enumerate(routes_of(extent)))):
        holders = [next((k for k in range(len(slots)) if slots[k][p] == c), None) for p in range(extent)]
        used = sorted({k for k in holders if k is not None})
        choice = [k if k is not None else used[0] for k in holders]
        outgoing = chosen({k: pieces[k] for k in used}, choice, axis).astype(jnp.bfloat16)
        arrived.append(lax.ppermute(outgoing, axis, [(p, s) for s, p in route]))
    return arrived


def give_back(pieces, axis):
    arrived = returned(pieces[1:], axis)
    return functools.reduce(jnp.add, [pieces[0]] + [a.astype(jnp.float32) for a in arrived])


def flip(block, axes, bits):
    sizes = [lax.axis_size(axis) for axis in axes]
    route = []
    for flat in range(math.prod(sizes)):
        rest, target, scale = flat, 0, 1
        for size, bit in zip(reversed(sizes), reversed(bits)):
            target += ((rest % size) ^ bit) * scale
            rest //= size
            scale *= size
        route.append((flat, target))
    return lax.ppermute(block, axes, route)


def rows_of(refs, part):
    block = refs[0][:, part]
    for ref in refs[1:]:
        block = block + ref[:, part]
    return block.reshape(-1, block.shape[-1])


def token_kernel(
    place, queries, queries_other, grads, weight, payload, grads_half, grad_rows, both_queries
):
    half = grads_half.shape[1]
    product = lax.dot_general(
        grads[...], weight[...], (((1,), (1,)), ((), ())), preferred_element_type=jnp.float32
    ).astype(jnp.bfloat16)
    grad_rows[...] = product
    payload[:, half:] = product
    payload[:, :half] = grads[:, pl.ds(pl.multiple_of((1 - place[0]) * half, half), half)]
    grads_half[...] = grads[:, pl.ds(pl.multiple_of(place[0] * half, half), half)]
    both_tiles(place, queries[...], queries_other[...], both_queries)


def both_tiles(place, mine, theirs, both):
    tile = mine.shape[0]
    both[pl.ds(pl.multiple_of(place[0] * tile, tile), tile), :] = mine
    both[pl.ds(pl.multiple_of((1 - place[0]) * tile, tile), tile), :] = theirs


def forward_kernel(inv_root, layout, carried, both_queries, *refs):
    groups, rest = split_groups(layout, refs)
    partial, scores = rest[-2:]
    dim = both_queries.shape[1]
    query_rows = both_queries[...]
    top, start, spans = None, 0, []
    if carried:
        top = rest[0][dim : dim + 1, :]
    for group in groups:
        keys = rows_of(group, 0)
        piece = lax.dot_general(
            keys, query_rows, (((1,), (1,)), ((), ())), preferred_element_type=jnp.float32
        )
        scores[start : start + keys.shape[0], :] = piece
        spans.append((start, keys.shape[0]))
        start += keys.shape[0]
        piece_top = jnp.max(piece, axis=0, keepdims=True) * inv_root
        top = piece_top if top is None else jnp.maximum(top, piece_top)
    if carried:
        share = jnp.exp(rest[0][dim : dim + 1, :] - top)
        total = rest[0][dim + 1 : dim + 2, :] * share
        mixed = rest[0][:dim, :] * share
    else:
        total = jnp.zeros_like(top)
        mixed = jnp.zeros((dim, query_rows.shape[0]), jnp.float32)
    for group, (start, count) in zip(groups, spans):
        weights = jnp.exp(scores[start : start + count, :] * inv_root - top)
        total = total + jnp.sum(weights, axis=0, keepdims=True)
        mixed = mixed + lax.dot_general(
            rows_of(group, 1),
            weights.astype(jnp.bfloat16),
            (((0,), (0,)), ((), ())),
            preferred_element_type=jnp.float32,
        )
    partial[:dim, :] = mixed
    row = lax.broadcasted_iota(jnp.int32, (STAT_ROWS, query_rows.shape[0]), 0)
    partial[dim:, :] = jnp.where(row == 0, top, total)


def merge_kernel(scale, plane, place, mine, theirs, payload, grads_half, grad_rows, *refs):
    stats, attended_own, terms, both_grads, both_attended, term_rows = (
        refs[0],
        refs[1],
        refs[2:-3],
        refs[-3],
        refs[-2],
        refs[-1],
    )
    tile, dim = grad_rows.shape
    half = grads_half.shape[1]
    top_a, top_b = mine[dim : dim + 1, :], theirs[dim : dim + 1, :]
    sum_a, sum_b = mine[dim + 1 : dim + 2, :], theirs[dim + 1 : dim + 2, :]
    top = jnp.maximum(top_a, top_b)
    share_a, share_b = jnp.exp(top_a - top), jnp.exp(top_b - top)
    total = share_a * sum_a + share_b * sum_b
    mixed = mine[:dim, :] * (share_a / total) + theirs[:dim, :] * (share_b / total)
    attended_t = mixed.astype(jnp.bfloat16).astype(jnp.float32)
    both_tiles(place, grad_rows[...], payload[:, half:], both_grads)
    row_dot = jnp.sum(both_grads[...].astype(jnp.float32).T * attended_t, axis=0, keepdims=True)
    row = lax.broadcasted_iota(jnp.int32, (STAT_ROWS, mixed.shape[1]), 0)
    stats[...] = jnp.where(row == 0, top + jnp.log(total), row_dot)
    both_attended[...] = attended_t.T.astype(jnp.bfloat16)
    rows_mine = both_attended[pl.ds(pl.multiple_of(place[0] * tile, tile), tile), :]
    rows_theirs = both_attended[pl.ds(pl.multiple_of((1 - place[0]) * tile, tile), tile), :]
    attended_own[...] = rows_mine
    if not terms:
        return
    contract = (((0,), (0,)), ((), ()))
    term = lax.dot_general(
        rows_mine, grads_half[...], contract, preferred_element_type=jnp.float32
    )
    term = term + lax.dot_general(
        rows_theirs, payload[:, :half], contract, preferred_element_type=jnp.float32
    )
    term_rows[...] = term * scale
    count = dim // plane
    for order, out in enumerate(terms):
        chunk = place[1] ^ order
        out[...] = term_rows[pl.ds(pl.multiple_of(chunk * count, count), count), :].astype(jnp.bfloat16)


def split_groups(layout, refs):
    groups, start = [], 0
    for count in layout:
        groups.append(refs[start : start + count])
        start += count
    return groups, refs[start:]


def backward_kernel(
    inv_root, layout, targets, place, stats, both_queries, payload, grad_rows, *refs
):
    groups, rest = split_groups(layout, refs)
    count = 1 + max(out for out, _ in targets)
    outs, (query_own, query_other, both_grads, both_out) = rest[:count], rest[count:]
    tile, dim = grad_rows.shape
    columns = payload.shape[1]
    both_tiles(place, grad_rows[...], payload[:, columns - dim :], both_grads)
    query_rows, out_grads = both_queries[...], both_grads[...]
    level, row_dot = stats[0:1, :], stats[1:2, :]
    along = (((1,), (1,)), ((), ()))
    query_grad = jnp.zeros((dim, 2 * tile), jnp.float32)
    for group, (target, first) in zip(groups, targets):
        out, tiles = outs[target], group[0].shape[0]
        keys, values = rows_of(group, 0), rows_of(group, 1)
        scores = lax.dot_general(keys, query_rows, along, preferred_element_type=jnp.float32)
        probability = jnp.exp(scores * inv_root - level)
        prob_grad = lax.dot_general(values, out_grads, along, preferred_element_type=jnp.float32)
        score_grad = (probability * (prob_grad - row_dot)).astype(jnp.bfloat16)
        shape = (tiles,) + out.shape[2:]
        key_grad = jnp.dot(score_grad, query_rows, preferred_element_type=jnp.float32) * inv_root
        value_grad = jnp.dot(
            probability.astype(jnp.bfloat16), out_grads, preferred_element_type=jnp.float32
        )
        out[first : first + tiles, 0] = key_grad.reshape(shape).astype(out.dtype)
        out[first : first + tiles, 1] = value_grad.reshape(shape).astype(out.dtype)
        query_grad = query_grad + lax.dot_general(
            keys, score_grad, (((0,), (0,)), ((), ())), preferred_element_type=jnp.float32
        )
    both_out[...] = query_grad.T * inv_root
    query_own[...] = both_out[pl.ds(pl.multiple_of(place[0] * tile, tile), tile), :]
    other = both_out[pl.ds(pl.multiple_of((1 - place[0]) * tile, tile), tile), :]
    other = other.astype(jnp.bfloat16)
    rows = query_other.shape[0]
    for block in range(tile // rows):
        query_other[:, block * dim : (block + 1) * dim] = other[block * rows : (block + 1) * rows]


def assemble_kernel(flipped, rows, place, part, *refs):
    rows_ref, done = refs[-2:]
    count, width = rows_ref.shape
    copies = []
    if flipped:
        query_own, _, whole, grad_query, sums = refs[:-2]
        dim, step = query_own.shape[1], part.shape[0] - count
        for block in range(width // dim):
            piece = part[count:, block * dim : (block + 1) * dim].astype(jnp.float32)
            span = slice(block * step, (block + 1) * step)
            sums[span, :] = (query_own[span, :] + piece).astype(jnp.bfloat16)
        copies.append(pltpu.make_async_copy(sums, grad_query, done.at[count // rows]))
        copies[-1].start()
    else:
        whole = refs[0]
    core = 1 - place[0] if flipped else place[0]
    columns = pl.ds(pl.multiple_of(core * width, width), width)
    for order in range(count // rows):
        span = pl.ds(pl.multiple_of((place[1] ^ order) * rows, rows), rows)
        rows_ref[span, :] = part[order * rows : (order + 1) * rows, :].astype(jnp.float32)
        copies.append(
            pltpu.make_async_copy(rows_ref.at[span, :], whole.at[span, columns], done.at[order])
        )
        copies[-1].start()
    for copy in copies:
        copy.wait()


def assemble(flipped, place, part, rows, shape, whole=None, query_own=None):
    anywhere = pl.BlockSpec(memory_space=pl.ANY)
    outs, out_specs, operands, in_specs = shape, anywhere, (place, part), [SMEM, VMEM]
    scratch = [
        pltpu.VMEM((shape.shape[0], part.shape[1]), jnp.float32),
        pltpu.SemaphoreType.DMA((shape.shape[0] // rows + flipped,)),
    ]
    if flipped:
        outs, out_specs = (shape, shaped(*query_own.shape)), (anywhere, anywhere)
        operands, in_specs = operands + (query_own, whole), in_specs + [VMEM, anywhere]
        scratch = [pltpu.VMEM(query_own.shape, jnp.bfloat16)] + scratch
    return pl.pallas_call(
        functools.partial(assemble_kernel, flipped, rows),
        out_shape=outs,
        in_specs=in_specs,
        out_specs=out_specs,
        scratch_shapes=scratch,
        input_output_aliases={3: 0} if flipped else {},
        compiler_params=PARAMS,
    )(*operands)


def owner_kernel(own_grad, *refs):
    for k, out in enumerate(refs[-2:]):
        total = own_grad[k]
        for block in refs[:-2]:
            total = total + block[k].astype(jnp.float32)
        out[...] = total.astype(jnp.bfloat16)


def pack_kernel(*refs):
    start = 0
    for piece in refs[:-1]:
        refs[-1][start : start + piece.shape[0], :] = piece[...]
        start += piece.shape[0]


def combine_kernel(column, *refs):
    arrived, pieces = refs[: -column.shape[0]], refs[-column.shape[0] :]
    for k, piece in enumerate(pieces):
        total = column[k]
        for block in arrived:
            total = total + block[k].astype(jnp.float32)
        piece[...] = total.astype(piece.dtype)


def shaped(*shape, kind=jnp.bfloat16):
    return jax.ShapeDtypeStruct(shape, kind)


def kernel_call(kernel, operands, outs, scratch=(), cost=None):
    many = isinstance(outs, (list, tuple))
    return pl.pallas_call(
        kernel,
        out_shape=outs,
        in_specs=[SMEM] + [VMEM] * (len(operands) - 1),
        out_specs=[VMEM] * len(outs) if many else VMEM,
        scratch_shapes=list(scratch),
        compiler_params=PARAMS,
        cost_estimate=cost,
    )(*operands)


def cost_of(flops, moved):
    return pl.CostEstimate(flops=int(flops), bytes_accessed=int(moved), transcendentals=0)


PLANE_BITS = ((0, 0), (0, 1), (2, 0), (2, 1))


def sum_over_plane(terms):
    summed = terms[0].astype(jnp.float32)
    for term, bit in zip(terms[1:], PLANE_BITS[1:]):
        summed = summed + flip(term, ("frame", "width"), bit).astype(jnp.float32)
    return summed.astype(jnp.bfloat16)


def join_sum(part, query_own, query_other, place):
    plane = len(part)
    pieces = part + [query_other]
    part = pl.pallas_call(
        pack_kernel,
        out_shape=shaped(sum(p.shape[0] for p in pieces), pieces[0].shape[1]),
        in_specs=[VMEM] * len(pieces),
        out_specs=VMEM,
        compiler_params=PARAMS,
    )(*pieces)
    other = flip(part, ("frame",), (1,))
    rows = (part.shape[0] - query_other.shape[0]) // plane
    shape = shaped(plane * rows, 2 * part.shape[1], kind=jnp.float32)
    whole = assemble(False, place, part, rows, shape)
    return whole, lambda whole: assemble(True, place, other, rows, shape, whole, query_own)


def body(queries, key_vectors, value_vectors, out_weight, projected_grad):
    head_dim = queries.shape[-1]
    model_dim = out_weight.shape[1]
    half = model_dim // 2
    inv_root = 1.0 / math.sqrt(head_dim)
    extents = tuple(lax.axis_size(axis) for axis in AXES)
    assert extents[0] == 4
    small = extents[1:] == (4, 2)
    frame, height, width = (lax.axis_index(axis) for axis in AXES)
    core = frame % 2
    place = jnp.stack([core, (frame // 2) * 2 + width, height]).astype(jnp.int32)
    query_rows = queries.reshape(-1, head_dim)
    grads = projected_grad.reshape(-1, model_dim)
    tile = query_rows.shape[0]

    own = jnp.stack((key_vectors.reshape(tile, head_dim), value_vectors.reshape(tile, head_dim)))
    cross = [(2 * s + y, 2 * p + 1 - y) for s, p in ((2, 1), (1, 2)) for y in (0, 1)]

    if small:
        swap = [(0, 1), (1, 0)]
        tiles = fetch(own, "height")
        own_beside = lax.ppermute(own[None], "width", swap)
        others = jnp.stack(tiles)
        column = jnp.stack([own] + tiles)
        others, column, own_beside, query_rows_late = lax.optimization_barrier(
            (others, column, own_beside, query_rows)
        )
        others_beside = lax.ppermute(others, "width", swap)
        far = [
            lax.ppermute(column, "frame", [(2, 0), (1, 3)]),
            lax.ppermute(column, ("frame", "width"), cross),
        ]
        blocks = [column, own_beside, others_beside, *far]
        layout = (1, 1, 1, 2)
        targets = ((0, 0), (1, 0), (1, 1), (2, 0))
        column_tiles, kinds = 1 + others.shape[0], 3
    else:
        query_rows_late = query_rows
        column = jnp.stack([own] + fetch(own, "height"))
        beside = fetch(column, "width")
        everything = jnp.concatenate([column] + beside, axis=0)
        far = [
            lax.ppermute(everything[:, :, : tile // 2], "frame", [(2, 0), (1, 3)]),
            lax.ppermute(everything[:, :, tile // 2 :], "frame", [(2, 1), (1, 2)]),
        ]
        blocks = [column] + beside + far
        layout = (1,) * (1 + len(beside)) + (2,)
        targets = tuple((k, 0) for k in range(len(layout)))
        column_tiles, kinds = column.shape[0], len(layout)
    queries_other = flip(query_rows_late, ("frame",), (1,))
    payload, grads_half, grad_rows, both_queries = kernel_call(
        token_kernel,
        (place, query_rows, queries_other, grads, out_weight),
        (
            shaped(tile, half + head_dim),
            shaped(tile, half),
            shaped(tile, head_dim),
            shaped(2 * tile, head_dim),
        ),
        cost=cost_of(2 * tile * head_dim * model_dim, 4 * tile * model_dim),
    )
    grad_shapes = [(column_tiles, 2, tile, head_dim)] * (kinds - 1)
    grad_shapes.append((column_tiles, 2, tile, head_dim) if small else far[0].shape)
    key_count = sum(shape[0] * shape[2] for shape in grad_shapes)
    product = 2 * key_count * 2 * tile * head_dim
    moved = sum(b.size * 2 for b in blocks)

    def forward(operands, groups, carried):
        keys, start = 0, 0
        for count in groups:
            keys += operands[start].shape[0] * operands[start].shape[2]
            start += count
        return pl.pallas_call(
            functools.partial(forward_kernel, inv_root, groups, bool(carried)),
            out_shape=shaped(head_dim + STAT_ROWS, 2 * tile, kind=jnp.float32),
            in_specs=[VMEM] * (1 + len(operands) + len(carried)),
            out_specs=VMEM,
            scratch_shapes=[pltpu.VMEM((keys, 2 * tile), jnp.float32)],
            compiler_params=PARAMS,
            cost_estimate=cost_of(8 * keys * tile * head_dim, moved * keys // key_count),
        )(both_queries, *operands, *carried)

    partial = forward(blocks[:1], (1,), ())
    payload, partial, *blocks[1:] = lax.optimization_barrier((payload, partial, *blocks[1:]))
    payload = flip(payload, ("frame",), (1,))
    partial = forward(blocks[1:], layout[1:], (partial,))
    partial_other = flip(partial, ("frame",), (1,))
    plane = 4
    chunks = plane if small else 0
    merged = kernel_call(
        functools.partial(merge_kernel, 1.0 / float(math.prod(extents)), plane),
        (place, partial, partial_other, payload, grads_half, grad_rows),
        (
            shaped(STAT_ROWS, 2 * tile, kind=jnp.float32),
            shaped(tile, head_dim),
            *[shaped(head_dim // plane, half)] * chunks,
        ),
        scratch=(
            pltpu.VMEM((2 * tile, head_dim), jnp.bfloat16),
            pltpu.VMEM((2 * tile, head_dim), jnp.bfloat16),
            pltpu.VMEM((head_dim, half), jnp.float32),
        ),
        cost=cost_of(4 * tile * head_dim * half, 4 * tile * model_dim),
    )
    stats, attended, *terms = merged
    back = kernel_call(
        functools.partial(backward_kernel, inv_root, layout, targets),
        (place, stats, both_queries, payload, grad_rows, *blocks),
        (
            shaped(*grad_shapes[0], kind=jnp.float32),
            *[shaped(*shape) for shape in grad_shapes[1:]],
            shaped(tile, head_dim, kind=jnp.float32),
            shaped(tile * head_dim // half, half),
        ),
        scratch=(
            pltpu.VMEM((2 * tile, head_dim), jnp.bfloat16),
            pltpu.VMEM((2 * tile, head_dim), jnp.float32),
        ),
        cost=cost_of(5 * product, 2 * moved),
    )
    if small:
        terms[0], *back = lax.optimization_barrier((terms[0], *back))
        part = sum_over_plane(terms)
        other = flip(part, ("height",), (1,))
        part = (part.astype(jnp.float32) + other.astype(jnp.float32)).astype(jnp.bfloat16)
        part, attended = lax.optimization_barrier((part, attended))
        other = flip(part, ("height",), (2,))
    else:
        weight_term = jnp.einsum("td,tm->dm", attended, grads, preferred_element_type=jnp.float32)
        grad_out_weight = lax.psum(weight_term, AXES) / float(math.prod(extents))
    projected = (
        jnp.dot(attended, out_weight, preferred_element_type=jnp.float32)
        .astype(jnp.bfloat16)
        .reshape(projected_grad.shape)
    )
    column_grad, *beside_grads, far_grad, query_own, query_other = back
    if small:
        arrived = [
            lax.ppermute(beside_grads[0], "width", [(0, 1), (1, 0)]),
            lax.ppermute(far_grad, "frame", [(0, 2), (3, 1)]),
            lax.ppermute(far_grad, ("frame", "width"), [(p, s) for s, p in cross]),
        ]
        other, projected = lax.optimization_barrier((other, projected))
        part = (part.astype(jnp.float32) + other.astype(jnp.float32)).astype(jnp.bfloat16)
        part, column_grad = lax.optimization_barrier((part, column_grad))
        part = [part] + [flip(part, ("frame", "width"), bit) for bit in PLANE_BITS[1:]]
        shape = column_grad.shape[1:]
        pieces = pl.pallas_call(
            combine_kernel,
            out_shape=[shaped(*shape, kind=jnp.float32)] + [shaped(*shape)] * (column_tiles - 1),
            in_specs=[VMEM] * 4,
            out_specs=[VMEM] * column_tiles,
            compiler_params=PARAMS,
        )(column_grad, *arrived)
        pieces = list(pieces)
    else:
        arrived = jnp.concatenate(
            (
                lax.ppermute(far_grad, "frame", [(0, 2), (3, 1)]),
                lax.ppermute(far_grad, "frame", [(1, 2), (2, 1)]),
            ),
            axis=2,
        ).astype(jnp.float32)
        pieces = [column_grad] + [b.astype(jnp.float32) for b in beside_grads]
        span = column_tiles
        pieces = [p + arrived[i * span : (i + 1) * span] for i, p in enumerate(pieces)]
        column_grad = give_back(pieces, "width")
        pieces = [column_grad[k] for k in range(column_tiles)]
    if small:
        whole, finish = join_sum(part, query_own, query_other, place)
        whole, pieces[0] = lax.optimization_barrier((whole, pieces[0]))
        grad_out_weight, grad_query = finish(whole)
    else:
        query_other = flip(query_other, ("frame",), (1,)).reshape(-1, half // head_dim, head_dim)
        query_other = query_other.transpose(1, 0, 2).reshape(tile, head_dim)
        grad_query = (query_own + query_other.astype(jnp.float32)).astype(jnp.bfloat16)
    operands = (pieces[0], *returned(pieces[1:], "height"))
    grad_key, grad_value = pl.pallas_call(
        owner_kernel,
        out_shape=[shaped(tile, head_dim)] * 2,
        in_specs=[VMEM] * len(operands),
        out_specs=[VMEM] * 2,
        compiler_params=PARAMS,
        cost_estimate=cost_of(10**10, 10**8),
    )(*operands)
    grad_key = grad_key.reshape(key_vectors.shape)
    grad_value = grad_value.reshape(value_vectors.shape)
    grad_query = grad_query.reshape(queries.shape)
    return (projected, grad_query, grad_key, grad_value, grad_out_weight)


def solution(mesh):
    tokens = P("frame", "height", "width", None)
    return jax.shard_map(
        body,
        mesh=mesh,
        in_specs=(tokens, tokens, tokens, P(), tokens),
        out_specs=(tokens, tokens, tokens, tokens, P()),
        check_vma=False,
    )
```

```python
import functools
import math

import jax
import jax.numpy as jnp
from jax import lax
from jax.experimental import pallas as pl
from jax.experimental.pallas import tpu as pltpu
from jax.sharding import PartitionSpec as P

AXES = ("frame", "height", "width")
VMEM = pl.BlockSpec(memory_space=pltpu.VMEM)
SMEM = pl.BlockSpec(memory_space=pltpu.SMEM)
PARAMS = pltpu.CompilerParams(vmem_limit_bytes=24 * 1024 * 1024)
STAT_ROWS = 8
FREE = pl.CostEstimate(flops=0, bytes_accessed=0, transcendentals=0)


def window_of(position, extent):
    span = min(3, extent)
    start = max(0, min(position - 1, extent - 3))
    return range(start, start + span)


def routes_of(extent):
    first = [(p ^ 1, p) for p in range(extent) if (p ^ 1) in window_of(p, extent)]
    if extent > 4:
        first = [(p + 1, p) for p in range(extent - 1)]
    wanted = [(s, p) for p in range(extent) for s in window_of(p, extent) if s != p]
    wanted.sort(key=lambda pair: (pair[0] ^ pair[1], pair))
    routes = [first]
    for pair in wanted:
        if pair in first:
            continue
        for route in routes[1:]:
            if all(pair[0] != s and pair[1] != p for s, p in route):
                route.append(pair)
                break
        else:
            routes.append([pair])
    return [route for route in routes if route]


def slots_of(extent):
    routes = routes_of(extent)
    arrivals = [[c for c, r in enumerate(routes) if any(q == p for _, q in r)] for p in range(extent)]
    return [[arrivals[p][k] for p in range(extent)] for k in range(min(3, extent) - 1)]


def chosen(options, choice, axis):
    value = options[choice[0]]
    position = lax.axis_index(axis)
    for option in sorted(set(choice)):
        if option != choice[0]:
            here = functools.reduce(
                jnp.logical_or, [position == p for p, c in enumerate(choice) if c == option]
            )
            value = jnp.where(here, options[option], value)
    return value


def fetch(block, axis):
    extent = lax.axis_size(axis)
    routes = routes_of(extent)
    arrived = [lax.ppermute(block, axis, route) for route in routes]
    tiles = []
    for slot in slots_of(extent):
        used = sorted(set(slot))
        reached = sum(len(routes[c]) for c in used)
        if reached == extent:
            tiles.append(functools.reduce(jnp.add, [arrived[c] for c in used]))
        else:
            tiles.append(chosen(arrived, slot, axis))
    return tiles


def returned(pieces, axis):
    extent = lax.axis_size(axis)
    slots = slots_of(extent)
    arrived = []
    order = (0, 2, 1) if extent == 4 else range(len(routes_of(extent)))
    for c, route in ((c, routes_of(extent)[c]) for c in order):
        holders = [next((k for k in range(len(slots)) if slots[k][p] == c), None) for p in range(extent)]
        used = sorted({k for k in holders if k is not None})
        choice = [k if k is not None else used[0] for k in holders]
        outgoing = chosen({k: pieces[k] for k in used}, choice, axis).astype(jnp.bfloat16)
        arrived.append(lax.ppermute(outgoing, axis, [(p, s) for s, p in route]))
    return arrived


def give_back(pieces, axis):
    arrived = returned(pieces[1:], axis)
    return functools.reduce(jnp.add, [pieces[0]] + [a.astype(jnp.float32) for a in arrived])


def flip(block, axes, bits):
    sizes = [lax.axis_size(axis) for axis in axes]
    route = []
    for flat in range(math.prod(sizes)):
        rest, target, scale = flat, 0, 1
        for size, bit in zip(reversed(sizes), reversed(bits)):
            target += ((rest % size) ^ bit) * scale
            rest //= size
            scale *= size
        route.append((flat, target))
    return lax.ppermute(block, axes, route)


def rows_of(refs, part):
    block = refs[0][:, part]
    for ref in refs[1:]:
        block = block + ref[:, part]
    return block.reshape(-1, block.shape[-1])


def token_kernel(
    place, queries, queries_other, grads, weight, payload, grads_half, grad_rows, both_queries
):
    half = grads_half.shape[1]
    product = lax.dot_general(
        grads[...], weight[...], (((1,), (1,)), ((), ())), preferred_element_type=jnp.float32
    ).astype(jnp.bfloat16)
    grad_rows[...] = product
    payload[:, half:] = product
    payload[:, :half] = grads[:, pl.ds(pl.multiple_of((1 - place[0]) * half, half), half)]
    grads_half[...] = grads[:, pl.ds(pl.multiple_of(place[0] * half, half), half)]
    both_tiles(place, queries[...], queries_other[...], both_queries)


def both_tiles(place, mine, theirs, both):
    tile = mine.shape[0]
    both[pl.ds(pl.multiple_of(place[0] * tile, tile), tile), :] = mine
    both[pl.ds(pl.multiple_of((1 - place[0]) * tile, tile), tile), :] = theirs


def forward_kernel(inv_root, layout, carried, both_queries, *refs):
    groups, rest = split_groups(layout, refs)
    partial, scores = rest[-2:]
    dim = both_queries.shape[1]
    query_rows = both_queries[...]
    top, start, spans = None, 0, []
    if carried:
        top = rest[0][dim : dim + 1, :]
    for group in groups:
        keys = rows_of(group, 0)
        piece = lax.dot_general(
            keys, query_rows, (((1,), (1,)), ((), ())), preferred_element_type=jnp.float32
        )
        scores[start : start + keys.shape[0], :] = piece
        spans.append((start, keys.shape[0]))
        start += keys.shape[0]
        piece_top = jnp.max(piece, axis=0, keepdims=True) * inv_root
        top = piece_top if top is None else jnp.maximum(top, piece_top)
    if carried:
        share = jnp.exp(rest[0][dim : dim + 1, :] - top)
        total = rest[0][dim + 1 : dim + 2, :] * share
        mixed = rest[0][:dim, :] * share
    else:
        total = jnp.zeros_like(top)
        mixed = jnp.zeros((dim, query_rows.shape[0]), jnp.float32)
    for group, (start, count) in zip(groups, spans):
        weights = jnp.exp(scores[start : start + count, :] * inv_root - top)
        total = total + jnp.sum(weights, axis=0, keepdims=True)
        mixed = mixed + lax.dot_general(
            rows_of(group, 1),
            weights.astype(jnp.bfloat16),
            (((0,), (0,)), ((), ())),
            preferred_element_type=jnp.float32,
        )
    partial[:dim, :] = mixed
    row = lax.broadcasted_iota(jnp.int32, (STAT_ROWS, query_rows.shape[0]), 0)
    partial[dim:, :] = jnp.where(row == 0, top, total)


def merge_kernel(scale, plane, place, mine, theirs, payload, grads_half, grad_rows, *refs):
    stats, attended_own, terms, both_grads, both_attended, term_rows = (
        refs[0],
        refs[1],
        refs[2:-3],
        refs[-3],
        refs[-2],
        refs[-1],
    )
    tile, dim = grad_rows.shape
    half = grads_half.shape[1]
    top_a, top_b = mine[dim : dim + 1, :], theirs[dim : dim + 1, :]
    sum_a, sum_b = mine[dim + 1 : dim + 2, :], theirs[dim + 1 : dim + 2, :]
    top = jnp.maximum(top_a, top_b)
    share_a, share_b = jnp.exp(top_a - top), jnp.exp(top_b - top)
    total = share_a * sum_a + share_b * sum_b
    mixed = mine[:dim, :] * (share_a / total) + theirs[:dim, :] * (share_b / total)
    attended_t = mixed.astype(jnp.bfloat16).astype(jnp.float32)
    both_tiles(place, grad_rows[...], payload[:, half:], both_grads)
    row_dot = jnp.sum(both_grads[...].astype(jnp.float32).T * attended_t, axis=0, keepdims=True)
    row = lax.broadcasted_iota(jnp.int32, (STAT_ROWS, mixed.shape[1]), 0)
    stats[...] = jnp.where(row == 0, top + jnp.log(total), row_dot)
    both_attended[...] = attended_t.T.astype(jnp.bfloat16)
    rows_mine = both_attended[pl.ds(pl.multiple_of(place[0] * tile, tile), tile), :]
    rows_theirs = both_attended[pl.ds(pl.multiple_of((1 - place[0]) * tile, tile), tile), :]
    attended_own[...] = rows_mine
    if not terms:
        return
    contract = (((0,), (0,)), ((), ()))
    term = lax.dot_general(
        rows_mine, grads_half[...], contract, preferred_element_type=jnp.float32
    )
    term = term + lax.dot_general(
        rows_theirs, payload[:, :half], contract, preferred_element_type=jnp.float32
    )
    term_rows[...] = term * scale
    count = dim // plane
    for order, out in enumerate(terms):
        chunk = place[1] ^ order
        out[...] = term_rows[pl.ds(pl.multiple_of(chunk * count, count), count), :].astype(jnp.bfloat16)


def split_groups(layout, refs):
    groups, start = [], 0
    for count in layout:
        groups.append(refs[start : start + count])
        start += count
    return groups, refs[start:]


def backward_kernel(
    inv_root, layout, targets, place, stats, both_queries, payload, grad_rows, *refs
):
    groups, rest = split_groups(layout, refs)
    count = 1 + max(out for out, _ in targets)
    outs, (query_own, query_other, both_grads, both_out) = rest[:count], rest[count:]
    tile, dim = grad_rows.shape
    columns = payload.shape[1]
    both_tiles(place, grad_rows[...], payload[:, columns - dim :], both_grads)
    query_rows, out_grads = both_queries[...], both_grads[...]
    level, row_dot = stats[0:1, :], stats[1:2, :]
    along = (((1,), (1,)), ((), ()))
    query_grad = jnp.zeros((dim, 2 * tile), jnp.float32)
    for group, (target, first) in zip(groups, targets):
        out, tiles = outs[target], group[0].shape[0]
        keys, values = rows_of(group, 0), rows_of(group, 1)
        scores = lax.dot_general(keys, query_rows, along, preferred_element_type=jnp.float32)
        probability = jnp.exp(scores * inv_root - level)
        prob_grad = lax.dot_general(values, out_grads, along, preferred_element_type=jnp.float32)
        score_grad = (probability * (prob_grad - row_dot)).astype(jnp.bfloat16)
        shape = (tiles,) + out.shape[2:]
        key_grad = jnp.dot(score_grad, query_rows, preferred_element_type=jnp.float32) * inv_root
        value_grad = jnp.dot(
            probability.astype(jnp.bfloat16), out_grads, preferred_element_type=jnp.float32
        )
        out[first : first + tiles, 0] = key_grad.reshape(shape).astype(out.dtype)
        out[first : first + tiles, 1] = value_grad.reshape(shape).astype(out.dtype)
        query_grad = query_grad + lax.dot_general(
            keys, score_grad, (((0,), (0,)), ((), ())), preferred_element_type=jnp.float32
        )
    both_out[...] = query_grad.T * inv_root
    query_own[...] = both_out[pl.ds(pl.multiple_of(place[0] * tile, tile), tile), :]
    other = both_out[pl.ds(pl.multiple_of((1 - place[0]) * tile, tile), tile), :]
    other = other.astype(jnp.bfloat16)
    rows = query_other.shape[0]
    for block in range(tile // rows):
        query_other[:, block * dim : (block + 1) * dim] = other[block * rows : (block + 1) * rows]


def assemble_kernel(flipped, rows, place, part, *refs):
    rows_ref, done = refs[-2:]
    count, width = rows_ref.shape
    copies = []
    if flipped:
        query_own, _, whole, grad_query, sums = refs[:-2]
        dim, step = query_own.shape[1], part.shape[0] - count
        for block in range(width // dim):
            piece = part[count:, block * dim : (block + 1) * dim].astype(jnp.float32)
            span = slice(block * step, (block + 1) * step)
            sums[span, :] = (query_own[span, :] + piece).astype(jnp.bfloat16)
        copies.append(pltpu.make_async_copy(sums, grad_query, done.at[count // rows]))
        copies[-1].start()
    else:
        whole = refs[0]
    core = 1 - place[0] if flipped else place[0]
    columns = pl.ds(pl.multiple_of(core * width, width), width)
    for order in range(count // rows):
        span = pl.ds(pl.multiple_of((place[1] ^ order) * rows, rows), rows)
        rows_ref[span, :] = part[order * rows : (order + 1) * rows, :].astype(jnp.float32)
        copies.append(
            pltpu.make_async_copy(rows_ref.at[span, :], whole.at[span, columns], done.at[order])
        )
        copies[-1].start()
    for copy in copies:
        copy.wait()


def assemble(flipped, place, part, rows, shape, whole=None, query_own=None):
    anywhere = pl.BlockSpec(memory_space=pl.ANY)
    outs, out_specs, operands, in_specs = shape, anywhere, (place, part), [SMEM, VMEM]
    scratch = [
        pltpu.VMEM((shape.shape[0], part.shape[1]), jnp.float32),
        pltpu.SemaphoreType.DMA((shape.shape[0] // rows + flipped,)),
    ]
    if flipped:
        outs, out_specs = (shape, shaped(*query_own.shape)), (anywhere, anywhere)
        operands, in_specs = operands + (query_own, whole), in_specs + [VMEM, anywhere]
        scratch = [pltpu.VMEM(query_own.shape, jnp.bfloat16)] + scratch
    return pl.pallas_call(
        functools.partial(assemble_kernel, flipped, rows),
        out_shape=outs,
        in_specs=in_specs,
        out_specs=out_specs,
        scratch_shapes=scratch,
        input_output_aliases={3: 0} if flipped else {},
        compiler_params=PARAMS,
        cost_estimate=cost_of(10**10, 10**8),
    )(*operands)


def owner_kernel(own_grad, *refs):
    for k, out in enumerate(refs[-2:]):
        total = own_grad[k]
        for block in refs[:-2]:
            total = total + block[k].astype(jnp.float32)
        out[...] = total.astype(jnp.bfloat16)


def pack_kernel(*refs):
    start = 0
    for piece in refs[:-1]:
        refs[-1][start : start + piece.shape[0], :] = piece[...]
        start += piece.shape[0]


def combine_kernel(column, *refs):
    arrived, pieces = refs[: -column.shape[0]], refs[-column.shape[0] :]
    for k, piece in enumerate(pieces):
        total = column[k]
        for block in arrived:
            total = total + block[k].astype(jnp.float32)
        piece[...] = total.astype(piece.dtype)


def shaped(*shape, kind=jnp.bfloat16):
    return jax.ShapeDtypeStruct(shape, kind)


def kernel_call(kernel, operands, outs, scratch=(), cost=None):
    many = isinstance(outs, (list, tuple))
    return pl.pallas_call(
        kernel,
        out_shape=outs,
        in_specs=[SMEM] + [VMEM] * (len(operands) - 1),
        out_specs=[VMEM] * len(outs) if many else VMEM,
        scratch_shapes=list(scratch),
        compiler_params=PARAMS,
        cost_estimate=cost,
    )(*operands)


def cost_of(flops, moved):
    return pl.CostEstimate(flops=int(flops), bytes_accessed=int(moved), transcendentals=0)


PLANE_BITS = ((0, 0), (0, 1), (2, 0), (2, 1))


def sum_over_plane(terms):
    summed = terms[0].astype(jnp.float32)
    for term, bit in zip(terms[1:], PLANE_BITS[1:]):
        summed = summed + flip(term, ("frame", "width"), bit).astype(jnp.float32)
    return summed.astype(jnp.bfloat16)


def join_sum(part, query_own, query_other, place):
    plane = len(part)
    pieces = part + [query_other]
    part = pl.pallas_call(
        pack_kernel,
        out_shape=shaped(sum(p.shape[0] for p in pieces), pieces[0].shape[1]),
        in_specs=[VMEM] * len(pieces),
        out_specs=VMEM,
        compiler_params=PARAMS,
    )(*pieces)
    other = flip(part, ("frame",), (1,))
    rows = (part.shape[0] - query_other.shape[0]) // plane
    shape = shaped(plane * rows, 2 * part.shape[1], kind=jnp.float32)
    whole = assemble(False, place, part, rows, shape)
    return whole, lambda whole: assemble(True, place, other, rows, shape, whole, query_own)


def body(queries, key_vectors, value_vectors, out_weight, projected_grad):
    head_dim = queries.shape[-1]
    model_dim = out_weight.shape[1]
    half = model_dim // 2
    inv_root = 1.0 / math.sqrt(head_dim)
    extents = tuple(lax.axis_size(axis) for axis in AXES)
    assert extents[0] == 4
    small = extents[1:] == (4, 2)
    frame, height, width = (lax.axis_index(axis) for axis in AXES)
    core = frame % 2
    place = jnp.stack([core, (frame // 2) * 2 + width, height]).astype(jnp.int32)
    query_rows = queries.reshape(-1, head_dim)
    grads = projected_grad.reshape(-1, model_dim)
    tile = query_rows.shape[0]

    own = jnp.stack((key_vectors.reshape(tile, head_dim), value_vectors.reshape(tile, head_dim)))
    cross = [(2 * s + y, 2 * p + 1 - y) for s, p in ((2, 1), (1, 2)) for y in (0, 1)]

    if small:
        swap = [(0, 1), (1, 0)]
        tiles = fetch(own, "height")
        own_beside = lax.ppermute(own[None], "width", swap)
        others = jnp.stack(tiles)
        column = jnp.stack([own] + tiles)
        others, column, own_beside, query_rows_late = lax.optimization_barrier(
            (others, column, own_beside, query_rows)
        )
        others_beside = lax.ppermute(others, "width", swap)
        far = [
            lax.ppermute(column, "frame", [(2, 0), (1, 3)]),
            lax.ppermute(column, ("frame", "width"), cross),
        ]
        blocks = [column, own_beside, others_beside, *far]
        layout = (1, 1, 1, 2)
        targets = ((0, 0), (1, 0), (1, 1), (2, 0))
        column_tiles, kinds = 1 + others.shape[0], 3
    else:
        query_rows_late = query_rows
        column = jnp.stack([own] + fetch(own, "height"))
        beside = fetch(column, "width")
        everything = jnp.concatenate([column] + beside, axis=0)
        far = [
            lax.ppermute(everything[:, :, : tile // 2], "frame", [(2, 0), (1, 3)]),
            lax.ppermute(everything[:, :, tile // 2 :], "frame", [(2, 1), (1, 2)]),
        ]
        blocks = [column] + beside + far
        layout = (1,) * (1 + len(beside)) + (2,)
        targets = tuple((k, 0) for k in range(len(layout)))
        column_tiles, kinds = column.shape[0], len(layout)
    queries_other = flip(query_rows_late, ("frame",), (1,))
    payload, grads_half, grad_rows, both_queries = kernel_call(
        token_kernel,
        (place, query_rows, queries_other, grads, out_weight),
        (
            shaped(tile, half + head_dim),
            shaped(tile, half),
            shaped(tile, head_dim),
            shaped(2 * tile, head_dim),
        ),
        cost=cost_of(2 * tile * head_dim * model_dim, 4 * tile * model_dim),
    )
    grad_shapes = [(column_tiles, 2, tile, head_dim)] * (kinds - 1)
    grad_shapes.append((column_tiles, 2, tile, head_dim) if small else far[0].shape)
    key_count = sum(shape[0] * shape[2] for shape in grad_shapes)
    product = 2 * key_count * 2 * tile * head_dim
    moved = sum(b.size * 2 for b in blocks)

    def forward(operands, groups, carried):
        keys, start = 0, 0
        for count in groups:
            keys += operands[start].shape[0] * operands[start].shape[2]
            start += count
        return pl.pallas_call(
            functools.partial(forward_kernel, inv_root, groups, bool(carried)),
            out_shape=shaped(head_dim + STAT_ROWS, 2 * tile, kind=jnp.float32),
            in_specs=[VMEM] * (1 + len(operands) + len(carried)),
            out_specs=VMEM,
            scratch_shapes=[pltpu.VMEM((keys, 2 * tile), jnp.float32)],
            compiler_params=PARAMS,
            cost_estimate=cost_of(8 * keys * tile * head_dim, moved * keys // key_count),
        )(both_queries, *operands, *carried)

    partial = forward(blocks[:1], (1,), ())
    payload, partial, *blocks[1:] = lax.optimization_barrier((payload, partial, *blocks[1:]))
    payload = flip(payload, ("frame",), (1,))
    partial = forward(blocks[1:], layout[1:], (partial,))
    partial_other = flip(partial, ("frame",), (1,))
    plane = 4
    chunks = plane if small else 0
    merged = kernel_call(
        functools.partial(merge_kernel, 1.0 / float(math.prod(extents)), plane),
        (place, partial, partial_other, payload, grads_half, grad_rows),
        (
            shaped(STAT_ROWS, 2 * tile, kind=jnp.float32),
            shaped(tile, head_dim),
            *[shaped(head_dim // plane, half)] * chunks,
        ),
        scratch=(
            pltpu.VMEM((2 * tile, head_dim), jnp.bfloat16),
            pltpu.VMEM((2 * tile, head_dim), jnp.bfloat16),
            pltpu.VMEM((head_dim, half), jnp.float32),
        ),
        cost=cost_of(4 * tile * head_dim * half, 4 * tile * model_dim),
    )
    stats, attended, *terms = merged
    back = kernel_call(
        functools.partial(backward_kernel, inv_root, layout, targets),
        (place, stats, both_queries, payload, grad_rows, *blocks),
        (
            shaped(*grad_shapes[0], kind=jnp.float32),
            *[shaped(*shape) for shape in grad_shapes[1:]],
            shaped(tile, head_dim, kind=jnp.float32),
            shaped(tile * head_dim // half, half),
        ),
        scratch=(
            pltpu.VMEM((2 * tile, head_dim), jnp.bfloat16),
            pltpu.VMEM((2 * tile, head_dim), jnp.float32),
        ),
        cost=cost_of(5 * product, 2 * moved),
    )
    if small:
        terms[0], *back = lax.optimization_barrier((terms[0], *back))
        part = sum_over_plane(terms)
        other = flip(part, ("height",), (1,))
        part = (part.astype(jnp.float32) + other.astype(jnp.float32)).astype(jnp.bfloat16)
        part, attended = lax.optimization_barrier((part, attended))
        other = flip(part, ("height",), (2,))
    else:
        weight_term = jnp.einsum("td,tm->dm", attended, grads, preferred_element_type=jnp.float32)
        grad_out_weight = lax.psum(weight_term, AXES) / float(math.prod(extents))
    projected = (
        jnp.dot(attended, out_weight, preferred_element_type=jnp.float32)
        .astype(jnp.bfloat16)
        .reshape(projected_grad.shape)
    )
    column_grad, *beside_grads, far_grad, query_own, query_other = back
    if small:
        arrived = [
            lax.ppermute(beside_grads[0], "width", [(0, 1), (1, 0)]),
            lax.ppermute(far_grad, "frame", [(0, 2), (3, 1)]),
            lax.ppermute(far_grad, ("frame", "width"), [(p, s) for s, p in cross]),
        ]
        other, projected = lax.optimization_barrier((other, projected))
        part = (part.astype(jnp.float32) + other.astype(jnp.float32)).astype(jnp.bfloat16)
        part, column_grad = lax.optimization_barrier((part, column_grad))
        part = [part] + [flip(part, ("frame", "width"), bit) for bit in PLANE_BITS[1:]]
        shape = column_grad.shape[1:]
        pieces = pl.pallas_call(
            combine_kernel,
            out_shape=[shaped(*shape, kind=jnp.float32)] + [shaped(*shape)] * (column_tiles - 1),
            in_specs=[VMEM] * 4,
            out_specs=[VMEM] * column_tiles,
            compiler_params=PARAMS,
        )(column_grad, *arrived)
        pieces = list(pieces)
    else:
        arrived = jnp.concatenate(
            (
                lax.ppermute(far_grad, "frame", [(0, 2), (3, 1)]),
                lax.ppermute(far_grad, "frame", [(1, 2), (2, 1)]),
            ),
            axis=2,
        ).astype(jnp.float32)
        pieces = [column_grad] + [b.astype(jnp.float32) for b in beside_grads]
        span = column_tiles
        pieces = [p + arrived[i * span : (i + 1) * span] for i, p in enumerate(pieces)]
        column_grad = give_back(pieces, "width")
        pieces = [column_grad[k] for k in range(column_tiles)]
    if small:
        whole, finish = join_sum(part, query_own, query_other, place)
        grad_out_weight, grad_query = finish(whole)
        grad_out_weight, pieces[0] = lax.optimization_barrier((grad_out_weight, pieces[0]))
    else:
        query_other = flip(query_other, ("frame",), (1,)).reshape(-1, half // head_dim, head_dim)
        query_other = query_other.transpose(1, 0, 2).reshape(tile, head_dim)
        grad_query = (query_own + query_other.astype(jnp.float32)).astype(jnp.bfloat16)
    operands = (pieces[0], *returned(pieces[1:], "height"))
    grad_key, grad_value = pl.pallas_call(
        owner_kernel,
        out_shape=[shaped(tile, head_dim)] * 2,
        in_specs=[VMEM] * len(operands),
        out_specs=[VMEM] * 2,
        compiler_params=PARAMS,
        cost_estimate=cost_of(10**10, 10**8),
    )(*operands)
    grad_key = grad_key.reshape(key_vectors.shape)
    grad_value = grad_value.reshape(value_vectors.shape)
    grad_query = grad_query.reshape(queries.shape)
    return (projected, grad_query, grad_key, grad_value, grad_out_weight)


def solution(mesh):
    tokens = P("frame", "height", "width", None)
    return jax.shard_map(
        body,
        mesh=mesh,
        in_specs=(tokens, tokens, tokens, P(), tokens),
        out_specs=(tokens, tokens, tokens, tokens, P()),
        check_vma=False,
    )
```

```python
import functools
import math

import jax
import jax.numpy as jnp
from jax import lax
from jax.experimental import pallas as pl
from jax.experimental.pallas import tpu as pltpu
from jax.sharding import PartitionSpec as P

AXES = ("frame", "height", "width")
VMEM = pl.BlockSpec(memory_space=pltpu.VMEM)
SMEM = pl.BlockSpec(memory_space=pltpu.SMEM)
PARAMS = pltpu.CompilerParams(vmem_limit_bytes=24 * 1024 * 1024)
STAT_ROWS = 8
FREE = pl.CostEstimate(flops=0, bytes_accessed=0, transcendentals=0)


def window_of(position, extent):
    span = min(3, extent)
    start = max(0, min(position - 1, extent - 3))
    return range(start, start + span)


def routes_of(extent):
    first = [(p ^ 1, p) for p in range(extent) if (p ^ 1) in window_of(p, extent)]
    if extent > 4:
        first = [(p + 1, p) for p in range(extent - 1)]
    wanted = [(s, p) for p in range(extent) for s in window_of(p, extent) if s != p]
    wanted.sort(key=lambda pair: (pair[0] ^ pair[1], pair))
    routes = [first]
    for pair in wanted:
        if pair in first:
            continue
        for route in routes[1:]:
            if all(pair[0] != s and pair[1] != p for s, p in route):
                route.append(pair)
                break
        else:
            routes.append([pair])
    return [route for route in routes if route]


def slots_of(extent):
    routes = routes_of(extent)
    arrivals = [[c for c, r in enumerate(routes) if any(q == p for _, q in r)] for p in range(extent)]
    return [[arrivals[p][k] for p in range(extent)] for k in range(min(3, extent) - 1)]


def chosen(options, choice, axis):
    value = options[choice[0]]
    position = lax.axis_index(axis)
    for option in sorted(set(choice)):
        if option != choice[0]:
            here = functools.reduce(
                jnp.logical_or, [position == p for p, c in enumerate(choice) if c == option]
            )
            value = jnp.where(here, options[option], value)
    return value


def fetch(block, axis):
    extent = lax.axis_size(axis)
    routes = routes_of(extent)
    arrived = [lax.ppermute(block, axis, route) for route in routes]
    tiles = []
    for slot in slots_of(extent):
        used = sorted(set(slot))
        reached = sum(len(routes[c]) for c in used)
        if reached == extent:
            tiles.append(functools.reduce(jnp.add, [arrived[c] for c in used]))
        else:
            tiles.append(chosen(arrived, slot, axis))
    return tiles


def returned(pieces, axis):
    extent = lax.axis_size(axis)
    slots = slots_of(extent)
    arrived = []
    order = (0, 2, 1) if extent == 4 else range(len(routes_of(extent)))
    for c, route in ((c, routes_of(extent)[c]) for c in order):
        holders = [next((k for k in range(len(slots)) if slots[k][p] == c), None) for p in range(extent)]
        used = sorted({k for k in holders if k is not None})
        choice = [k if k is not None else used[0] for k in holders]
        outgoing = chosen({k: pieces[k] for k in used}, choice, axis).astype(jnp.bfloat16)
        arrived.append(lax.ppermute(outgoing, axis, [(p, s) for s, p in route]))
    return arrived


def give_back(pieces, axis):
    arrived = returned(pieces[1:], axis)
    return functools.reduce(jnp.add, [pieces[0]] + [a.astype(jnp.float32) for a in arrived])


def flip(block, axes, bits):
    sizes = [lax.axis_size(axis) for axis in axes]
    route = []
    for flat in range(math.prod(sizes)):
        rest, target, scale = flat, 0, 1
        for size, bit in zip(reversed(sizes), reversed(bits)):
            target += ((rest % size) ^ bit) * scale
            rest //= size
            scale *= size
        route.append((flat, target))
    return lax.ppermute(block, axes, route)


def rows_of(refs, part):
    block = refs[0][:, part]
    for ref in refs[1:]:
        block = block + ref[:, part]
    return block.reshape(-1, block.shape[-1])


def token_kernel(
    place, queries, queries_other, grads, weight, payload, grads_half, grad_rows, both_queries
):
    half = grads_half.shape[1]
    product = lax.dot_general(
        grads[...], weight[...], (((1,), (1,)), ((), ())), preferred_element_type=jnp.float32
    ).astype(jnp.bfloat16)
    grad_rows[...] = product
    payload[:, half:] = product
    payload[:, :half] = grads[:, pl.ds(pl.multiple_of((1 - place[0]) * half, half), half)]
    grads_half[...] = grads[:, pl.ds(pl.multiple_of(place[0] * half, half), half)]
    both_tiles(place, queries[...], queries_other[...], both_queries)


def both_tiles(place, mine, theirs, both):
    tile = mine.shape[0]
    both[pl.ds(pl.multiple_of(place[0] * tile, tile), tile), :] = mine
    both[pl.ds(pl.multiple_of((1 - place[0]) * tile, tile), tile), :] = theirs


def forward_kernel(inv_root, layout, carried, both_queries, *refs):
    groups, rest = split_groups(layout, refs)
    partial, scores = rest[-2:]
    dim = both_queries.shape[1]
    query_rows = both_queries[...]
    top, start, spans = None, 0, []
    if carried:
        top = rest[0][dim : dim + 1, :]
    for group in groups:
        keys = rows_of(group, 0)
        piece = lax.dot_general(
            keys, query_rows, (((1,), (1,)), ((), ())), preferred_element_type=jnp.float32
        )
        scores[start : start + keys.shape[0], :] = piece
        spans.append((start, keys.shape[0]))
        start += keys.shape[0]
        piece_top = jnp.max(piece, axis=0, keepdims=True) * inv_root
        top = piece_top if top is None else jnp.maximum(top, piece_top)
    if carried:
        share = jnp.exp(rest[0][dim : dim + 1, :] - top)
        total = rest[0][dim + 1 : dim + 2, :] * share
        mixed = rest[0][:dim, :] * share
    else:
        total = jnp.zeros_like(top)
        mixed = jnp.zeros((dim, query_rows.shape[0]), jnp.float32)
    for group, (start, count) in zip(groups, spans):
        weights = jnp.exp(scores[start : start + count, :] * inv_root - top)
        total = total + jnp.sum(weights, axis=0, keepdims=True)
        mixed = mixed + lax.dot_general(
            rows_of(group, 1),
            weights.astype(jnp.bfloat16),
            (((0,), (0,)), ((), ())),
            preferred_element_type=jnp.float32,
        )
    partial[:dim, :] = mixed
    row = lax.broadcasted_iota(jnp.int32, (STAT_ROWS, query_rows.shape[0]), 0)
    partial[dim:, :] = jnp.where(row == 0, top, total)


def merge_kernel(scale, plane, place, mine, theirs, payload, grads_half, grad_rows, *refs):
    stats, attended_own, terms, both_grads, both_attended, term_rows = (
        refs[0],
        refs[1],
        refs[2:-3],
        refs[-3],
        refs[-2],
        refs[-1],
    )
    tile, dim = grad_rows.shape
    half = grads_half.shape[1]
    top_a, top_b = mine[dim : dim + 1, :], theirs[dim : dim + 1, :]
    sum_a, sum_b = mine[dim + 1 : dim + 2, :], theirs[dim + 1 : dim + 2, :]
    top = jnp.maximum(top_a, top_b)
    share_a, share_b = jnp.exp(top_a - top), jnp.exp(top_b - top)
    total = share_a * sum_a + share_b * sum_b
    mixed = mine[:dim, :] * (share_a / total) + theirs[:dim, :] * (share_b / total)
    attended_t = mixed.astype(jnp.bfloat16).astype(jnp.float32)
    both_tiles(place, grad_rows[...], payload[:, half:], both_grads)
    row_dot = jnp.sum(both_grads[...].astype(jnp.float32).T * attended_t, axis=0, keepdims=True)
    row = lax.broadcasted_iota(jnp.int32, (STAT_ROWS, mixed.shape[1]), 0)
    stats[...] = jnp.where(row == 0, top + jnp.log(total), row_dot)
    both_attended[...] = attended_t.T.astype(jnp.bfloat16)
    rows_mine = both_attended[pl.ds(pl.multiple_of(place[0] * tile, tile), tile), :]
    rows_theirs = both_attended[pl.ds(pl.multiple_of((1 - place[0]) * tile, tile), tile), :]
    attended_own[...] = rows_mine
    if not terms:
        return
    contract = (((0,), (0,)), ((), ()))
    term = lax.dot_general(
        rows_mine, grads_half[...], contract, preferred_element_type=jnp.float32
    )
    term = term + lax.dot_general(
        rows_theirs, payload[:, :half], contract, preferred_element_type=jnp.float32
    )
    term_rows[...] = term * scale
    count = dim // plane
    for order, out in enumerate(terms):
        chunk = place[1] ^ order
        out[...] = term_rows[pl.ds(pl.multiple_of(chunk * count, count), count), :].astype(jnp.bfloat16)


def split_groups(layout, refs):
    groups, start = [], 0
    for count in layout:
        groups.append(refs[start : start + count])
        start += count
    return groups, refs[start:]


def backward_kernel(
    inv_root, layout, targets, place, stats, both_queries, payload, grad_rows, *refs
):
    groups, rest = split_groups(layout, refs)
    count = 1 + max(out for out, _ in targets)
    outs, (query_own, query_other, both_grads, both_out) = rest[:count], rest[count:]
    tile, dim = grad_rows.shape
    columns = payload.shape[1]
    both_tiles(place, grad_rows[...], payload[:, columns - dim :], both_grads)
    query_rows, out_grads = both_queries[...], both_grads[...]
    level, row_dot = stats[0:1, :], stats[1:2, :]
    along = (((1,), (1,)), ((), ()))
    query_grad = jnp.zeros((dim, 2 * tile), jnp.float32)
    for group, (target, first) in zip(groups, targets):
        out, tiles = outs[target], group[0].shape[0]
        keys, values = rows_of(group, 0), rows_of(group, 1)
        scores = lax.dot_general(keys, query_rows, along, preferred_element_type=jnp.float32)
        probability = jnp.exp(scores * inv_root - level)
        prob_grad = lax.dot_general(values, out_grads, along, preferred_element_type=jnp.float32)
        score_grad = (probability * (prob_grad - row_dot)).astype(jnp.bfloat16)
        shape = (tiles,) + out.shape[2:]
        key_grad = jnp.dot(score_grad, query_rows, preferred_element_type=jnp.float32) * inv_root
        value_grad = jnp.dot(
            probability.astype(jnp.bfloat16), out_grads, preferred_element_type=jnp.float32
        )
        out[first : first + tiles, 0] = key_grad.reshape(shape).astype(out.dtype)
        out[first : first + tiles, 1] = value_grad.reshape(shape).astype(out.dtype)
        query_grad = query_grad + lax.dot_general(
            keys, score_grad, (((0,), (0,)), ((), ())), preferred_element_type=jnp.float32
        )
    both_out[...] = query_grad.T * inv_root
    query_own[...] = both_out[pl.ds(pl.multiple_of(place[0] * tile, tile), tile), :]
    other = both_out[pl.ds(pl.multiple_of((1 - place[0]) * tile, tile), tile), :]
    other = other.astype(jnp.bfloat16)
    rows = query_other.shape[0]
    for block in range(tile // rows):
        query_other[:, block * dim : (block + 1) * dim] = other[block * rows : (block + 1) * rows]


def assemble_kernel(flipped, rows, place, part, *refs):
    rows_ref, done = refs[-2:]
    count, width = rows_ref.shape
    copies = []
    if flipped:
        query_own, _, whole, grad_query, sums = refs[:-2]
        dim, step = query_own.shape[1], part.shape[0] - count
        for block in range(width // dim):
            piece = part[count:, block * dim : (block + 1) * dim].astype(jnp.float32)
            span = slice(block * step, (block + 1) * step)
            sums[span, :] = (query_own[span, :] + piece).astype(jnp.bfloat16)
        copies.append(pltpu.make_async_copy(sums, grad_query, done.at[count // rows]))
        copies[-1].start()
    else:
        whole = refs[0]
    core = 1 - place[0] if flipped else place[0]
    columns = pl.ds(pl.multiple_of(core * width, width), width)
    for order in range(count // rows):
        span = pl.ds(pl.multiple_of((place[1] ^ order) * rows, rows), rows)
        rows_ref[span, :] = part[order * rows : (order + 1) * rows, :].astype(jnp.float32)
        copies.append(
            pltpu.make_async_copy(rows_ref.at[span, :], whole.at[span, columns], done.at[order])
        )
        copies[-1].start()
    for copy in copies:
        copy.wait()


def assemble(flipped, place, part, rows, shape, whole=None, query_own=None):
    anywhere = pl.BlockSpec(memory_space=pl.ANY)
    outs, out_specs, operands, in_specs = shape, anywhere, (place, part), [SMEM, VMEM]
    scratch = [
        pltpu.VMEM((shape.shape[0], part.shape[1]), jnp.float32),
        pltpu.SemaphoreType.DMA((shape.shape[0] // rows + flipped,)),
    ]
    if flipped:
        outs, out_specs = (shape, shaped(*query_own.shape)), (anywhere, anywhere)
        operands, in_specs = operands + (query_own, whole), in_specs + [VMEM, anywhere]
        scratch = [pltpu.VMEM(query_own.shape, jnp.bfloat16)] + scratch
    return pl.pallas_call(
        functools.partial(assemble_kernel, flipped, rows),
        out_shape=outs,
        in_specs=in_specs,
        out_specs=out_specs,
        scratch_shapes=scratch,
        input_output_aliases={3: 0} if flipped else {},
        compiler_params=PARAMS,
        cost_estimate=cost_of(10**10, 10**8),
    )(*operands)


def owner_kernel(own_grad, *refs):
    for k, out in enumerate(refs[-2:]):
        total = own_grad[k]
        for block in refs[:-2]:
            total = total + block[k].astype(jnp.float32)
        out[...] = total.astype(jnp.bfloat16)


def pack_kernel(*refs):
    start = 0
    for piece in refs[:-1]:
        refs[-1][start : start + piece.shape[0], :] = piece[...]
        start += piece.shape[0]


def combine_kernel(column, *refs):
    arrived, pieces = refs[: -column.shape[0]], refs[-column.shape[0] :]
    for k, piece in enumerate(pieces):
        total = column[k]
        for block in arrived:
            total = total + block[k].astype(jnp.float32)
        piece[...] = total.astype(piece.dtype)


def shaped(*shape, kind=jnp.bfloat16):
    return jax.ShapeDtypeStruct(shape, kind)


def kernel_call(kernel, operands, outs, scratch=(), cost=None):
    many = isinstance(outs, (list, tuple))
    return pl.pallas_call(
        kernel,
        out_shape=outs,
        in_specs=[SMEM] + [VMEM] * (len(operands) - 1),
        out_specs=[VMEM] * len(outs) if many else VMEM,
        scratch_shapes=list(scratch),
        compiler_params=PARAMS,
        cost_estimate=cost,
    )(*operands)


def cost_of(flops, moved):
    return pl.CostEstimate(flops=int(flops), bytes_accessed=int(moved), transcendentals=0)


PLANE_BITS = ((0, 0), (0, 1), (2, 0), (2, 1))


def sum_over_plane(terms):
    summed = terms[0].astype(jnp.float32)
    for term, bit in zip(terms[1:], PLANE_BITS[1:]):
        summed = summed + flip(term, ("frame", "width"), bit).astype(jnp.float32)
    return summed.astype(jnp.bfloat16)


def join_sum(part, query_own, query_other, place):
    plane = len(part)
    pieces = part + [query_other]
    part = pl.pallas_call(
        pack_kernel,
        out_shape=shaped(sum(p.shape[0] for p in pieces), pieces[0].shape[1]),
        in_specs=[VMEM] * len(pieces),
        out_specs=VMEM,
        compiler_params=PARAMS,
    )(*pieces)
    other = flip(part, ("frame",), (1,))
    rows = (part.shape[0] - query_other.shape[0]) // plane
    shape = shaped(plane * rows, 2 * part.shape[1], kind=jnp.float32)
    whole = assemble(False, place, part, rows, shape)
    return whole, lambda whole: assemble(True, place, other, rows, shape, whole, query_own)


def body(queries, key_vectors, value_vectors, out_weight, projected_grad):
    head_dim = queries.shape[-1]
    model_dim = out_weight.shape[1]
    half = model_dim // 2
    inv_root = 1.0 / math.sqrt(head_dim)
    extents = tuple(lax.axis_size(axis) for axis in AXES)
    assert extents[0] == 4
    small = extents[1:] == (4, 2)
    frame, height, width = (lax.axis_index(axis) for axis in AXES)
    core = frame % 2
    place = jnp.stack([core, (frame // 2) * 2 + width, height]).astype(jnp.int32)
    query_rows = queries.reshape(-1, head_dim)
    grads = projected_grad.reshape(-1, model_dim)
    tile = query_rows.shape[0]

    own = jnp.stack((key_vectors.reshape(tile, head_dim), value_vectors.reshape(tile, head_dim)))
    cross = [(2 * s + y, 2 * p + 1 - y) for s, p in ((2, 0), (1, 3)) for y in (0, 1)]

    if small:
        swap = [(0, 1), (1, 0)]
        tiles = fetch(own, "height")
        own_beside = lax.ppermute(own[None], "width", swap)
        others = jnp.stack(tiles)
        column = jnp.stack([own] + tiles)
        others, column, own_beside, query_rows_late = lax.optimization_barrier(
            (others, column, own_beside, query_rows)
        )
        others_beside = lax.ppermute(others, "width", swap)
        far = [
            lax.ppermute(column, "frame", [(2, 1), (1, 2)]),
            lax.ppermute(column, ("frame", "width"), cross),
        ]
        blocks = [column, own_beside, others_beside, *far]
        layout = (1, 1, 1, 2)
        targets = ((0, 0), (1, 0), (1, 1), (2, 0))
        column_tiles, kinds = 1 + others.shape[0], 3
    else:
        query_rows_late = query_rows
        column = jnp.stack([own] + fetch(own, "height"))
        beside = fetch(column, "width")
        everything = jnp.concatenate([column] + beside, axis=0)
        far = [
            lax.ppermute(everything[:, :, : tile // 2], "frame", [(2, 0), (1, 3)]),
            lax.ppermute(everything[:, :, tile // 2 :], "frame", [(2, 1), (1, 2)]),
        ]
        blocks = [column] + beside + far
        layout = (1,) * (1 + len(beside)) + (2,)
        targets = tuple((k, 0) for k in range(len(layout)))
        column_tiles, kinds = column.shape[0], len(layout)
    queries_other = flip(query_rows_late, ("frame",), (1,))
    payload, grads_half, grad_rows, both_queries = kernel_call(
        token_kernel,
        (place, query_rows, queries_other, grads, out_weight),
        (
            shaped(tile, half + head_dim),
            shaped(tile, half),
            shaped(tile, head_dim),
            shaped(2 * tile, head_dim),
        ),
        cost=cost_of(2 * tile * head_dim * model_dim, 4 * tile * model_dim),
    )
    grad_shapes = [(column_tiles, 2, tile, head_dim)] * (kinds - 1)
    grad_shapes.append((column_tiles, 2, tile, head_dim) if small else far[0].shape)
    key_count = sum(shape[0] * shape[2] for shape in grad_shapes)
    product = 2 * key_count * 2 * tile * head_dim
    moved = sum(b.size * 2 for b in blocks)

    def forward(operands, groups, carried):
        keys, start = 0, 0
        for count in groups:
            keys += operands[start].shape[0] * operands[start].shape[2]
            start += count
        return pl.pallas_call(
            functools.partial(forward_kernel, inv_root, groups, bool(carried)),
            out_shape=shaped(head_dim + STAT_ROWS, 2 * tile, kind=jnp.float32),
            in_specs=[VMEM] * (1 + len(operands) + len(carried)),
            out_specs=VMEM,
            scratch_shapes=[pltpu.VMEM((keys, 2 * tile), jnp.float32)],
            compiler_params=PARAMS,
            cost_estimate=cost_of(8 * keys * tile * head_dim, moved * keys // key_count),
        )(both_queries, *operands, *carried)

    partial = forward(blocks[:1], (1,), ())
    payload, partial, *blocks[1:] = lax.optimization_barrier((payload, partial, *blocks[1:]))
    payload = flip(payload, ("frame",), (1,))
    partial = forward(blocks[1:], layout[1:], (partial,))
    partial_other = flip(partial, ("frame",), (1,))
    plane = 4
    chunks = plane if small else 0
    merged = kernel_call(
        functools.partial(merge_kernel, 1.0 / float(math.prod(extents)), plane),
        (place, partial, partial_other, payload, grads_half, grad_rows),
        (
            shaped(STAT_ROWS, 2 * tile, kind=jnp.float32),
            shaped(tile, head_dim),
            *[shaped(head_dim // plane, half)] * chunks,
        ),
        scratch=(
            pltpu.VMEM((2 * tile, head_dim), jnp.bfloat16),
            pltpu.VMEM((2 * tile, head_dim), jnp.bfloat16),
            pltpu.VMEM((head_dim, half), jnp.float32),
        ),
        cost=cost_of(4 * tile * head_dim * half, 4 * tile * model_dim),
    )
    stats, attended, *terms = merged
    back = kernel_call(
        functools.partial(backward_kernel, inv_root, layout, targets),
        (place, stats, both_queries, payload, grad_rows, *blocks),
        (
            shaped(*grad_shapes[0], kind=jnp.float32),
            *[shaped(*shape) for shape in grad_shapes[1:]],
            shaped(tile, head_dim, kind=jnp.float32),
            shaped(tile * head_dim // half, half),
        ),
        scratch=(
            pltpu.VMEM((2 * tile, head_dim), jnp.bfloat16),
            pltpu.VMEM((2 * tile, head_dim), jnp.float32),
        ),
        cost=cost_of(5 * product, 2 * moved),
    )
    if small:
        terms[0], *back = lax.optimization_barrier((terms[0], *back))
        part = sum_over_plane(terms)
        other = flip(part, ("height",), (1,))
        part = (part.astype(jnp.float32) + other.astype(jnp.float32)).astype(jnp.bfloat16)
        part, attended = lax.optimization_barrier((part, attended))
        other = flip(part, ("height",), (2,))
    else:
        weight_term = jnp.einsum("td,tm->dm", attended, grads, preferred_element_type=jnp.float32)
        grad_out_weight = lax.psum(weight_term, AXES) / float(math.prod(extents))
    projected = (
        jnp.dot(attended, out_weight, preferred_element_type=jnp.float32)
        .astype(jnp.bfloat16)
        .reshape(projected_grad.shape)
    )
    column_grad, *beside_grads, far_grad, query_own, query_other = back
    if small:
        arrived = [
            lax.ppermute(beside_grads[0], "width", [(0, 1), (1, 0)]),
            lax.ppermute(far_grad, "frame", [(1, 2), (2, 1)]),
            lax.ppermute(far_grad, ("frame", "width"), [(p, s) for s, p in cross]),
        ]
        other, projected = lax.optimization_barrier((other, projected))
        part = (part.astype(jnp.float32) + other.astype(jnp.float32)).astype(jnp.bfloat16)
        part, column_grad = lax.optimization_barrier((part, column_grad))
        part = [part] + [flip(part, ("frame", "width"), bit) for bit in PLANE_BITS[1:]]
        shape = column_grad.shape[1:]
        pieces = pl.pallas_call(
            combine_kernel,
            out_shape=[shaped(*shape, kind=jnp.float32)] + [shaped(*shape)] * (column_tiles - 1),
            in_specs=[VMEM] * 4,
            out_specs=[VMEM] * column_tiles,
            compiler_params=PARAMS,
        )(column_grad, *arrived)
        pieces = list(pieces)
    else:
        arrived = jnp.concatenate(
            (
                lax.ppermute(far_grad, "frame", [(0, 2), (3, 1)]),
                lax.ppermute(far_grad, "frame", [(1, 2), (2, 1)]),
            ),
            axis=2,
        ).astype(jnp.float32)
        pieces = [column_grad] + [b.astype(jnp.float32) for b in beside_grads]
        span = column_tiles
        pieces = [p + arrived[i * span : (i + 1) * span] for i, p in enumerate(pieces)]
        column_grad = give_back(pieces, "width")
        pieces = [column_grad[k] for k in range(column_tiles)]
    if small:
        whole, finish = join_sum(part, query_own, query_other, place)
        grad_out_weight, grad_query = finish(whole)
        grad_out_weight, pieces[0] = lax.optimization_barrier((grad_out_weight, pieces[0]))
    else:
        query_other = flip(query_other, ("frame",), (1,)).reshape(-1, half // head_dim, head_dim)
        query_other = query_other.transpose(1, 0, 2).reshape(tile, head_dim)
        grad_query = (query_own + query_other.astype(jnp.float32)).astype(jnp.bfloat16)
    operands = (pieces[0], *returned(pieces[1:], "height"))
    grad_key, grad_value = pl.pallas_call(
        owner_kernel,
        out_shape=[shaped(tile, head_dim)] * 2,
        in_specs=[VMEM] * len(operands),
        out_specs=[VMEM] * 2,
        compiler_params=PARAMS,
        cost_estimate=cost_of(10**10, 10**8),
    )(*operands)
    grad_key = grad_key.reshape(key_vectors.shape)
    grad_value = grad_value.reshape(value_vectors.shape)
    grad_query = grad_query.reshape(queries.shape)
    return (projected, grad_query, grad_key, grad_value, grad_out_weight)


def solution(mesh):
    tokens = P("frame", "height", "width", None)
    return jax.shard_map(
        body,
        mesh=mesh,
        in_specs=(tokens, tokens, tokens, P(), tokens),
        out_specs=(tokens, tokens, tokens, tokens, P()),
        check_vma=False,
    )
```

```python
import functools
import math

import jax
import jax.numpy as jnp
from jax import lax
from jax.experimental import pallas as pl
from jax.experimental.pallas import tpu as pltpu
from jax.sharding import PartitionSpec as P

AXES = ("frame", "height", "width")
VMEM = pl.BlockSpec(memory_space=pltpu.VMEM)
SMEM = pl.BlockSpec(memory_space=pltpu.SMEM)
PARAMS = pltpu.CompilerParams(vmem_limit_bytes=24 * 1024 * 1024)
STAT_ROWS = 8
FREE = pl.CostEstimate(flops=0, bytes_accessed=0, transcendentals=0)


def window_of(position, extent):
    span = min(3, extent)
    start = max(0, min(position - 1, extent - 3))
    return range(start, start + span)


def routes_of(extent):
    first = [(p ^ 1, p) for p in range(extent) if (p ^ 1) in window_of(p, extent)]
    if extent > 4:
        first = [(p + 1, p) for p in range(extent - 1)]
    wanted = [(s, p) for p in range(extent) for s in window_of(p, extent) if s != p]
    wanted.sort(key=lambda pair: (pair[0] ^ pair[1], pair))
    routes = [first]
    for pair in wanted:
        if pair in first:
            continue
        for route in routes[1:]:
            if all(pair[0] != s and pair[1] != p for s, p in route):
                route.append(pair)
                break
        else:
            routes.append([pair])
    return [route for route in routes if route]


def slots_of(extent):
    routes = routes_of(extent)
    arrivals = [[c for c, r in enumerate(routes) if any(q == p for _, q in r)] for p in range(extent)]
    return [[arrivals[p][k] for p in range(extent)] for k in range(min(3, extent) - 1)]


def chosen(options, choice, axis):
    value = options[choice[0]]
    position = lax.axis_index(axis)
    for option in sorted(set(choice)):
        if option != choice[0]:
            here = functools.reduce(
                jnp.logical_or, [position == p for p, c in enumerate(choice) if c == option]
            )
            value = jnp.where(here, options[option], value)
    return value


def fetch(block, axis):
    extent = lax.axis_size(axis)
    routes = routes_of(extent)
    arrived = [lax.ppermute(block, axis, route) for route in routes]
    tiles = []
    for slot in slots_of(extent):
        used = sorted(set(slot))
        reached = sum(len(routes[c]) for c in used)
        if reached == extent:
            tiles.append(functools.reduce(jnp.add, [arrived[c] for c in used]))
        else:
            tiles.append(chosen(arrived, slot, axis))
    return tiles


def returned(pieces, axis):
    extent = lax.axis_size(axis)
    slots = slots_of(extent)
    arrived = []
    order = (0, 2, 1) if extent == 4 else range(len(routes_of(extent)))
    for c, route in ((c, routes_of(extent)[c]) for c in order):
        holders = [next((k for k in range(len(slots)) if slots[k][p] == c), None) for p in range(extent)]
        used = sorted({k for k in holders if k is not None})
        choice = [k if k is not None else used[0] for k in holders]
        outgoing = chosen({k: pieces[k] for k in used}, choice, axis).astype(jnp.bfloat16)
        arrived.append(lax.ppermute(outgoing, axis, [(p, s) for s, p in route]))
    return arrived


def give_back(pieces, axis):
    arrived = returned(pieces[1:], axis)
    return functools.reduce(jnp.add, [pieces[0]] + [a.astype(jnp.float32) for a in arrived])


def flip(block, axes, bits):
    sizes = [lax.axis_size(axis) for axis in axes]
    route = []
    for flat in range(math.prod(sizes)):
        rest, target, scale = flat, 0, 1
        for size, bit in zip(reversed(sizes), reversed(bits)):
            target += ((rest % size) ^ bit) * scale
            rest //= size
            scale *= size
        route.append((flat, target))
    return lax.ppermute(block, axes, route)


def rows_of(refs, part):
    block = refs[0][:, part]
    for ref in refs[1:]:
        block = block + ref[:, part]
    return block.reshape(-1, block.shape[-1])


def token_kernel(
    place, queries, queries_other, grads, weight, payload, grads_half, grad_rows, both_queries
):
    half = grads_half.shape[1]
    product = lax.dot_general(
        grads[...], weight[...], (((1,), (1,)), ((), ())), preferred_element_type=jnp.float32
    ).astype(jnp.bfloat16)
    grad_rows[...] = product
    payload[:, half:] = product
    payload[:, :half] = grads[:, pl.ds(pl.multiple_of((1 - place[0]) * half, half), half)]
    grads_half[...] = grads[:, pl.ds(pl.multiple_of(place[0] * half, half), half)]
    both_tiles(place, queries[...], queries_other[...], both_queries)


def both_tiles(place, mine, theirs, both):
    tile = mine.shape[0]
    both[pl.ds(pl.multiple_of(place[0] * tile, tile), tile), :] = mine
    both[pl.ds(pl.multiple_of((1 - place[0]) * tile, tile), tile), :] = theirs


def forward_kernel(inv_root, layout, carried, both_queries, *refs):
    groups, rest = split_groups(layout, refs)
    partial, scores = rest[-2:]
    dim = both_queries.shape[1]
    query_rows = both_queries[...]
    top, start, spans = None, 0, []
    if carried:
        top = rest[0][dim : dim + 1, :]
    for group in groups:
        keys = rows_of(group, 0)
        piece = lax.dot_general(
            keys, query_rows, (((1,), (1,)), ((), ())), preferred_element_type=jnp.float32
        )
        scores[start : start + keys.shape[0], :] = piece
        spans.append((start, keys.shape[0]))
        start += keys.shape[0]
        piece_top = jnp.max(piece, axis=0, keepdims=True) * inv_root
        top = piece_top if top is None else jnp.maximum(top, piece_top)
    if carried:
        share = jnp.exp(rest[0][dim : dim + 1, :] - top)
        total = rest[0][dim + 1 : dim + 2, :] * share
        mixed = rest[0][:dim, :] * share
    else:
        total = jnp.zeros_like(top)
        mixed = jnp.zeros((dim, query_rows.shape[0]), jnp.float32)
    for group, (start, count) in zip(groups, spans):
        weights = jnp.exp(scores[start : start + count, :] * inv_root - top)
        total = total + jnp.sum(weights, axis=0, keepdims=True)
        mixed = mixed + lax.dot_general(
            rows_of(group, 1),
            weights.astype(jnp.bfloat16),
            (((0,), (0,)), ((), ())),
            preferred_element_type=jnp.float32,
        )
    partial[:dim, :] = mixed
    row = lax.broadcasted_iota(jnp.int32, (STAT_ROWS, query_rows.shape[0]), 0)
    partial[dim:, :] = jnp.where(row == 0, top, total)


def merge_kernel(scale, plane, place, mine, theirs, payload, grads_half, grad_rows, *refs):
    stats, attended_own, terms, both_grads, both_attended, term_rows = (
        refs[0],
        refs[1],
        refs[2:-3],
        refs[-3],
        refs[-2],
        refs[-1],
    )
    tile, dim = grad_rows.shape
    half = grads_half.shape[1]
    top_a, top_b = mine[dim : dim + 1, :], theirs[dim : dim + 1, :]
    sum_a, sum_b = mine[dim + 1 : dim + 2, :], theirs[dim + 1 : dim + 2, :]
    top = jnp.maximum(top_a, top_b)
    share_a, share_b = jnp.exp(top_a - top), jnp.exp(top_b - top)
    total = share_a * sum_a + share_b * sum_b
    mixed = mine[:dim, :] * (share_a / total) + theirs[:dim, :] * (share_b / total)
    attended_t = mixed.astype(jnp.bfloat16).astype(jnp.float32)
    both_tiles(place, grad_rows[...], payload[:, half:], both_grads)
    row_dot = jnp.sum(both_grads[...].astype(jnp.float32).T * attended_t, axis=0, keepdims=True)
    row = lax.broadcasted_iota(jnp.int32, (STAT_ROWS, mixed.shape[1]), 0)
    stats[...] = jnp.where(row == 0, top + jnp.log(total), row_dot)
    both_attended[...] = attended_t.T.astype(jnp.bfloat16)
    rows_mine = both_attended[pl.ds(pl.multiple_of(place[0] * tile, tile), tile), :]
    rows_theirs = both_attended[pl.ds(pl.multiple_of((1 - place[0]) * tile, tile), tile), :]
    attended_own[...] = rows_mine
    if not terms:
        return
    contract = (((0,), (0,)), ((), ()))
    term = lax.dot_general(
        rows_mine, grads_half[...], contract, preferred_element_type=jnp.float32
    )
    term = term + lax.dot_general(
        rows_theirs, payload[:, :half], contract, preferred_element_type=jnp.float32
    )
    term_rows[...] = term * scale
    count = dim // plane
    for order, out in enumerate(terms):
        chunk = place[1] ^ order
        out[...] = term_rows[pl.ds(pl.multiple_of(chunk * count, count), count), :].astype(jnp.bfloat16)


def split_groups(layout, refs):
    groups, start = [], 0
    for count in layout:
        groups.append(refs[start : start + count])
        start += count
    return groups, refs[start:]


def backward_kernel(
    inv_root, layout, targets, carried, last, place, stats, both_queries, payload, grad_rows, *refs
):
    groups, rest = split_groups(layout, refs)
    given, rest = (rest[0], rest[1:]) if carried else (None, rest)
    count = 1 + max(out for out, _ in targets)
    outs, rest = rest[:count], rest[count:]
    both_grads = rest[-2] if last else rest[-1]
    tile, dim = grad_rows.shape
    columns = payload.shape[1]
    both_tiles(place, grad_rows[...], payload[:, columns - dim :], both_grads)
    query_rows, out_grads = both_queries[...], both_grads[...]
    level, row_dot = stats[0:1, :], stats[1:2, :]
    along = (((1,), (1,)), ((), ()))
    query_grad = given[...] if carried else jnp.zeros((dim, 2 * tile), jnp.float32)
    for group, (target, first) in zip(groups, targets):
        out, tiles = outs[target], group[0].shape[0]
        keys, values = rows_of(group, 0), rows_of(group, 1)
        scores = lax.dot_general(keys, query_rows, along, preferred_element_type=jnp.float32)
        probability = jnp.exp(scores * inv_root - level)
        prob_grad = lax.dot_general(values, out_grads, along, preferred_element_type=jnp.float32)
        score_grad = (probability * (prob_grad - row_dot)).astype(jnp.bfloat16)
        shape = (tiles,) + out.shape[2:]
        key_grad = jnp.dot(score_grad, query_rows, preferred_element_type=jnp.float32) * inv_root
        value_grad = jnp.dot(
            probability.astype(jnp.bfloat16), out_grads, preferred_element_type=jnp.float32
        )
        out[first : first + tiles, 0] = key_grad.reshape(shape).astype(out.dtype)
        out[first : first + tiles, 1] = value_grad.reshape(shape).astype(out.dtype)
        query_grad = query_grad + lax.dot_general(
            keys, score_grad, (((0,), (0,)), ((), ())), preferred_element_type=jnp.float32
        )
    if not last:
        rest[0][...] = query_grad
        return
    query_own, query_other, both_out = rest[0], rest[1], rest[-1]
    both_out[...] = query_grad.T * inv_root
    query_own[...] = both_out[pl.ds(pl.multiple_of(place[0] * tile, tile), tile), :]
    other = both_out[pl.ds(pl.multiple_of((1 - place[0]) * tile, tile), tile), :]
    other = other.astype(jnp.bfloat16)
    rows = query_other.shape[0]
    for block in range(tile // rows):
        query_other[:, block * dim : (block + 1) * dim] = other[block * rows : (block + 1) * rows]


def assemble_kernel(flipped, rows, place, part, *refs):
    rows_ref, done = refs[-2:]
    count, width = rows_ref.shape
    copies = []
    if flipped:
        query_own, _, whole, grad_query, sums = refs[:-2]
        dim, step = query_own.shape[1], part.shape[0] - count
        for block in range(width // dim):
            piece = part[count:, block * dim : (block + 1) * dim].astype(jnp.float32)
            span = slice(block * step, (block + 1) * step)
            sums[span, :] = (query_own[span, :] + piece).astype(jnp.bfloat16)
        copies.append(pltpu.make_async_copy(sums, grad_query, done.at[count // rows]))
        copies[-1].start()
    else:
        whole = refs[0]
    core = 1 - place[0] if flipped else place[0]
    columns = pl.ds(pl.multiple_of(core * width, width), width)
    for order in range(count // rows):
        span = pl.ds(pl.multiple_of((place[1] ^ order) * rows, rows), rows)
        rows_ref[span, :] = part[order * rows : (order + 1) * rows, :].astype(jnp.float32)
        copies.append(
            pltpu.make_async_copy(rows_ref.at[span, :], whole.at[span, columns], done.at[order])
        )
        copies[-1].start()
    for copy in copies:
        copy.wait()


def assemble(flipped, place, part, rows, shape, whole=None, query_own=None):
    anywhere = pl.BlockSpec(memory_space=pl.ANY)
    outs, out_specs, operands, in_specs = shape, anywhere, (place, part), [SMEM, VMEM]
    scratch = [
        pltpu.VMEM((shape.shape[0], part.shape[1]), jnp.float32),
        pltpu.SemaphoreType.DMA((shape.shape[0] // rows + flipped,)),
    ]
    if flipped:
        outs, out_specs = (shape, shaped(*query_own.shape)), (anywhere, anywhere)
        operands, in_specs = operands + (query_own, whole), in_specs + [VMEM, anywhere]
        scratch = [pltpu.VMEM(query_own.shape, jnp.bfloat16)] + scratch
    return pl.pallas_call(
        functools.partial(assemble_kernel, flipped, rows),
        out_shape=outs,
        in_specs=in_specs,
        out_specs=out_specs,
        scratch_shapes=scratch,
        input_output_aliases={3: 0} if flipped else {},
        compiler_params=PARAMS,
        cost_estimate=cost_of(10**10, 10**8),
    )(*operands)


def owner_kernel(own_grad, *refs):
    for k, out in enumerate(refs[-2:]):
        total = own_grad[k]
        for block in refs[:-2]:
            total = total + block[k].astype(jnp.float32)
        out[...] = total.astype(jnp.bfloat16)


def pack_kernel(*refs):
    start = 0
    for piece in refs[:-1]:
        refs[-1][start : start + piece.shape[0], :] = piece[...]
        start += piece.shape[0]


def combine_kernel(column, *refs):
    arrived, pieces = refs[: -column.shape[0]], refs[-column.shape[0] :]
    for k, piece in enumerate(pieces):
        total = column[k]
        for block in arrived:
            total = total + block[k].astype(jnp.float32)
        piece[...] = total.astype(piece.dtype)


def shaped(*shape, kind=jnp.bfloat16):
    return jax.ShapeDtypeStruct(shape, kind)


def kernel_call(kernel, operands, outs, scratch=(), cost=None):
    many = isinstance(outs, (list, tuple))
    return pl.pallas_call(
        kernel,
        out_shape=outs,
        in_specs=[SMEM] + [VMEM] * (len(operands) - 1),
        out_specs=[VMEM] * len(outs) if many else VMEM,
        scratch_shapes=list(scratch),
        compiler_params=PARAMS,
        cost_estimate=cost,
    )(*operands)


def cost_of(flops, moved):
    return pl.CostEstimate(flops=int(flops), bytes_accessed=int(moved), transcendentals=0)


PLANE_BITS = ((0, 0), (0, 1), (2, 0), (2, 1))


def sum_over_plane(terms):
    summed = terms[0].astype(jnp.float32)
    for term, bit in zip(terms[1:], PLANE_BITS[1:]):
        summed = summed + flip(term, ("frame", "width"), bit).astype(jnp.float32)
    return summed.astype(jnp.bfloat16)


def join_sum(part, query_own, query_other, place):
    plane = len(part)
    pieces = part + [query_other]
    part = pl.pallas_call(
        pack_kernel,
        out_shape=shaped(sum(p.shape[0] for p in pieces), pieces[0].shape[1]),
        in_specs=[VMEM] * len(pieces),
        out_specs=VMEM,
        compiler_params=PARAMS,
    )(*pieces)
    other = flip(part, ("frame",), (1,))
    rows = (part.shape[0] - query_other.shape[0]) // plane
    shape = shaped(plane * rows, 2 * part.shape[1], kind=jnp.float32)
    whole = assemble(False, place, part, rows, shape)
    return whole, lambda whole: assemble(True, place, other, rows, shape, whole, query_own)


def body(queries, key_vectors, value_vectors, out_weight, projected_grad):
    head_dim = queries.shape[-1]
    model_dim = out_weight.shape[1]
    half = model_dim // 2
    inv_root = 1.0 / math.sqrt(head_dim)
    extents = tuple(lax.axis_size(axis) for axis in AXES)
    assert extents[0] == 4
    small = extents[1:] == (4, 2)
    frame, height, width = (lax.axis_index(axis) for axis in AXES)
    core = frame % 2
    place = jnp.stack([core, (frame // 2) * 2 + width, height]).astype(jnp.int32)
    query_rows = queries.reshape(-1, head_dim)
    grads = projected_grad.reshape(-1, model_dim)
    tile = query_rows.shape[0]

    own = jnp.stack((key_vectors.reshape(tile, head_dim), value_vectors.reshape(tile, head_dim)))
    cross = [(2 * s + y, 2 * p + 1 - y) for s, p in ((2, 0), (1, 3)) for y in (0, 1)]

    if small:
        swap = [(0, 1), (1, 0)]
        tiles = fetch(own, "height")
        own_beside = lax.ppermute(own[None], "width", swap)
        others = jnp.stack(tiles)
        column = jnp.stack([own] + tiles)
        others, column, own_beside, query_rows_late = lax.optimization_barrier(
            (others, column, own_beside, query_rows)
        )
        others_beside = lax.ppermute(others, "width", swap)
        far = [
            lax.ppermute(column, ("frame", "width"), cross),
            lax.ppermute(column, "frame", [(2, 1), (1, 2)]),
        ]
        blocks = [column, own_beside, others_beside, *far]
        layout = (1, 1, 1, 2)
        targets = ((0, 0), (1, 0), (1, 1), (2, 0))
        column_tiles, kinds = 1 + others.shape[0], 3
    else:
        query_rows_late = query_rows
        column = jnp.stack([own] + fetch(own, "height"))
        beside = fetch(column, "width")
        everything = jnp.concatenate([column] + beside, axis=0)
        far = [
            lax.ppermute(everything[:, :, : tile // 2], "frame", [(2, 0), (1, 3)]),
            lax.ppermute(everything[:, :, tile // 2 :], "frame", [(2, 1), (1, 2)]),
        ]
        blocks = [column] + beside + far
        layout = (1,) * (1 + len(beside)) + (2,)
        targets = tuple((k, 0) for k in range(len(layout)))
        column_tiles, kinds = column.shape[0], len(layout)
    queries_other = flip(query_rows_late, ("frame",), (1,))
    payload, grads_half, grad_rows, both_queries = kernel_call(
        token_kernel,
        (place, query_rows, queries_other, grads, out_weight),
        (
            shaped(tile, half + head_dim),
            shaped(tile, half),
            shaped(tile, head_dim),
            shaped(2 * tile, head_dim),
        ),
        cost=cost_of(2 * tile * head_dim * model_dim, 4 * tile * model_dim),
    )
    grad_shapes = [(column_tiles, 2, tile, head_dim)] * (kinds - 1)
    grad_shapes.append((column_tiles, 2, tile, head_dim) if small else far[0].shape)
    key_count = sum(shape[0] * shape[2] for shape in grad_shapes)
    product = 2 * key_count * 2 * tile * head_dim
    moved = sum(b.size * 2 for b in blocks)

    def forward(operands, groups, carried):
        keys, start = 0, 0
        for count in groups:
            keys += operands[start].shape[0] * operands[start].shape[2]
            start += count
        return pl.pallas_call(
            functools.partial(forward_kernel, inv_root, groups, bool(carried)),
            out_shape=shaped(head_dim + STAT_ROWS, 2 * tile, kind=jnp.float32),
            in_specs=[VMEM] * (1 + len(operands) + len(carried)),
            out_specs=VMEM,
            scratch_shapes=[pltpu.VMEM((keys, 2 * tile), jnp.float32)],
            compiler_params=PARAMS,
            cost_estimate=cost_of(8 * keys * tile * head_dim, moved * keys // key_count),
        )(both_queries, *operands, *carried)

    partial = forward(blocks[:1], (1,), ())
    payload, partial, *blocks[1:] = lax.optimization_barrier((payload, partial, *blocks[1:]))
    payload = flip(payload, ("frame",), (1,))
    partial = forward(blocks[1:], layout[1:], (partial,))
    partial_other = flip(partial, ("frame",), (1,))
    plane = 4
    chunks = plane if small else 0
    merged = kernel_call(
        functools.partial(merge_kernel, 1.0 / float(math.prod(extents)), plane),
        (place, partial, partial_other, payload, grads_half, grad_rows),
        (
            shaped(STAT_ROWS, 2 * tile, kind=jnp.float32),
            shaped(tile, head_dim),
            *[shaped(head_dim // plane, half)] * chunks,
        ),
        scratch=(
            pltpu.VMEM((2 * tile, head_dim), jnp.bfloat16),
            pltpu.VMEM((2 * tile, head_dim), jnp.bfloat16),
            pltpu.VMEM((head_dim, half), jnp.float32),
        ),
        cost=cost_of(4 * tile * head_dim * half, 4 * tile * model_dim),
    )
    stats, attended, *terms = merged
    def backward(operands, groups, places, outs, carried=(), last=False):
        scratch = [pltpu.VMEM((2 * tile, head_dim), jnp.bfloat16)]
        if last:
            scratch.append(pltpu.VMEM((2 * tile, head_dim), jnp.float32))
            sums = (
                shaped(tile, head_dim, kind=jnp.float32),
                shaped(tile * head_dim // half, half),
            )
        else:
            sums = (shaped(head_dim, 2 * tile, kind=jnp.float32),)
        return kernel_call(
            functools.partial(backward_kernel, inv_root, groups, places, bool(carried), last),
            (place, stats, both_queries, payload, grad_rows, *operands, *carried),
            (*outs, *sums),
            scratch=scratch,
            cost=cost_of(10**9 if not last else 10**10, 10**8),
        )

    near = len(blocks) - len(far)
    *near_grads, query_grad = backward(
        blocks[:near],
        layout[:-1],
        targets[:-1],
        (shaped(*grad_shapes[0], kind=jnp.float32), *[shaped(*g) for g in grad_shapes[1:-1]]),
    )
    if small:
        terms[0], query_grad = lax.optimization_barrier((terms[0], query_grad))
        part = sum_over_plane(terms)
        part, query_grad = lax.optimization_barrier((part, query_grad))
    far_grad, query_own, query_other = backward(
        blocks[near:], layout[-1:], ((0, 0),), (shaped(*grad_shapes[-1]),), (query_grad,), True
    )
    back = (*near_grads, far_grad, query_own, query_other)
    if small:
        other = flip(part, ("height",), (1,))
        part = (part.astype(jnp.float32) + other.astype(jnp.float32)).astype(jnp.bfloat16)
        part, attended = lax.optimization_barrier((part, attended))
        other = flip(part, ("height",), (2,))
    else:
        weight_term = jnp.einsum("td,tm->dm", attended, grads, preferred_element_type=jnp.float32)
        grad_out_weight = lax.psum(weight_term, AXES) / float(math.prod(extents))
    projected = (
        jnp.dot(attended, out_weight, preferred_element_type=jnp.float32)
        .astype(jnp.bfloat16)
        .reshape(projected_grad.shape)
    )
    column_grad, *beside_grads, far_grad, query_own, query_other = back
    if small:
        arrived = [
            lax.ppermute(beside_grads[0], "width", [(0, 1), (1, 0)]),
            lax.ppermute(far_grad, "frame", [(1, 2), (2, 1)]),
            lax.ppermute(far_grad, ("frame", "width"), [(p, s) for s, p in cross]),
        ]
        other, projected = lax.optimization_barrier((other, projected))
        part = (part.astype(jnp.float32) + other.astype(jnp.float32)).astype(jnp.bfloat16)
        part, column_grad = lax.optimization_barrier((part, column_grad))
        part = [part] + [flip(part, ("frame", "width"), bit) for bit in PLANE_BITS[1:]]
        shape = column_grad.shape[1:]
        pieces = pl.pallas_call(
            combine_kernel,
            out_shape=[shaped(*shape, kind=jnp.float32)] + [shaped(*shape)] * (column_tiles - 1),
            in_specs=[VMEM] * 4,
            out_specs=[VMEM] * column_tiles,
            compiler_params=PARAMS,
        )(column_grad, *arrived)
        pieces = list(pieces)
    else:
        arrived = jnp.concatenate(
            (
                lax.ppermute(far_grad, "frame", [(0, 2), (3, 1)]),
                lax.ppermute(far_grad, "frame", [(1, 2), (2, 1)]),
            ),
            axis=2,
        ).astype(jnp.float32)
        pieces = [column_grad] + [b.astype(jnp.float32) for b in beside_grads]
        span = column_tiles
        pieces = [p + arrived[i * span : (i + 1) * span] for i, p in enumerate(pieces)]
        column_grad = give_back(pieces, "width")
        pieces = [column_grad[k] for k in range(column_tiles)]
    if small:
        whole, finish = join_sum(part, query_own, query_other, place)
        grad_out_weight, grad_query = finish(whole)
        grad_out_weight, pieces[0] = lax.optimization_barrier((grad_out_weight, pieces[0]))
    else:
        query_other = flip(query_other, ("frame",), (1,)).reshape(-1, half // head_dim, head_dim)
        query_other = query_other.transpose(1, 0, 2).reshape(tile, head_dim)
        grad_query = (query_own + query_other.astype(jnp.float32)).astype(jnp.bfloat16)
    operands = (pieces[0], *returned(pieces[1:], "height"))
    grad_key, grad_value = pl.pallas_call(
        owner_kernel,
        out_shape=[shaped(tile, head_dim)] * 2,
        in_specs=[VMEM] * len(operands),
        out_specs=[VMEM] * 2,
        compiler_params=PARAMS,
        cost_estimate=cost_of(10**10, 10**8),
    )(*operands)
    grad_key = grad_key.reshape(key_vectors.shape)
    grad_value = grad_value.reshape(value_vectors.shape)
    grad_query = grad_query.reshape(queries.shape)
    return (projected, grad_query, grad_key, grad_value, grad_out_weight)


def solution(mesh):
    tokens = P("frame", "height", "width", None)
    return jax.shard_map(
        body,
        mesh=mesh,
        in_specs=(tokens, tokens, tokens, P(), tokens),
        out_specs=(tokens, tokens, tokens, tokens, P()),
        check_vma=False,
    )
```

```python
import functools
import math

import jax
import jax.numpy as jnp
from jax import lax
from jax.experimental import pallas as pl
from jax.experimental.pallas import tpu as pltpu
from jax.sharding import PartitionSpec as P

AXES = ("frame", "height", "width")
VMEM = pl.BlockSpec(memory_space=pltpu.VMEM)
SMEM = pl.BlockSpec(memory_space=pltpu.SMEM)
PARAMS = pltpu.CompilerParams(vmem_limit_bytes=24 * 1024 * 1024)
STAT_ROWS = 8
FREE = pl.CostEstimate(flops=0, bytes_accessed=0, transcendentals=0)


def window_of(position, extent):
    span = min(3, extent)
    start = max(0, min(position - 1, extent - 3))
    return range(start, start + span)


def routes_of(extent):
    first = [(p ^ 1, p) for p in range(extent) if (p ^ 1) in window_of(p, extent)]
    if extent > 4:
        first = [(p + 1, p) for p in range(extent - 1)]
    wanted = [(s, p) for p in range(extent) for s in window_of(p, extent) if s != p]
    wanted.sort(key=lambda pair: (pair[0] ^ pair[1], pair))
    routes = [first]
    for pair in wanted:
        if pair in first:
            continue
        for route in routes[1:]:
            if all(pair[0] != s and pair[1] != p for s, p in route):
                route.append(pair)
                break
        else:
            routes.append([pair])
    return [route for route in routes if route]


def slots_of(extent):
    routes = routes_of(extent)
    arrivals = [[c for c, r in enumerate(routes) if any(q == p for _, q in r)] for p in range(extent)]
    return [[arrivals[p][k] for p in range(extent)] for k in range(min(3, extent) - 1)]


def chosen(options, choice, axis):
    value = options[choice[0]]
    position = lax.axis_index(axis)
    for option in sorted(set(choice)):
        if option != choice[0]:
            here = functools.reduce(
                jnp.logical_or, [position == p for p, c in enumerate(choice) if c == option]
            )
            value = jnp.where(here, options[option], value)
    return value


def fetch(block, axis):
    extent = lax.axis_size(axis)
    routes = routes_of(extent)
    arrived = [lax.ppermute(block, axis, route) for route in routes]
    tiles = []
    for slot in slots_of(extent):
        used = sorted(set(slot))
        reached = sum(len(routes[c]) for c in used)
        if reached == extent:
            tiles.append(functools.reduce(jnp.add, [arrived[c] for c in used]))
        else:
            tiles.append(chosen(arrived, slot, axis))
    return tiles


def returned(pieces, axis):
    extent = lax.axis_size(axis)
    slots = slots_of(extent)
    arrived = []
    order = (0, 2, 1) if extent == 4 else range(len(routes_of(extent)))
    for c, route in ((c, routes_of(extent)[c]) for c in order):
        holders = [next((k for k in range(len(slots)) if slots[k][p] == c), None) for p in range(extent)]
        used = sorted({k for k in holders if k is not None})
        choice = [k if k is not None else used[0] for k in holders]
        outgoing = chosen({k: pieces[k] for k in used}, choice, axis).astype(jnp.bfloat16)
        arrived.append(lax.ppermute(outgoing, axis, [(p, s) for s, p in route]))
    return arrived


def give_back(pieces, axis):
    arrived = returned(pieces[1:], axis)
    return functools.reduce(jnp.add, [pieces[0]] + [a.astype(jnp.float32) for a in arrived])


def flip(block, axes, bits):
    sizes = [lax.axis_size(axis) for axis in axes]
    route = []
    for flat in range(math.prod(sizes)):
        rest, target, scale = flat, 0, 1
        for size, bit in zip(reversed(sizes), reversed(bits)):
            target += ((rest % size) ^ bit) * scale
            rest //= size
            scale *= size
        route.append((flat, target))
    return lax.ppermute(block, axes, route)


def rows_of(refs, part):
    block = refs[0][:, part]
    for ref in refs[1:]:
        block = block + ref[:, part]
    return block.reshape(-1, block.shape[-1])


def token_kernel(
    place, queries, queries_other, grads, weight, payload, grads_half, grad_rows, both_queries
):
    half = grads_half.shape[1]
    product = lax.dot_general(
        grads[...], weight[...], (((1,), (1,)), ((), ())), preferred_element_type=jnp.float32
    ).astype(jnp.bfloat16)
    grad_rows[...] = product
    payload[:, half:] = product
    payload[:, :half] = grads[:, pl.ds(pl.multiple_of((1 - place[0]) * half, half), half)]
    grads_half[...] = grads[:, pl.ds(pl.multiple_of(place[0] * half, half), half)]
    both_tiles(place, queries[...], queries_other[...], both_queries)


def both_tiles(place, mine, theirs, both):
    tile = mine.shape[0]
    both[pl.ds(pl.multiple_of(place[0] * tile, tile), tile), :] = mine
    both[pl.ds(pl.multiple_of((1 - place[0]) * tile, tile), tile), :] = theirs


def forward_kernel(inv_root, layout, carried, both_queries, *refs):
    groups, rest = split_groups(layout, refs)
    partial, scores = rest[-2:]
    dim = both_queries.shape[1]
    query_rows = both_queries[...]
    top, start, spans = None, 0, []
    if carried:
        top = rest[0][dim : dim + 1, :]
    for group in groups:
        keys = rows_of(group, 0)
        piece = lax.dot_general(
            keys, query_rows, (((1,), (1,)), ((), ())), preferred_element_type=jnp.float32
        )
        scores[start : start + keys.shape[0], :] = piece
        spans.append((start, keys.shape[0]))
        start += keys.shape[0]
        piece_top = jnp.max(piece, axis=0, keepdims=True) * inv_root
        top = piece_top if top is None else jnp.maximum(top, piece_top)
    if carried:
        share = jnp.exp(rest[0][dim : dim + 1, :] - top)
        total = rest[0][dim + 1 : dim + 2, :] * share
        mixed = rest[0][:dim, :] * share
    else:
        total = jnp.zeros_like(top)
        mixed = jnp.zeros((dim, query_rows.shape[0]), jnp.float32)
    for group, (start, count) in zip(groups, spans):
        weights = jnp.exp(scores[start : start + count, :] * inv_root - top)
        total = total + jnp.sum(weights, axis=0, keepdims=True)
        mixed = mixed + lax.dot_general(
            rows_of(group, 1),
            weights.astype(jnp.bfloat16),
            (((0,), (0,)), ((), ())),
            preferred_element_type=jnp.float32,
        )
    partial[:dim, :] = mixed
    row = lax.broadcasted_iota(jnp.int32, (STAT_ROWS, query_rows.shape[0]), 0)
    partial[dim:, :] = jnp.where(row == 0, top, total)


def merge_kernel(scale, plane, place, mine, theirs, payload, grads_half, grad_rows, *refs):
    stats, attended_own, terms, both_grads, both_attended, term_rows = (
        refs[0],
        refs[1],
        refs[2:-3],
        refs[-3],
        refs[-2],
        refs[-1],
    )
    tile, dim = grad_rows.shape
    half = grads_half.shape[1]
    top_a, top_b = mine[dim : dim + 1, :], theirs[dim : dim + 1, :]
    sum_a, sum_b = mine[dim + 1 : dim + 2, :], theirs[dim + 1 : dim + 2, :]
    top = jnp.maximum(top_a, top_b)
    share_a, share_b = jnp.exp(top_a - top), jnp.exp(top_b - top)
    total = share_a * sum_a + share_b * sum_b
    mixed = mine[:dim, :] * (share_a / total) + theirs[:dim, :] * (share_b / total)
    attended_t = mixed.astype(jnp.bfloat16).astype(jnp.float32)
    both_tiles(place, grad_rows[...], payload[:, half:], both_grads)
    row_dot = jnp.sum(both_grads[...].astype(jnp.float32).T * attended_t, axis=0, keepdims=True)
    row = lax.broadcasted_iota(jnp.int32, (STAT_ROWS, mixed.shape[1]), 0)
    stats[...] = jnp.where(row == 0, top + jnp.log(total), row_dot)
    both_attended[...] = attended_t.T.astype(jnp.bfloat16)
    rows_mine = both_attended[pl.ds(pl.multiple_of(place[0] * tile, tile), tile), :]
    rows_theirs = both_attended[pl.ds(pl.multiple_of((1 - place[0]) * tile, tile), tile), :]
    attended_own[...] = rows_mine
    if not terms:
        return
    contract = (((0,), (0,)), ((), ()))
    term = lax.dot_general(
        rows_mine, grads_half[...], contract, preferred_element_type=jnp.float32
    )
    term = term + lax.dot_general(
        rows_theirs, payload[:, :half], contract, preferred_element_type=jnp.float32
    )
    term_rows[...] = term * scale
    count = dim // plane
    for order, out in enumerate(terms):
        chunk = place[1] ^ order
        out[...] = term_rows[pl.ds(pl.multiple_of(chunk * count, count), count), :].astype(jnp.bfloat16)


def split_groups(layout, refs):
    groups, start = [], 0
    for count in layout:
        groups.append(refs[start : start + count])
        start += count
    return groups, refs[start:]


def backward_kernel(
    inv_root, layout, targets, carried, last, place, stats, both_queries, payload, grad_rows, *refs
):
    groups, rest = split_groups(layout, refs)
    given, rest = (rest[0], rest[1:]) if carried else (None, rest)
    count = 1 + max(out for out, _ in targets)
    outs, rest = rest[:count], rest[count:]
    both_grads = rest[-2] if last else rest[-1]
    tile, dim = grad_rows.shape
    columns = payload.shape[1]
    both_tiles(place, grad_rows[...], payload[:, columns - dim :], both_grads)
    query_rows, out_grads = both_queries[...], both_grads[...]
    level, row_dot = stats[0:1, :], stats[1:2, :]
    along = (((1,), (1,)), ((), ()))
    query_grad = given[...] if carried else jnp.zeros((dim, 2 * tile), jnp.float32)
    for group, (target, first) in zip(groups, targets):
        out, tiles = outs[target], group[0].shape[0]
        keys, values = rows_of(group, 0), rows_of(group, 1)
        scores = lax.dot_general(keys, query_rows, along, preferred_element_type=jnp.float32)
        probability = jnp.exp(scores * inv_root - level)
        prob_grad = lax.dot_general(values, out_grads, along, preferred_element_type=jnp.float32)
        score_grad = (probability * (prob_grad - row_dot)).astype(jnp.bfloat16)
        shape = (tiles,) + out.shape[2:]
        key_grad = jnp.dot(score_grad, query_rows, preferred_element_type=jnp.float32) * inv_root
        value_grad = jnp.dot(
            probability.astype(jnp.bfloat16), out_grads, preferred_element_type=jnp.float32
        )
        out[first : first + tiles, 0] = key_grad.reshape(shape).astype(out.dtype)
        out[first : first + tiles, 1] = value_grad.reshape(shape).astype(out.dtype)
        query_grad = query_grad + lax.dot_general(
            keys, score_grad, (((0,), (0,)), ((), ())), preferred_element_type=jnp.float32
        )
    if not last:
        rest[0][...] = query_grad
        return
    query_own, query_other, both_out = rest[0], rest[1], rest[-1]
    both_out[...] = query_grad.T * inv_root
    query_own[...] = both_out[pl.ds(pl.multiple_of(place[0] * tile, tile), tile), :]
    other = both_out[pl.ds(pl.multiple_of((1 - place[0]) * tile, tile), tile), :]
    other = other.astype(jnp.bfloat16)
    rows = query_other.shape[0]
    for block in range(tile // rows):
        query_other[:, block * dim : (block + 1) * dim] = other[block * rows : (block + 1) * rows]


def assemble_kernel(flipped, rows, place, part, *refs):
    rows_ref, done = refs[-2:]
    count, width = rows_ref.shape
    copies = []
    if flipped:
        query_own, _, whole, grad_query, sums = refs[:-2]
        dim, step = query_own.shape[1], part.shape[0] - count
        for block in range(width // dim):
            piece = part[count:, block * dim : (block + 1) * dim].astype(jnp.float32)
            span = slice(block * step, (block + 1) * step)
            sums[span, :] = (query_own[span, :] + piece).astype(jnp.bfloat16)
        copies.append(pltpu.make_async_copy(sums, grad_query, done.at[count // rows]))
        copies[-1].start()
    else:
        whole = refs[0]
    core = 1 - place[0] if flipped else place[0]
    columns = pl.ds(pl.multiple_of(core * width, width), width)
    for order in range(count // rows):
        span = pl.ds(pl.multiple_of((place[1] ^ order) * rows, rows), rows)
        rows_ref[span, :] = part[order * rows : (order + 1) * rows, :].astype(jnp.float32)
        copies.append(
            pltpu.make_async_copy(rows_ref.at[span, :], whole.at[span, columns], done.at[order])
        )
        copies[-1].start()
    for copy in copies:
        copy.wait()


def assemble(flipped, place, part, rows, shape, whole=None, query_own=None):
    anywhere = pl.BlockSpec(memory_space=pl.ANY)
    outs, out_specs, operands, in_specs = shape, anywhere, (place, part), [SMEM, VMEM]
    scratch = [
        pltpu.VMEM((shape.shape[0], part.shape[1]), jnp.float32),
        pltpu.SemaphoreType.DMA((shape.shape[0] // rows + flipped,)),
    ]
    if flipped:
        outs, out_specs = (shape, shaped(*query_own.shape)), (anywhere, anywhere)
        operands, in_specs = operands + (query_own, whole), in_specs + [VMEM, anywhere]
        scratch = [pltpu.VMEM(query_own.shape, jnp.bfloat16)] + scratch
    return pl.pallas_call(
        functools.partial(assemble_kernel, flipped, rows),
        out_shape=outs,
        in_specs=in_specs,
        out_specs=out_specs,
        scratch_shapes=scratch,
        input_output_aliases={3: 0} if flipped else {},
        compiler_params=PARAMS,
        cost_estimate=cost_of(10**10, 10**8),
    )(*operands)


def owner_kernel(own_grad, *refs):
    for k, out in enumerate(refs[-2:]):
        total = own_grad[k]
        for block in refs[:-2]:
            total = total + block[k].astype(jnp.float32)
        out[...] = total.astype(jnp.bfloat16)


def pack_kernel(*refs):
    start = 0
    for piece in refs[:-1]:
        refs[-1][start : start + piece.shape[0], :] = piece[...]
        start += piece.shape[0]


def combine_kernel(column, *refs):
    arrived, pieces = refs[: -column.shape[0]], refs[-column.shape[0] :]
    for k, piece in enumerate(pieces):
        total = column[k]
        for block in arrived:
            total = total + block[k].astype(jnp.float32)
        piece[...] = total.astype(piece.dtype)


def shaped(*shape, kind=jnp.bfloat16):
    return jax.ShapeDtypeStruct(shape, kind)


def kernel_call(kernel, operands, outs, scratch=(), cost=None):
    many = isinstance(outs, (list, tuple))
    return pl.pallas_call(
        kernel,
        out_shape=outs,
        in_specs=[SMEM] + [VMEM] * (len(operands) - 1),
        out_specs=[VMEM] * len(outs) if many else VMEM,
        scratch_shapes=list(scratch),
        compiler_params=PARAMS,
        cost_estimate=cost,
    )(*operands)


def cost_of(flops, moved):
    return pl.CostEstimate(flops=int(flops), bytes_accessed=int(moved), transcendentals=0)


PLANE_BITS = ((0, 0), (0, 1), (2, 0), (2, 1))


def sum_over_plane(terms):
    summed = terms[0].astype(jnp.float32)
    for term, bit in zip(terms[1:], PLANE_BITS[1:]):
        summed = summed + flip(term, ("frame", "width"), bit).astype(jnp.float32)
    return summed.astype(jnp.bfloat16)


def join_sum(part, query_own, query_other, place):
    plane = len(part)
    pieces = part + [query_other]
    part = pl.pallas_call(
        pack_kernel,
        out_shape=shaped(sum(p.shape[0] for p in pieces), pieces[0].shape[1]),
        in_specs=[VMEM] * len(pieces),
        out_specs=VMEM,
        compiler_params=PARAMS,
    )(*pieces)
    other = flip(part, ("frame",), (1,))
    rows = (part.shape[0] - query_other.shape[0]) // plane
    shape = shaped(plane * rows, 2 * part.shape[1], kind=jnp.float32)
    whole = assemble(False, place, part, rows, shape)
    return whole, lambda whole: assemble(True, place, other, rows, shape, whole, query_own)


def body(queries, key_vectors, value_vectors, out_weight, projected_grad):
    head_dim = queries.shape[-1]
    model_dim = out_weight.shape[1]
    half = model_dim // 2
    inv_root = 1.0 / math.sqrt(head_dim)
    extents = tuple(lax.axis_size(axis) for axis in AXES)
    assert extents[0] == 4
    small = extents[1:] == (4, 2)
    frame, height, width = (lax.axis_index(axis) for axis in AXES)
    core = frame % 2
    place = jnp.stack([core, (frame // 2) * 2 + width, height]).astype(jnp.int32)
    query_rows = queries.reshape(-1, head_dim)
    grads = projected_grad.reshape(-1, model_dim)
    tile = query_rows.shape[0]

    own = jnp.stack((key_vectors.reshape(tile, head_dim), value_vectors.reshape(tile, head_dim)))
    cross = [(2 * s + y, 2 * p + 1 - y) for s, p in ((2, 0), (1, 3)) for y in (0, 1)]

    if small:
        swap = [(0, 1), (1, 0)]
        tiles = fetch(own, "height")
        own_beside = lax.ppermute(own[None], "width", swap)
        others = jnp.stack(tiles)
        column = jnp.stack([own] + tiles)
        others, column, own_beside, query_rows_late = lax.optimization_barrier(
            (others, column, own_beside, query_rows)
        )
        others_beside = lax.ppermute(others, "width", swap)
        far = [
            lax.ppermute(column, "frame", [(2, 1), (1, 2)]),
            lax.ppermute(column, ("frame", "width"), cross),
        ]
        blocks = [column, own_beside, others_beside, *far]
        layout = (1, 1, 1, 2)
        targets = ((0, 0), (1, 0), (1, 1), (2, 0))
        column_tiles, kinds = 1 + others.shape[0], 3
    else:
        query_rows_late = query_rows
        column = jnp.stack([own] + fetch(own, "height"))
        beside = fetch(column, "width")
        everything = jnp.concatenate([column] + beside, axis=0)
        far = [
            lax.ppermute(everything[:, :, : tile // 2], "frame", [(2, 0), (1, 3)]),
            lax.ppermute(everything[:, :, tile // 2 :], "frame", [(2, 1), (1, 2)]),
        ]
        blocks = [column] + beside + far
        layout = (1,) * (1 + len(beside)) + (2,)
        targets = tuple((k, 0) for k in range(len(layout)))
        column_tiles, kinds = column.shape[0], len(layout)
    queries_other = flip(query_rows_late, ("frame",), (1,))
    payload, grads_half, grad_rows, both_queries = kernel_call(
        token_kernel,
        (place, query_rows, queries_other, grads, out_weight),
        (
            shaped(tile, half + head_dim),
            shaped(tile, half),
            shaped(tile, head_dim),
            shaped(2 * tile, head_dim),
        ),
        cost=cost_of(2 * tile * head_dim * model_dim, 4 * tile * model_dim),
    )
    grad_shapes = [(column_tiles, 2, tile, head_dim)] * (kinds - 1)
    grad_shapes.append((column_tiles, 2, tile, head_dim) if small else far[0].shape)
    key_count = sum(shape[0] * shape[2] for shape in grad_shapes)
    product = 2 * key_count * 2 * tile * head_dim
    moved = sum(b.size * 2 for b in blocks)

    def forward(operands, groups, carried):
        keys, start = 0, 0
        for count in groups:
            keys += operands[start].shape[0] * operands[start].shape[2]
            start += count
        return pl.pallas_call(
            functools.partial(forward_kernel, inv_root, groups, bool(carried)),
            out_shape=shaped(head_dim + STAT_ROWS, 2 * tile, kind=jnp.float32),
            in_specs=[VMEM] * (1 + len(operands) + len(carried)),
            out_specs=VMEM,
            scratch_shapes=[pltpu.VMEM((keys, 2 * tile), jnp.float32)],
            compiler_params=PARAMS,
            cost_estimate=cost_of(8 * keys * tile * head_dim, moved * keys // key_count),
        )(both_queries, *operands, *carried)

    partial = forward(blocks[:1], (1,), ())
    payload, partial, *blocks[1:] = lax.optimization_barrier((payload, partial, *blocks[1:]))
    payload = flip(payload, ("frame",), (1,))
    partial = forward(blocks[1:], layout[1:], (partial,))
    partial_other = flip(partial, ("frame",), (1,))
    plane = 4
    chunks = plane if small else 0
    merged = kernel_call(
        functools.partial(merge_kernel, 1.0 / float(math.prod(extents)), plane),
        (place, partial, partial_other, payload, grads_half, grad_rows),
        (
            shaped(STAT_ROWS, 2 * tile, kind=jnp.float32),
            shaped(tile, head_dim),
            *[shaped(head_dim // plane, half)] * chunks,
        ),
        scratch=(
            pltpu.VMEM((2 * tile, head_dim), jnp.bfloat16),
            pltpu.VMEM((2 * tile, head_dim), jnp.bfloat16),
            pltpu.VMEM((head_dim, half), jnp.float32),
        ),
        cost=cost_of(4 * tile * head_dim * half, 4 * tile * model_dim),
    )
    stats, attended, *terms = merged
    def backward(operands, groups, places, outs, carried=(), last=False):
        scratch = [pltpu.VMEM((2 * tile, head_dim), jnp.bfloat16)]
        if last:
            scratch.append(pltpu.VMEM((2 * tile, head_dim), jnp.float32))
            sums = (
                shaped(tile, head_dim, kind=jnp.float32),
                shaped(tile * head_dim // half, half),
            )
        else:
            sums = (shaped(head_dim, 2 * tile, kind=jnp.float32),)
        return kernel_call(
            functools.partial(backward_kernel, inv_root, groups, places, bool(carried), last),
            (place, stats, both_queries, payload, grad_rows, *operands, *carried),
            (*outs, *sums),
            scratch=scratch,
            cost=cost_of(10**9 if not last else 10**10, 10**8),
        )

    near = len(blocks) - len(far)
    *near_grads, query_grad = backward(
        blocks[:near],
        layout[:-1],
        targets[:-1],
        (shaped(*grad_shapes[0], kind=jnp.float32), *[shaped(*g) for g in grad_shapes[1:-1]]),
    )
    if small:
        terms[0], query_grad = lax.optimization_barrier((terms[0], query_grad))
        part = sum_over_plane(terms)
        part, query_grad = lax.optimization_barrier((part, query_grad))
    far_grad, query_own, query_other = backward(
        blocks[near:], layout[-1:], ((0, 0),), (shaped(*grad_shapes[-1]),), (query_grad,), True
    )
    back = (*near_grads, far_grad, query_own, query_other)
    if small:
        other = flip(part, ("height",), (1,))
        part = (part.astype(jnp.float32) + other.astype(jnp.float32)).astype(jnp.bfloat16)
        part, attended = lax.optimization_barrier((part, attended))
        other = flip(part, ("height",), (2,))
    else:
        weight_term = jnp.einsum("td,tm->dm", attended, grads, preferred_element_type=jnp.float32)
        grad_out_weight = lax.psum(weight_term, AXES) / float(math.prod(extents))
    projected = (
        jnp.dot(attended, out_weight, preferred_element_type=jnp.float32)
        .astype(jnp.bfloat16)
        .reshape(projected_grad.shape)
    )
    column_grad, *beside_grads, far_grad, query_own, query_other = back
    if small:
        arrived = [
            lax.ppermute(beside_grads[0], "width", [(0, 1), (1, 0)]),
            lax.ppermute(far_grad, "frame", [(1, 2), (2, 1)]),
            lax.ppermute(far_grad, ("frame", "width"), [(p, s) for s, p in cross]),
        ]
        other, projected = lax.optimization_barrier((other, projected))
        part = (part.astype(jnp.float32) + other.astype(jnp.float32)).astype(jnp.bfloat16)
        part, column_grad = lax.optimization_barrier((part, column_grad))
        part = [part] + [flip(part, ("frame", "width"), bit) for bit in PLANE_BITS[1:]]
        shape = column_grad.shape[1:]
        pieces = pl.pallas_call(
            combine_kernel,
            out_shape=[shaped(*shape, kind=jnp.float32)] + [shaped(*shape)] * (column_tiles - 1),
            in_specs=[VMEM] * 4,
            out_specs=[VMEM] * column_tiles,
            compiler_params=PARAMS,
        )(column_grad, *arrived)
        pieces = list(pieces)
    else:
        arrived = jnp.concatenate(
            (
                lax.ppermute(far_grad, "frame", [(0, 2), (3, 1)]),
                lax.ppermute(far_grad, "frame", [(1, 2), (2, 1)]),
            ),
            axis=2,
        ).astype(jnp.float32)
        pieces = [column_grad] + [b.astype(jnp.float32) for b in beside_grads]
        span = column_tiles
        pieces = [p + arrived[i * span : (i + 1) * span] for i, p in enumerate(pieces)]
        column_grad = give_back(pieces, "width")
        pieces = [column_grad[k] for k in range(column_tiles)]
    if small:
        whole, finish = join_sum(part, query_own, query_other, place)
        grad_out_weight, grad_query = finish(whole)
        grad_out_weight, pieces[0] = lax.optimization_barrier((grad_out_weight, pieces[0]))
    else:
        query_other = flip(query_other, ("frame",), (1,)).reshape(-1, half // head_dim, head_dim)
        query_other = query_other.transpose(1, 0, 2).reshape(tile, head_dim)
        grad_query = (query_own + query_other.astype(jnp.float32)).astype(jnp.bfloat16)
    operands = (pieces[0], *returned(pieces[1:], "height"))
    grad_key, grad_value = pl.pallas_call(
        owner_kernel,
        out_shape=[shaped(tile, head_dim)] * 2,
        in_specs=[VMEM] * len(operands),
        out_specs=[VMEM] * 2,
        compiler_params=PARAMS,
        cost_estimate=cost_of(10**10, 10**8),
    )(*operands)
    grad_key = grad_key.reshape(key_vectors.shape)
    grad_value = grad_value.reshape(value_vectors.shape)
    grad_query = grad_query.reshape(queries.shape)
    return (projected, grad_query, grad_key, grad_value, grad_out_weight)


def solution(mesh):
    tokens = P("frame", "height", "width", None)
    return jax.shard_map(
        body,
        mesh=mesh,
        in_specs=(tokens, tokens, tokens, P(), tokens),
        out_specs=(tokens, tokens, tokens, tokens, P()),
        check_vma=False,
    )
```

```python
import functools
import math

import jax
import jax.numpy as jnp
from jax import lax
from jax.experimental import pallas as pl
from jax.experimental.pallas import tpu as pltpu
from jax.sharding import PartitionSpec as P

AXES = ("frame", "height", "width")
VMEM = pl.BlockSpec(memory_space=pltpu.VMEM)
SMEM = pl.BlockSpec(memory_space=pltpu.SMEM)
PARAMS = pltpu.CompilerParams(vmem_limit_bytes=24 * 1024 * 1024)
STAT_ROWS = 8
FREE = pl.CostEstimate(flops=0, bytes_accessed=0, transcendentals=0)


def window_of(position, extent):
    span = min(3, extent)
    start = max(0, min(position - 1, extent - 3))
    return range(start, start + span)


def routes_of(extent):
    first = [(p ^ 1, p) for p in range(extent) if (p ^ 1) in window_of(p, extent)]
    if extent > 4:
        first = [(p + 1, p) for p in range(extent - 1)]
    wanted = [(s, p) for p in range(extent) for s in window_of(p, extent) if s != p]
    wanted.sort(key=lambda pair: (pair[0] ^ pair[1], pair))
    routes = [first]
    for pair in wanted:
        if pair in first:
            continue
        for route in routes[1:]:
            if all(pair[0] != s and pair[1] != p for s, p in route):
                route.append(pair)
                break
        else:
            routes.append([pair])
    return [route for route in routes if route]


def slots_of(extent):
    routes = routes_of(extent)
    arrivals = [[c for c, r in enumerate(routes) if any(q == p for _, q in r)] for p in range(extent)]
    return [[arrivals[p][k] for p in range(extent)] for k in range(min(3, extent) - 1)]


def chosen(options, choice, axis):
    value = options[choice[0]]
    position = lax.axis_index(axis)
    for option in sorted(set(choice)):
        if option != choice[0]:
            here = functools.reduce(
                jnp.logical_or, [position == p for p, c in enumerate(choice) if c == option]
            )
            value = jnp.where(here, options[option], value)
    return value


def fetch(block, axis):
    extent = lax.axis_size(axis)
    routes = routes_of(extent)
    arrived = [lax.ppermute(block, axis, route) for route in routes]
    tiles = []
    for slot in slots_of(extent):
        used = sorted(set(slot))
        reached = sum(len(routes[c]) for c in used)
        if reached == extent:
            tiles.append(functools.reduce(jnp.add, [arrived[c] for c in used]))
        else:
            tiles.append(chosen(arrived, slot, axis))
    return tiles


def returned(pieces, axis):
    extent = lax.axis_size(axis)
    slots = slots_of(extent)
    arrived = []
    order = (0, 2, 1) if extent == 4 else range(len(routes_of(extent)))
    for c, route in ((c, routes_of(extent)[c]) for c in order):
        holders = [next((k for k in range(len(slots)) if slots[k][p] == c), None) for p in range(extent)]
        used = sorted({k for k in holders if k is not None})
        choice = [k if k is not None else used[0] for k in holders]
        outgoing = chosen({k: pieces[k] for k in used}, choice, axis).astype(jnp.bfloat16)
        arrived.append(lax.ppermute(outgoing, axis, [(p, s) for s, p in route]))
    return arrived


def give_back(pieces, axis):
    arrived = returned(pieces[1:], axis)
    return functools.reduce(jnp.add, [pieces[0]] + [a.astype(jnp.float32) for a in arrived])


def flip(block, axes, bits):
    sizes = [lax.axis_size(axis) for axis in axes]
    route = []
    for flat in range(math.prod(sizes)):
        rest, target, scale = flat, 0, 1
        for size, bit in zip(reversed(sizes), reversed(bits)):
            target += ((rest % size) ^ bit) * scale
            rest //= size
            scale *= size
        route.append((flat, target))
    return lax.ppermute(block, axes, route)


def rows_of(refs, part):
    block = refs[0][:, part]
    for ref in refs[1:]:
        block = block + ref[:, part]
    return block.reshape(-1, block.shape[-1])


def token_kernel(
    place, queries, queries_other, grads, weight, payload, grads_half, grad_rows, both_queries
):
    half = grads_half.shape[1]
    product = lax.dot_general(
        grads[...], weight[...], (((1,), (1,)), ((), ())), preferred_element_type=jnp.float32
    ).astype(jnp.bfloat16)
    grad_rows[...] = product
    payload[:, half:] = product
    payload[:, :half] = grads[:, pl.ds(pl.multiple_of((1 - place[0]) * half, half), half)]
    grads_half[...] = grads[:, pl.ds(pl.multiple_of(place[0] * half, half), half)]
    both_tiles(place, queries[...], queries_other[...], both_queries)


def both_tiles(place, mine, theirs, both):
    tile = mine.shape[0]
    both[pl.ds(pl.multiple_of(place[0] * tile, tile), tile), :] = mine
    both[pl.ds(pl.multiple_of((1 - place[0]) * tile, tile), tile), :] = theirs


def forward_kernel(inv_root, layout, carried, both_queries, *refs):
    groups, rest = split_groups(layout, refs)
    partial, scores = rest[-2:]
    dim = both_queries.shape[1]
    query_rows = both_queries[...]
    top, start, spans = None, 0, []
    if carried:
        top = rest[0][dim : dim + 1, :]
    for group in groups:
        keys = rows_of(group, 0)
        piece = lax.dot_general(
            keys, query_rows, (((1,), (1,)), ((), ())), preferred_element_type=jnp.float32
        )
        scores[start : start + keys.shape[0], :] = piece
        spans.append((start, keys.shape[0]))
        start += keys.shape[0]
        piece_top = jnp.max(piece, axis=0, keepdims=True) * inv_root
        top = piece_top if top is None else jnp.maximum(top, piece_top)
    if carried:
        share = jnp.exp(rest[0][dim : dim + 1, :] - top)
        total = rest[0][dim + 1 : dim + 2, :] * share
        mixed = rest[0][:dim, :] * share
    else:
        total = jnp.zeros_like(top)
        mixed = jnp.zeros((dim, query_rows.shape[0]), jnp.float32)
    for group, (start, count) in zip(groups, spans):
        weights = jnp.exp(scores[start : start + count, :] * inv_root - top)
        total = total + jnp.sum(weights, axis=0, keepdims=True)
        mixed = mixed + lax.dot_general(
            rows_of(group, 1),
            weights.astype(jnp.bfloat16),
            (((0,), (0,)), ((), ())),
            preferred_element_type=jnp.float32,
        )
    partial[:dim, :] = mixed
    row = lax.broadcasted_iota(jnp.int32, (STAT_ROWS, query_rows.shape[0]), 0)
    partial[dim:, :] = jnp.where(row == 0, top, total)


def merge_kernel(scale, plane, place, mine, theirs, payload, grads_half, grad_rows, *refs):
    stats, attended_own, terms, both_grads, both_attended, term_rows = (
        refs[0],
        refs[1],
        refs[2:-3],
        refs[-3],
        refs[-2],
        refs[-1],
    )
    tile, dim = grad_rows.shape
    half = grads_half.shape[1]
    top_a, top_b = mine[dim : dim + 1, :], theirs[dim : dim + 1, :]
    sum_a, sum_b = mine[dim + 1 : dim + 2, :], theirs[dim + 1 : dim + 2, :]
    top = jnp.maximum(top_a, top_b)
    share_a, share_b = jnp.exp(top_a - top), jnp.exp(top_b - top)
    total = share_a * sum_a + share_b * sum_b
    mixed = mine[:dim, :] * (share_a / total) + theirs[:dim, :] * (share_b / total)
    attended_t = mixed.astype(jnp.bfloat16).astype(jnp.float32)
    both_tiles(place, grad_rows[...], payload[:, half:], both_grads)
    row_dot = jnp.sum(both_grads[...].astype(jnp.float32).T * attended_t, axis=0, keepdims=True)
    row = lax.broadcasted_iota(jnp.int32, (STAT_ROWS, mixed.shape[1]), 0)
    stats[...] = jnp.where(row == 0, top + jnp.log(total), row_dot)
    both_attended[...] = attended_t.T.astype(jnp.bfloat16)
    rows_mine = both_attended[pl.ds(pl.multiple_of(place[0] * tile, tile), tile), :]
    rows_theirs = both_attended[pl.ds(pl.multiple_of((1 - place[0]) * tile, tile), tile), :]
    attended_own[...] = rows_mine
    if not terms:
        return
    contract = (((0,), (0,)), ((), ()))
    term = lax.dot_general(
        rows_mine, grads_half[...], contract, preferred_element_type=jnp.float32
    )
    term = term + lax.dot_general(
        rows_theirs, payload[:, :half], contract, preferred_element_type=jnp.float32
    )
    term_rows[...] = term * scale
    count = dim // plane
    for order, out in enumerate(terms):
        chunk = place[1] ^ order
        out[...] = term_rows[pl.ds(pl.multiple_of(chunk * count, count), count), :].astype(jnp.bfloat16)


def split_groups(layout, refs):
    groups, start = [], 0
    for count in layout:
        groups.append(refs[start : start + count])
        start += count
    return groups, refs[start:]


def backward_kernel(
    inv_root, layout, targets, place, stats, both_queries, payload, grad_rows, *refs
):
    groups, rest = split_groups(layout, refs)
    count = 1 + max(out for out, _ in targets)
    outs, rest = rest[:count], rest[count:]
    both_grads = rest[-1]
    tile, dim = grad_rows.shape
    columns = payload.shape[1]
    both_tiles(place, grad_rows[...], payload[:, columns - dim :], both_grads)
    query_rows, out_grads = both_queries[...], both_grads[...]
    level, row_dot = stats[0:1, :], stats[1:2, :]
    along = (((1,), (1,)), ((), ()))
    query_grad = jnp.zeros((dim, 2 * tile), jnp.float32)
    for group, (target, first) in zip(groups, targets):
        out, tiles = outs[target], group[0].shape[0]
        keys, values = rows_of(group, 0), rows_of(group, 1)
        scores = lax.dot_general(keys, query_rows, along, preferred_element_type=jnp.float32)
        probability = jnp.exp(scores * inv_root - level)
        prob_grad = lax.dot_general(values, out_grads, along, preferred_element_type=jnp.float32)
        score_grad = (probability * (prob_grad - row_dot)).astype(jnp.bfloat16)
        shape = (tiles,) + out.shape[2:]
        key_grad = jnp.dot(score_grad, query_rows, preferred_element_type=jnp.float32) * inv_root
        value_grad = jnp.dot(
            probability.astype(jnp.bfloat16), out_grads, preferred_element_type=jnp.float32
        )
        out[first : first + tiles, 0] = key_grad.reshape(shape).astype(out.dtype)
        out[first : first + tiles, 1] = value_grad.reshape(shape).astype(out.dtype)
        query_grad = query_grad + lax.dot_general(
            keys, score_grad, (((0,), (0,)), ((), ())), preferred_element_type=jnp.float32
        )
    rest[0][...] = query_grad


def query_kernel(inv_root, place, query_grad, query_own, query_other, both_out):
    tile, dim = query_own.shape
    both_out[...] = query_grad[...].T * inv_root
    query_own[...] = both_out[pl.ds(pl.multiple_of(place[0] * tile, tile), tile), :]
    other = both_out[pl.ds(pl.multiple_of((1 - place[0]) * tile, tile), tile), :]
    other = other.astype(jnp.bfloat16)
    rows = query_other.shape[0]
    for block in range(tile // rows):
        query_other[:, block * dim : (block + 1) * dim] = other[block * rows : (block + 1) * rows]


def assemble_kernel(flipped, rows, place, part, *refs):
    rows_ref, done = refs[-2:]
    count, width = rows_ref.shape
    copies = []
    if flipped:
        query_own, _, whole, grad_query, sums = refs[:-2]
        dim, step = query_own.shape[1], part.shape[0] - count
        for block in range(width // dim):
            piece = part[count:, block * dim : (block + 1) * dim].astype(jnp.float32)
            span = slice(block * step, (block + 1) * step)
            sums[span, :] = (query_own[span, :] + piece).astype(jnp.bfloat16)
        copies.append(pltpu.make_async_copy(sums, grad_query, done.at[count // rows]))
        copies[-1].start()
    else:
        whole = refs[0]
    core = 1 - place[0] if flipped else place[0]
    columns = pl.ds(pl.multiple_of(core * width, width), width)
    for order in range(count // rows):
        span = pl.ds(pl.multiple_of((place[1] ^ order) * rows, rows), rows)
        rows_ref[span, :] = part[order * rows : (order + 1) * rows, :].astype(jnp.float32)
        copies.append(
            pltpu.make_async_copy(rows_ref.at[span, :], whole.at[span, columns], done.at[order])
        )
        copies[-1].start()
    for copy in copies:
        copy.wait()


def assemble(flipped, place, part, rows, shape, whole=None, query_own=None):
    anywhere = pl.BlockSpec(memory_space=pl.ANY)
    outs, out_specs, operands, in_specs = shape, anywhere, (place, part), [SMEM, VMEM]
    scratch = [
        pltpu.VMEM((shape.shape[0], part.shape[1]), jnp.float32),
        pltpu.SemaphoreType.DMA((shape.shape[0] // rows + flipped,)),
    ]
    if flipped:
        outs, out_specs = (shape, shaped(*query_own.shape)), (anywhere, anywhere)
        operands, in_specs = operands + (query_own, whole), in_specs + [VMEM, anywhere]
        scratch = [pltpu.VMEM(query_own.shape, jnp.bfloat16)] + scratch
    return pl.pallas_call(
        functools.partial(assemble_kernel, flipped, rows),
        out_shape=outs,
        in_specs=in_specs,
        out_specs=out_specs,
        scratch_shapes=scratch,
        input_output_aliases={3: 0} if flipped else {},
        compiler_params=PARAMS,
        cost_estimate=cost_of(10**10, 10**8),
    )(*operands)


def owner_kernel(own_grad, *refs):
    for k, out in enumerate(refs[-2:]):
        total = own_grad[k]
        for block in refs[:-2]:
            total = total + block[k].astype(jnp.float32)
        out[...] = total.astype(jnp.bfloat16)


def pack_kernel(*refs):
    start = 0
    for piece in refs[:-1]:
        refs[-1][start : start + piece.shape[0], :] = piece[...]
        start += piece.shape[0]


def combine_kernel(column, *refs):
    arrived, pieces = refs[: -column.shape[0]], refs[-column.shape[0] :]
    for k, piece in enumerate(pieces):
        total = column[k]
        for block in arrived:
            total = total + block[k].astype(jnp.float32)
        piece[...] = total.astype(piece.dtype)


def shaped(*shape, kind=jnp.bfloat16):
    return jax.ShapeDtypeStruct(shape, kind)


def kernel_call(kernel, operands, outs, scratch=(), cost=None):
    many = isinstance(outs, (list, tuple))
    return pl.pallas_call(
        kernel,
        out_shape=outs,
        in_specs=[SMEM] + [VMEM] * (len(operands) - 1),
        out_specs=[VMEM] * len(outs) if many else VMEM,
        scratch_shapes=list(scratch),
        compiler_params=PARAMS,
        cost_estimate=cost,
    )(*operands)


def cost_of(flops, moved):
    return pl.CostEstimate(flops=int(flops), bytes_accessed=int(moved), transcendentals=0)


PLANE_BITS = ((0, 0), (0, 1), (2, 0), (2, 1))


def sum_over_plane(terms):
    summed = terms[0].astype(jnp.float32)
    for term, bit in zip(terms[1:], PLANE_BITS[1:]):
        summed = summed + flip(term, ("frame", "width"), bit).astype(jnp.float32)
    return summed.astype(jnp.bfloat16)


def join_sum(part, query_own, query_other, place):
    plane = len(part)
    pieces = part + [query_other]
    part = pl.pallas_call(
        pack_kernel,
        out_shape=shaped(sum(p.shape[0] for p in pieces), pieces[0].shape[1]),
        in_specs=[VMEM] * len(pieces),
        out_specs=VMEM,
        compiler_params=PARAMS,
    )(*pieces)
    other = flip(part, ("frame",), (1,))
    rows = (part.shape[0] - query_other.shape[0]) // plane
    shape = shaped(plane * rows, 2 * part.shape[1], kind=jnp.float32)
    whole = assemble(False, place, part, rows, shape)
    return whole, lambda whole: assemble(True, place, other, rows, shape, whole, query_own)


def body(queries, key_vectors, value_vectors, out_weight, projected_grad):
    head_dim = queries.shape[-1]
    model_dim = out_weight.shape[1]
    half = model_dim // 2
    inv_root = 1.0 / math.sqrt(head_dim)
    extents = tuple(lax.axis_size(axis) for axis in AXES)
    assert extents[0] == 4
    small = extents[1:] == (4, 2)
    frame, height, width = (lax.axis_index(axis) for axis in AXES)
    core = frame % 2
    place = jnp.stack([core, (frame // 2) * 2 + width, height]).astype(jnp.int32)
    query_rows = queries.reshape(-1, head_dim)
    grads = projected_grad.reshape(-1, model_dim)
    tile = query_rows.shape[0]

    own = jnp.stack((key_vectors.reshape(tile, head_dim), value_vectors.reshape(tile, head_dim)))
    cross = [(2 * s + y, 2 * p + 1 - y) for s, p in ((2, 0), (1, 3)) for y in (0, 1)]

    if small:
        swap = [(0, 1), (1, 0)]
        tiles = fetch(own, "height")
        own_beside = lax.ppermute(own[None], "width", swap)
        others = jnp.stack(tiles)
        column = jnp.stack([own] + tiles)
        others, column, own_beside, query_rows_late = lax.optimization_barrier(
            (others, column, own_beside, query_rows)
        )
        others_beside = lax.ppermute(others, "width", swap)
        far = [
            lax.ppermute(column, "frame", [(2, 1), (1, 2)]),
            lax.ppermute(column, ("frame", "width"), cross),
        ]
        blocks = [column, own_beside, others_beside, *far]
        layout = (1, 1, 1, 2)
        targets = ((0, 0), (1, 0), (1, 1), (2, 0))
        column_tiles, kinds = 1 + others.shape[0], 3
    else:
        query_rows_late = query_rows
        column = jnp.stack([own] + fetch(own, "height"))
        beside = fetch(column, "width")
        everything = jnp.concatenate([column] + beside, axis=0)
        far = [
            lax.ppermute(everything[:, :, : tile // 2], "frame", [(2, 0), (1, 3)]),
            lax.ppermute(everything[:, :, tile // 2 :], "frame", [(2, 1), (1, 2)]),
        ]
        blocks = [column] + beside + far
        layout = (1,) * (1 + len(beside)) + (2,)
        targets = tuple((k, 0) for k in range(len(layout)))
        column_tiles, kinds = column.shape[0], len(layout)
    queries_other = flip(query_rows_late, ("frame",), (1,))
    payload, grads_half, grad_rows, both_queries = kernel_call(
        token_kernel,
        (place, query_rows, queries_other, grads, out_weight),
        (
            shaped(tile, half + head_dim),
            shaped(tile, half),
            shaped(tile, head_dim),
            shaped(2 * tile, head_dim),
        ),
        cost=cost_of(2 * tile * head_dim * model_dim, 4 * tile * model_dim),
    )
    grad_shapes = [(column_tiles, 2, tile, head_dim)] * (kinds - 1)
    grad_shapes.append((column_tiles, 2, tile, head_dim) if small else far[0].shape)
    key_count = sum(shape[0] * shape[2] for shape in grad_shapes)
    product = 2 * key_count * 2 * tile * head_dim
    moved = sum(b.size * 2 for b in blocks)

    def forward(operands, groups, carried):
        keys, start = 0, 0
        for count in groups:
            keys += operands[start].shape[0] * operands[start].shape[2]
            start += count
        return pl.pallas_call(
            functools.partial(forward_kernel, inv_root, groups, bool(carried)),
            out_shape=shaped(head_dim + STAT_ROWS, 2 * tile, kind=jnp.float32),
            in_specs=[VMEM] * (1 + len(operands) + len(carried)),
            out_specs=VMEM,
            scratch_shapes=[pltpu.VMEM((keys, 2 * tile), jnp.float32)],
            compiler_params=PARAMS,
            cost_estimate=cost_of(8 * keys * tile * head_dim, moved * keys // key_count),
        )(both_queries, *operands, *carried)

    partial = forward(blocks[:1], (1,), ())
    payload, partial, *blocks[1:] = lax.optimization_barrier((payload, partial, *blocks[1:]))
    payload = flip(payload, ("frame",), (1,))
    partial = forward(blocks[1:], layout[1:], (partial,))
    partial_other = flip(partial, ("frame",), (1,))
    plane = 4
    chunks = plane if small else 0
    merged = kernel_call(
        functools.partial(merge_kernel, 1.0 / float(math.prod(extents)), plane),
        (place, partial, partial_other, payload, grads_half, grad_rows),
        (
            shaped(STAT_ROWS, 2 * tile, kind=jnp.float32),
            shaped(tile, head_dim),
            *[shaped(head_dim // plane, half)] * chunks,
        ),
        scratch=(
            pltpu.VMEM((2 * tile, head_dim), jnp.bfloat16),
            pltpu.VMEM((2 * tile, head_dim), jnp.bfloat16),
            pltpu.VMEM((head_dim, half), jnp.float32),
        ),
        cost=cost_of(4 * tile * head_dim * half, 4 * tile * model_dim),
    )
    stats, attended, *terms = merged
    *near_grads, far_grad, query_grad = kernel_call(
        functools.partial(backward_kernel, inv_root, layout, targets),
        (place, stats, both_queries, payload, grad_rows, *blocks),
        (
            shaped(*grad_shapes[0], kind=jnp.float32),
            *[shaped(*shape) for shape in grad_shapes[1:]],
            shaped(head_dim, 2 * tile, kind=jnp.float32),
        ),
        scratch=(pltpu.VMEM((2 * tile, head_dim), jnp.bfloat16),),
        cost=cost_of(5 * product, 2 * moved),
    )
    if small:
        terms[0], query_grad = lax.optimization_barrier((terms[0], query_grad))
        part = sum_over_plane(terms)
        part, query_grad = lax.optimization_barrier((part, query_grad))
    query_own, query_other = kernel_call(
        functools.partial(query_kernel, inv_root),
        (place, query_grad),
        (
            shaped(tile, head_dim, kind=jnp.float32),
            shaped(tile * head_dim // half, half),
        ),
        scratch=(pltpu.VMEM((2 * tile, head_dim), jnp.float32),),
        cost=cost_of(10**10, 10**8),
    )
    if small:
        far_grad, query_own = lax.optimization_barrier((far_grad, query_own))
    back = (*near_grads, far_grad, query_own, query_other)
    if small:
        other = flip(part, ("height",), (1,))
        part = (part.astype(jnp.float32) + other.astype(jnp.float32)).astype(jnp.bfloat16)
        part, attended = lax.optimization_barrier((part, attended))
        other = flip(part, ("height",), (2,))
    else:
        weight_term = jnp.einsum("td,tm->dm", attended, grads, preferred_element_type=jnp.float32)
        grad_out_weight = lax.psum(weight_term, AXES) / float(math.prod(extents))
    projected = (
        jnp.dot(attended, out_weight, preferred_element_type=jnp.float32)
        .astype(jnp.bfloat16)
        .reshape(projected_grad.shape)
    )
    column_grad, *beside_grads, far_grad, query_own, query_other = back
    if small:
        arrived = [
            lax.ppermute(beside_grads[0], "width", [(0, 1), (1, 0)]),
            lax.ppermute(far_grad, "frame", [(1, 2), (2, 1)]),
            lax.ppermute(far_grad, ("frame", "width"), [(p, s) for s, p in cross]),
        ]
        other, projected = lax.optimization_barrier((other, projected))
        part = (part.astype(jnp.float32) + other.astype(jnp.float32)).astype(jnp.bfloat16)
        part, column_grad = lax.optimization_barrier((part, column_grad))
        part = [part] + [flip(part, ("frame", "width"), bit) for bit in PLANE_BITS[1:]]
        shape = column_grad.shape[1:]
        pieces = pl.pallas_call(
            combine_kernel,
            out_shape=[shaped(*shape, kind=jnp.float32)] + [shaped(*shape)] * (column_tiles - 1),
            in_specs=[VMEM] * 4,
            out_specs=[VMEM] * column_tiles,
            compiler_params=PARAMS,
        )(column_grad, *arrived)
        pieces = list(pieces)
    else:
        arrived = jnp.concatenate(
            (
                lax.ppermute(far_grad, "frame", [(0, 2), (3, 1)]),
                lax.ppermute(far_grad, "frame", [(1, 2), (2, 1)]),
            ),
            axis=2,
        ).astype(jnp.float32)
        pieces = [column_grad] + [b.astype(jnp.float32) for b in beside_grads]
        span = column_tiles
        pieces = [p + arrived[i * span : (i + 1) * span] for i, p in enumerate(pieces)]
        column_grad = give_back(pieces, "width")
        pieces = [column_grad[k] for k in range(column_tiles)]
    if small:
        whole, finish = join_sum(part, query_own, query_other, place)
        grad_out_weight, grad_query = finish(whole)
        grad_out_weight, pieces[0] = lax.optimization_barrier((grad_out_weight, pieces[0]))
    else:
        query_other = flip(query_other, ("frame",), (1,)).reshape(-1, half // head_dim, head_dim)
        query_other = query_other.transpose(1, 0, 2).reshape(tile, head_dim)
        grad_query = (query_own + query_other.astype(jnp.float32)).astype(jnp.bfloat16)
    operands = (pieces[0], *returned(pieces[1:], "height"))
    grad_key, grad_value = pl.pallas_call(
        owner_kernel,
        out_shape=[shaped(tile, head_dim)] * 2,
        in_specs=[VMEM] * len(operands),
        out_specs=[VMEM] * 2,
        compiler_params=PARAMS,
        cost_estimate=cost_of(10**10, 10**8),
    )(*operands)
    grad_key = grad_key.reshape(key_vectors.shape)
    grad_value = grad_value.reshape(value_vectors.shape)
    grad_query = grad_query.reshape(queries.shape)
    return (projected, grad_query, grad_key, grad_value, grad_out_weight)


def solution(mesh):
    tokens = P("frame", "height", "width", None)
    return jax.shard_map(
        body,
        mesh=mesh,
        in_specs=(tokens, tokens, tokens, P(), tokens),
        out_specs=(tokens, tokens, tokens, tokens, P()),
        check_vma=False,
    )
```

```python
import functools
import math

import jax
import jax.numpy as jnp
from jax import lax
from jax.experimental import pallas as pl
from jax.experimental.pallas import tpu as pltpu
from jax.sharding import PartitionSpec as P

AXES = ("frame", "height", "width")
VMEM = pl.BlockSpec(memory_space=pltpu.VMEM)
SMEM = pl.BlockSpec(memory_space=pltpu.SMEM)
PARAMS = pltpu.CompilerParams(vmem_limit_bytes=24 * 1024 * 1024)
STAT_ROWS = 8
FREE = pl.CostEstimate(flops=0, bytes_accessed=0, transcendentals=0)


def window_of(position, extent):
    span = min(3, extent)
    start = max(0, min(position - 1, extent - 3))
    return range(start, start + span)


def routes_of(extent):
    first = [(p ^ 1, p) for p in range(extent) if (p ^ 1) in window_of(p, extent)]
    if extent > 4:
        first = [(p + 1, p) for p in range(extent - 1)]
    wanted = [(s, p) for p in range(extent) for s in window_of(p, extent) if s != p]
    wanted.sort(key=lambda pair: (pair[0] ^ pair[1], pair))
    routes = [first]
    for pair in wanted:
        if pair in first:
            continue
        for route in routes[1:]:
            if all(pair[0] != s and pair[1] != p for s, p in route):
                route.append(pair)
                break
        else:
            routes.append([pair])
    return [route for route in routes if route]


def slots_of(extent):
    routes = routes_of(extent)
    arrivals = [[c for c, r in enumerate(routes) if any(q == p for _, q in r)] for p in range(extent)]
    return [[arrivals[p][k] for p in range(extent)] for k in range(min(3, extent) - 1)]


def chosen(options, choice, axis):
    value = options[choice[0]]
    position = lax.axis_index(axis)
    for option in sorted(set(choice)):
        if option != choice[0]:
            here = functools.reduce(
                jnp.logical_or, [position == p for p, c in enumerate(choice) if c == option]
            )
            value = jnp.where(here, options[option], value)
    return value


def fetch(block, axis):
    extent = lax.axis_size(axis)
    routes = routes_of(extent)
    arrived = [lax.ppermute(block, axis, route) for route in routes]
    tiles = []
    for slot in slots_of(extent):
        used = sorted(set(slot))
        reached = sum(len(routes[c]) for c in used)
        if reached == extent:
            tiles.append(functools.reduce(jnp.add, [arrived[c] for c in used]))
        else:
            tiles.append(chosen(arrived, slot, axis))
    return tiles


def returned(pieces, axis):
    extent = lax.axis_size(axis)
    slots = slots_of(extent)
    arrived = []
    order = (0, 2, 1) if extent == 4 else range(len(routes_of(extent)))
    for c, route in ((c, routes_of(extent)[c]) for c in order):
        holders = [next((k for k in range(len(slots)) if slots[k][p] == c), None) for p in range(extent)]
        used = sorted({k for k in holders if k is not None})
        choice = [k if k is not None else used[0] for k in holders]
        outgoing = chosen({k: pieces[k] for k in used}, choice, axis).astype(jnp.bfloat16)
        arrived.append(lax.ppermute(outgoing, axis, [(p, s) for s, p in route]))
    return arrived


def give_back(pieces, axis):
    arrived = returned(pieces[1:], axis)
    return functools.reduce(jnp.add, [pieces[0]] + [a.astype(jnp.float32) for a in arrived])


def flip(block, axes, bits):
    sizes = [lax.axis_size(axis) for axis in axes]
    route = []
    for flat in range(math.prod(sizes)):
        rest, target, scale = flat, 0, 1
        for size, bit in zip(reversed(sizes), reversed(bits)):
            target += ((rest % size) ^ bit) * scale
            rest //= size
            scale *= size
        route.append((flat, target))
    return lax.ppermute(block, axes, route)


def rows_of(refs, part):
    block = refs[0][:, part]
    for ref in refs[1:]:
        block = block + ref[:, part]
    return block.reshape(-1, block.shape[-1])


def token_kernel(
    place, queries, queries_other, grads, weight, payload, grads_half, grad_rows, both_queries
):
    half = grads_half.shape[1]
    product = lax.dot_general(
        grads[...], weight[...], (((1,), (1,)), ((), ())), preferred_element_type=jnp.float32
    ).astype(jnp.bfloat16)
    grad_rows[...] = product
    payload[:, half:] = product
    payload[:, :half] = grads[:, pl.ds(pl.multiple_of((1 - place[0]) * half, half), half)]
    grads_half[...] = grads[:, pl.ds(pl.multiple_of(place[0] * half, half), half)]
    both_tiles(place, queries[...], queries_other[...], both_queries)


def both_tiles(place, mine, theirs, both):
    tile = mine.shape[0]
    both[pl.ds(pl.multiple_of(place[0] * tile, tile), tile), :] = mine
    both[pl.ds(pl.multiple_of((1 - place[0]) * tile, tile), tile), :] = theirs


def forward_kernel(inv_root, layout, carried, both_queries, *refs):
    groups, rest = split_groups(layout, refs)
    partial, scores = rest[-2:]
    dim = both_queries.shape[1]
    query_rows = both_queries[...]
    top, start, spans = None, 0, []
    if carried:
        top = rest[0][dim : dim + 1, :]
    for group in groups:
        keys = rows_of(group, 0)
        piece = lax.dot_general(
            keys, query_rows, (((1,), (1,)), ((), ())), preferred_element_type=jnp.float32
        )
        scores[start : start + keys.shape[0], :] = piece
        spans.append((start, keys.shape[0]))
        start += keys.shape[0]
        piece_top = jnp.max(piece, axis=0, keepdims=True) * inv_root
        top = piece_top if top is None else jnp.maximum(top, piece_top)
    if carried:
        share = jnp.exp(rest[0][dim : dim + 1, :] - top)
        total = rest[0][dim + 1 : dim + 2, :] * share
        mixed = rest[0][:dim, :] * share
    else:
        total = jnp.zeros_like(top)
        mixed = jnp.zeros((dim, query_rows.shape[0]), jnp.float32)
    for group, (start, count) in zip(groups, spans):
        weights = jnp.exp(scores[start : start + count, :] * inv_root - top)
        total = total + jnp.sum(weights, axis=0, keepdims=True)
        mixed = mixed + lax.dot_general(
            rows_of(group, 1),
            weights.astype(jnp.bfloat16),
            (((0,), (0,)), ((), ())),
            preferred_element_type=jnp.float32,
        )
    partial[:dim, :] = mixed
    row = lax.broadcasted_iota(jnp.int32, (STAT_ROWS, query_rows.shape[0]), 0)
    partial[dim:, :] = jnp.where(row == 0, top, total)


def merge_kernel(scale, plane, place, mine, theirs, payload, grads_half, grad_rows, *refs):
    stats, attended_own, terms, both_attended, term_rows = (
        refs[0],
        refs[1],
        refs[2:-2],
        refs[-2],
        refs[-1],
    )
    tile, dim = grad_rows.shape
    half = grads_half.shape[1]
    top_a, top_b = mine[dim : dim + 1, :], theirs[dim : dim + 1, :]
    sum_a, sum_b = mine[dim + 1 : dim + 2, :], theirs[dim + 1 : dim + 2, :]
    top = jnp.maximum(top_a, top_b)
    share_a, share_b = jnp.exp(top_a - top), jnp.exp(top_b - top)
    total = share_a * sum_a + share_b * sum_b
    mixed = mine[:dim, :] * (share_a / total) + theirs[:dim, :] * (share_b / total)
    attended_t = mixed.astype(jnp.bfloat16).astype(jnp.float32)
    stats[:dim, :] = attended_t
    stats[dim:, :] = jnp.broadcast_to(top + jnp.log(total), (STAT_ROWS, mixed.shape[1]))
    both_attended[...] = attended_t.T.astype(jnp.bfloat16)
    rows_mine = both_attended[pl.ds(pl.multiple_of(place[0] * tile, tile), tile), :]
    rows_theirs = both_attended[pl.ds(pl.multiple_of((1 - place[0]) * tile, tile), tile), :]
    attended_own[...] = rows_mine
    if not terms:
        return
    contract = (((0,), (0,)), ((), ()))
    term = lax.dot_general(
        rows_mine, grads_half[...], contract, preferred_element_type=jnp.float32
    )
    term = term + lax.dot_general(
        rows_theirs, payload[:, :half], contract, preferred_element_type=jnp.float32
    )
    term_rows[...] = term * scale
    count = dim // plane
    for order, out in enumerate(terms):
        chunk = place[1] ^ order
        out[...] = term_rows[pl.ds(pl.multiple_of(chunk * count, count), count), :].astype(jnp.bfloat16)


def split_groups(layout, refs):
    groups, start = [], 0
    for count in layout:
        groups.append(refs[start : start + count])
        start += count
    return groups, refs[start:]


def backward_kernel(
    inv_root, layout, targets, place, stats, both_queries, payload, grad_rows, *refs
):
    groups, rest = split_groups(layout, refs)
    count = 1 + max(out for out, _ in targets)
    outs, rest = rest[:count], rest[count:]
    both_grads = rest[-1]
    tile, dim = grad_rows.shape
    columns = payload.shape[1]
    both_tiles(place, grad_rows[...], payload[:, columns - dim :], both_grads)
    query_rows, out_grads = both_queries[...], both_grads[...]
    level = stats[dim : dim + 1, :]
    row_dot = jnp.sum(out_grads.astype(jnp.float32).T * stats[:dim, :], axis=0, keepdims=True)
    along = (((1,), (1,)), ((), ()))
    query_grad = jnp.zeros((dim, 2 * tile), jnp.float32)
    for group, (target, first) in zip(groups, targets):
        out, tiles = outs[target], group[0].shape[0]
        keys, values = rows_of(group, 0), rows_of(group, 1)
        scores = lax.dot_general(keys, query_rows, along, preferred_element_type=jnp.float32)
        probability = jnp.exp(scores * inv_root - level)
        prob_grad = lax.dot_general(values, out_grads, along, preferred_element_type=jnp.float32)
        score_grad = (probability * (prob_grad - row_dot)).astype(jnp.bfloat16)
        shape = (tiles,) + out.shape[2:]
        key_grad = jnp.dot(score_grad, query_rows, preferred_element_type=jnp.float32) * inv_root
        value_grad = jnp.dot(
            probability.astype(jnp.bfloat16), out_grads, preferred_element_type=jnp.float32
        )
        out[first : first + tiles, 0] = key_grad.reshape(shape).astype(out.dtype)
        out[first : first + tiles, 1] = value_grad.reshape(shape).astype(out.dtype)
        query_grad = query_grad + lax.dot_general(
            keys, score_grad, (((0,), (0,)), ((), ())), preferred_element_type=jnp.float32
        )
    rest[0][...] = query_grad


def query_kernel(inv_root, place, query_grad, query_own, query_other, both_out):
    tile, dim = query_own.shape
    both_out[...] = query_grad[...].T * inv_root
    query_own[...] = both_out[pl.ds(pl.multiple_of(place[0] * tile, tile), tile), :]
    other = both_out[pl.ds(pl.multiple_of((1 - place[0]) * tile, tile), tile), :]
    other = other.astype(jnp.bfloat16)
    rows = query_other.shape[0]
    for block in range(tile // rows):
        query_other[:, block * dim : (block + 1) * dim] = other[block * rows : (block + 1) * rows]


def assemble_kernel(flipped, rows, place, part, *refs):
    rows_ref, done = refs[-2:]
    count, width = rows_ref.shape
    copies = []
    if flipped:
        query_own, _, whole, grad_query, sums = refs[:-2]
        dim, step = query_own.shape[1], part.shape[0] - count
        for block in range(width // dim):
            piece = part[count:, block * dim : (block + 1) * dim].astype(jnp.float32)
            span = slice(block * step, (block + 1) * step)
            sums[span, :] = (query_own[span, :] + piece).astype(jnp.bfloat16)
        copies.append(pltpu.make_async_copy(sums, grad_query, done.at[count // rows]))
        copies[-1].start()
    else:
        whole = refs[0]
    core = 1 - place[0] if flipped else place[0]
    columns = pl.ds(pl.multiple_of(core * width, width), width)
    for order in range(count // rows):
        span = pl.ds(pl.multiple_of((place[1] ^ order) * rows, rows), rows)
        rows_ref[span, :] = part[order * rows : (order + 1) * rows, :].astype(jnp.float32)
        copies.append(
            pltpu.make_async_copy(rows_ref.at[span, :], whole.at[span, columns], done.at[order])
        )
        copies[-1].start()
    for copy in copies:
        copy.wait()


def assemble(flipped, place, part, rows, shape, whole=None, query_own=None):
    anywhere = pl.BlockSpec(memory_space=pl.ANY)
    outs, out_specs, operands, in_specs = shape, anywhere, (place, part), [SMEM, VMEM]
    scratch = [
        pltpu.VMEM((shape.shape[0], part.shape[1]), jnp.float32),
        pltpu.SemaphoreType.DMA((shape.shape[0] // rows + flipped,)),
    ]
    if flipped:
        outs, out_specs = (shape, shaped(*query_own.shape)), (anywhere, anywhere)
        operands, in_specs = operands + (query_own, whole), in_specs + [VMEM, anywhere]
        scratch = [pltpu.VMEM(query_own.shape, jnp.bfloat16)] + scratch
    return pl.pallas_call(
        functools.partial(assemble_kernel, flipped, rows),
        out_shape=outs,
        in_specs=in_specs,
        out_specs=out_specs,
        scratch_shapes=scratch,
        input_output_aliases={3: 0} if flipped else {},
        compiler_params=PARAMS,
        cost_estimate=cost_of(10**10, 10**8),
    )(*operands)


def owner_kernel(own_grad, *refs):
    for k, out in enumerate(refs[-2:]):
        total = own_grad[k]
        for block in refs[:-2]:
            total = total + block[k].astype(jnp.float32)
        out[...] = total.astype(jnp.bfloat16)


def pack_kernel(*refs):
    end = refs[-1].shape[0]
    for piece in refs[:-1]:
        refs[-1][end - piece.shape[0] : end, :] = piece[...]
        end -= piece.shape[0]


def combine_kernel(column, *refs):
    arrived, pieces = refs[: -column.shape[0]], refs[-column.shape[0] :]
    for k, piece in enumerate(pieces):
        total = column[k]
        for block in arrived:
            total = total + block[k].astype(jnp.float32)
        piece[...] = total.astype(piece.dtype)


def shaped(*shape, kind=jnp.bfloat16):
    return jax.ShapeDtypeStruct(shape, kind)


def kernel_call(kernel, operands, outs, scratch=(), cost=None):
    many = isinstance(outs, (list, tuple))
    return pl.pallas_call(
        kernel,
        out_shape=outs,
        in_specs=[SMEM] + [VMEM] * (len(operands) - 1),
        out_specs=[VMEM] * len(outs) if many else VMEM,
        scratch_shapes=list(scratch),
        compiler_params=PARAMS,
        cost_estimate=cost,
    )(*operands)


def cost_of(flops, moved):
    return pl.CostEstimate(flops=int(flops), bytes_accessed=int(moved), transcendentals=0)


PLANE_BITS = ((0, 0), (0, 1), (2, 0), (2, 1))


def sum_over_plane(terms):
    summed = terms[0].astype(jnp.float32)
    for term, bit in zip(terms[1:], PLANE_BITS[1:]):
        summed = summed + flip(term, ("frame", "width"), bit).astype(jnp.float32)
    return summed.astype(jnp.bfloat16)


def join_sum(part, query_own, query_other, place):
    plane = len(part)
    pieces = [query_other] + part[::-1]
    part = pl.pallas_call(
        pack_kernel,
        out_shape=shaped(sum(p.shape[0] for p in pieces), pieces[0].shape[1]),
        in_specs=[VMEM] * len(pieces),
        out_specs=VMEM,
        compiler_params=PARAMS,
    )(*pieces)
    other = flip(part, ("frame",), (1,))
    rows = (part.shape[0] - query_other.shape[0]) // plane
    shape = shaped(plane * rows, 2 * part.shape[1], kind=jnp.float32)
    whole = assemble(False, place, part, rows, shape)
    return whole, lambda whole: assemble(True, place, other, rows, shape, whole, query_own)


def body(queries, key_vectors, value_vectors, out_weight, projected_grad):
    head_dim = queries.shape[-1]
    model_dim = out_weight.shape[1]
    half = model_dim // 2
    inv_root = 1.0 / math.sqrt(head_dim)
    extents = tuple(lax.axis_size(axis) for axis in AXES)
    assert extents[0] == 4
    small = extents[1:] == (4, 2)
    frame, height, width = (lax.axis_index(axis) for axis in AXES)
    core = frame % 2
    place = jnp.stack([core, (frame // 2) * 2 + width, height]).astype(jnp.int32)
    query_rows = queries.reshape(-1, head_dim)
    grads = projected_grad.reshape(-1, model_dim)
    tile = query_rows.shape[0]

    own = jnp.stack((key_vectors.reshape(tile, head_dim), value_vectors.reshape(tile, head_dim)))
    cross = [(2 * s + y, 2 * p + 1 - y) for s, p in ((2, 0), (1, 3)) for y in (0, 1)]

    if small:
        swap = [(0, 1), (1, 0)]
        tiles = fetch(own, "height")
        own_beside = lax.ppermute(own[None], "width", swap)
        others = jnp.stack(tiles)
        column = jnp.stack([own] + tiles)
        others, column, own_beside, query_rows_late = lax.optimization_barrier(
            (others, column, own_beside, query_rows)
        )
        others_beside = lax.ppermute(others, "width", swap)
        far = [
            lax.ppermute(column, "frame", [(2, 1), (1, 2)]),
            lax.ppermute(column, ("frame", "width"), cross),
        ]
        blocks = [column, own_beside, others_beside, *far]
        layout = (1, 1, 1, 2)
        targets = ((0, 0), (1, 0), (1, 1), (2, 0))
        column_tiles, kinds = 1 + others.shape[0], 3
    else:
        query_rows_late = query_rows
        column = jnp.stack([own] + fetch(own, "height"))
        beside = fetch(column, "width")
        everything = jnp.concatenate([column] + beside, axis=0)
        far = [
            lax.ppermute(everything[:, :, : tile // 2], "frame", [(2, 0), (1, 3)]),
            lax.ppermute(everything[:, :, tile // 2 :], "frame", [(2, 1), (1, 2)]),
        ]
        blocks = [column] + beside + far
        layout = (1,) * (1 + len(beside)) + (2,)
        targets = tuple((k, 0) for k in range(len(layout)))
        column_tiles, kinds = column.shape[0], len(layout)
    queries_other = flip(query_rows_late, ("frame",), (1,))
    payload, grads_half, grad_rows, both_queries = kernel_call(
        token_kernel,
        (place, query_rows, queries_other, grads, out_weight),
        (
            shaped(tile, half + head_dim),
            shaped(tile, half),
            shaped(tile, head_dim),
            shaped(2 * tile, head_dim),
        ),
        cost=cost_of(2 * tile * head_dim * model_dim, 4 * tile * model_dim),
    )
    grad_shapes = [(column_tiles, 2, tile, head_dim)] * (kinds - 1)
    grad_shapes.append((column_tiles, 2, tile, head_dim) if small else far[0].shape)
    key_count = sum(shape[0] * shape[2] for shape in grad_shapes)
    product = 2 * key_count * 2 * tile * head_dim
    moved = sum(b.size * 2 for b in blocks)

    def forward(operands, groups, carried):
        keys, start = 0, 0
        for count in groups:
            keys += operands[start].shape[0] * operands[start].shape[2]
            start += count
        return pl.pallas_call(
            functools.partial(forward_kernel, inv_root, groups, bool(carried)),
            out_shape=shaped(head_dim + STAT_ROWS, 2 * tile, kind=jnp.float32),
            in_specs=[VMEM] * (1 + len(operands) + len(carried)),
            out_specs=VMEM,
            scratch_shapes=[pltpu.VMEM((keys, 2 * tile), jnp.float32)],
            compiler_params=PARAMS,
            cost_estimate=cost_of(8 * keys * tile * head_dim, moved * keys // key_count),
        )(both_queries, *operands, *carried)

    partial = forward(blocks[:1], (1,), ())
    payload, partial, *blocks[1:] = lax.optimization_barrier((payload, partial, *blocks[1:]))
    payload = flip(payload, ("frame",), (1,))
    partial = forward(blocks[1:], layout[1:], (partial,))
    partial_other = flip(partial, ("frame",), (1,))
    plane = 4
    chunks = plane if small else 0
    merged = kernel_call(
        functools.partial(merge_kernel, 1.0 / float(math.prod(extents)), plane),
        (place, partial, partial_other, payload, grads_half, grad_rows),
        (
            shaped(head_dim + STAT_ROWS, 2 * tile, kind=jnp.float32),
            shaped(tile, head_dim),
            *[shaped(head_dim // plane, half)] * chunks,
        ),
        scratch=(
            pltpu.VMEM((2 * tile, head_dim), jnp.bfloat16),
            pltpu.VMEM((head_dim, half), jnp.float32),
        ),
        cost=cost_of(4 * tile * head_dim * half, 4 * tile * model_dim),
    )
    stats, attended, *terms = merged
    *near_grads, far_grad, query_grad = kernel_call(
        functools.partial(backward_kernel, inv_root, layout, targets),
        (place, stats, both_queries, payload, grad_rows, *blocks),
        (
            shaped(*grad_shapes[0], kind=jnp.float32),
            *[shaped(*shape) for shape in grad_shapes[1:]],
            shaped(head_dim, 2 * tile, kind=jnp.float32),
        ),
        scratch=(pltpu.VMEM((2 * tile, head_dim), jnp.bfloat16),),
        cost=cost_of(5 * product, 2 * moved),
    )
    if small:
        terms[0], query_grad = lax.optimization_barrier((terms[0], query_grad))
        part = sum_over_plane(terms)
        part, query_grad = lax.optimization_barrier((part, query_grad))
    query_own, query_other = kernel_call(
        functools.partial(query_kernel, inv_root),
        (place, query_grad),
        (
            shaped(tile, head_dim, kind=jnp.float32),
            shaped(tile * head_dim // half, half),
        ),
        scratch=(pltpu.VMEM((2 * tile, head_dim), jnp.float32),),
        cost=cost_of(10**10, 10**8),
    )
    if small:
        far_grad, query_own = lax.optimization_barrier((far_grad, query_own))
    back = (*near_grads, far_grad, query_own, query_other)
    if small:
        other = flip(part, ("height",), (1,))
        part = (part.astype(jnp.float32) + other.astype(jnp.float32)).astype(jnp.bfloat16)
        part, attended = lax.optimization_barrier((part, attended))
        other = flip(part, ("height",), (2,))
    else:
        weight_term = jnp.einsum("td,tm->dm", attended, grads, preferred_element_type=jnp.float32)
        grad_out_weight = lax.psum(weight_term, AXES) / float(math.prod(extents))
    projected = (
        jnp.dot(attended, out_weight, preferred_element_type=jnp.float32)
        .astype(jnp.bfloat16)
        .reshape(projected_grad.shape)
    )
    column_grad, *beside_grads, far_grad, query_own, query_other = back
    if small:
        arrived = [
            lax.ppermute(beside_grads[0], "width", [(0, 1), (1, 0)]),
            lax.ppermute(far_grad, "frame", [(1, 2), (2, 1)]),
            lax.ppermute(far_grad, ("frame", "width"), [(p, s) for s, p in cross]),
        ]
        other, projected = lax.optimization_barrier((other, projected))
        part = (part.astype(jnp.float32) + other.astype(jnp.float32)).astype(jnp.bfloat16)
        part, column_grad = lax.optimization_barrier((part, column_grad))
        part = [part] + [flip(part, ("frame", "width"), bit) for bit in PLANE_BITS[1:]]
        shape = column_grad.shape[1:]
        pieces = pl.pallas_call(
            combine_kernel,
            out_shape=[shaped(*shape, kind=jnp.float32)] + [shaped(*shape)] * (column_tiles - 1),
            in_specs=[VMEM] * 4,
            out_specs=[VMEM] * column_tiles,
            compiler_params=PARAMS,
        )(column_grad, *arrived)
        pieces = list(pieces)
    else:
        arrived = jnp.concatenate(
            (
                lax.ppermute(far_grad, "frame", [(0, 2), (3, 1)]),
                lax.ppermute(far_grad, "frame", [(1, 2), (2, 1)]),
            ),
            axis=2,
        ).astype(jnp.float32)
        pieces = [column_grad] + [b.astype(jnp.float32) for b in beside_grads]
        span = column_tiles
        pieces = [p + arrived[i * span : (i + 1) * span] for i, p in enumerate(pieces)]
        column_grad = give_back(pieces, "width")
        pieces = [column_grad[k] for k in range(column_tiles)]
    if small:
        whole, finish = join_sum(part, query_own, query_other, place)
        grad_out_weight, grad_query = finish(whole)
        grad_out_weight, pieces[0] = lax.optimization_barrier((grad_out_weight, pieces[0]))
    else:
        query_other = flip(query_other, ("frame",), (1,)).reshape(-1, half // head_dim, head_dim)
        query_other = query_other.transpose(1, 0, 2).reshape(tile, head_dim)
        grad_query = (query_own + query_other.astype(jnp.float32)).astype(jnp.bfloat16)
    operands = (pieces[0], *returned(pieces[1:], "height"))
    grad_key, grad_value = pl.pallas_call(
        owner_kernel,
        out_shape=[shaped(tile, head_dim)] * 2,
        in_specs=[VMEM] * len(operands),
        out_specs=[VMEM] * 2,
        compiler_params=PARAMS,
        cost_estimate=cost_of(10**10, 10**8),
    )(*operands)
    grad_key = grad_key.reshape(key_vectors.shape)
    grad_value = grad_value.reshape(value_vectors.shape)
    grad_query = grad_query.reshape(queries.shape)
    return (projected, grad_query, grad_key, grad_value, grad_out_weight)


def solution(mesh):
    tokens = P("frame", "height", "width", None)
    return jax.shard_map(
        body,
        mesh=mesh,
        in_specs=(tokens, tokens, tokens, P(), tokens),
        out_specs=(tokens, tokens, tokens, tokens, P()),
        check_vma=False,
    )
```

```python
import functools
import math

import jax
import jax.numpy as jnp
from jax import lax
from jax.experimental import pallas as pl
from jax.experimental.pallas import tpu as pltpu
from jax.sharding import PartitionSpec as P

AXES = ("frame", "height", "width")
VMEM = pl.BlockSpec(memory_space=pltpu.VMEM)
SMEM = pl.BlockSpec(memory_space=pltpu.SMEM)
PARAMS = pltpu.CompilerParams(vmem_limit_bytes=24 * 1024 * 1024)
STAT_ROWS = 8
FREE = pl.CostEstimate(flops=0, bytes_accessed=0, transcendentals=0)


def window_of(position, extent):
    span = min(3, extent)
    start = max(0, min(position - 1, extent - 3))
    return range(start, start + span)


def routes_of(extent):
    first = [(p ^ 1, p) for p in range(extent) if (p ^ 1) in window_of(p, extent)]
    if extent > 4:
        first = [(p + 1, p) for p in range(extent - 1)]
    wanted = [(s, p) for p in range(extent) for s in window_of(p, extent) if s != p]
    wanted.sort(key=lambda pair: (pair[0] ^ pair[1], pair))
    routes = [first]
    for pair in wanted:
        if pair in first:
            continue
        for route in routes[1:]:
            if all(pair[0] != s and pair[1] != p for s, p in route):
                route.append(pair)
                break
        else:
            routes.append([pair])
    return [route for route in routes if route]


def slots_of(extent):
    routes = routes_of(extent)
    arrivals = [[c for c, r in enumerate(routes) if any(q == p for _, q in r)] for p in range(extent)]
    return [[arrivals[p][k] for p in range(extent)] for k in range(min(3, extent) - 1)]


def chosen(options, choice, axis):
    value = options[choice[0]]
    position = lax.axis_index(axis)
    for option in sorted(set(choice)):
        if option != choice[0]:
            here = functools.reduce(
                jnp.logical_or, [position == p for p, c in enumerate(choice) if c == option]
            )
            value = jnp.where(here, options[option], value)
    return value


def fetch(block, axis):
    extent = lax.axis_size(axis)
    routes = routes_of(extent)
    arrived = [lax.ppermute(block, axis, route) for route in routes]
    tiles = []
    for slot in slots_of(extent):
        used = sorted(set(slot))
        reached = sum(len(routes[c]) for c in used)
        if reached == extent:
            tiles.append(functools.reduce(jnp.add, [arrived[c] for c in used]))
        else:
            tiles.append(chosen(arrived, slot, axis))
    return tiles


def returned(pieces, axis):
    extent = lax.axis_size(axis)
    slots = slots_of(extent)
    arrived = []
    order = (0, 2, 1) if extent == 4 else range(len(routes_of(extent)))
    for c, route in ((c, routes_of(extent)[c]) for c in order):
        holders = [next((k for k in range(len(slots)) if slots[k][p] == c), None) for p in range(extent)]
        used = sorted({k for k in holders if k is not None})
        choice = [k if k is not None else used[0] for k in holders]
        outgoing = chosen({k: pieces[k] for k in used}, choice, axis).astype(jnp.bfloat16)
        arrived.append(lax.ppermute(outgoing, axis, [(p, s) for s, p in route]))
    return arrived


def give_back(pieces, axis):
    arrived = returned(pieces[1:], axis)
    return functools.reduce(jnp.add, [pieces[0]] + [a.astype(jnp.float32) for a in arrived])


def flip(block, axes, bits):
    sizes = [lax.axis_size(axis) for axis in axes]
    route = []
    for flat in range(math.prod(sizes)):
        rest, target, scale = flat, 0, 1
        for size, bit in zip(reversed(sizes), reversed(bits)):
            target += ((rest % size) ^ bit) * scale
            rest //= size
            scale *= size
        route.append((flat, target))
    return lax.ppermute(block, axes, route)


def rows_of(refs, part):
    block = refs[0][:, part]
    for ref in refs[1:]:
        block = block + ref[:, part]
    return block.reshape(-1, block.shape[-1])


def token_kernel(
    place, queries, queries_other, grads, weight, payload, grads_half, grad_rows, both_queries
):
    half = grads_half.shape[1]
    product = lax.dot_general(
        grads[...], weight[...], (((1,), (1,)), ((), ())), preferred_element_type=jnp.float32
    ).astype(jnp.bfloat16)
    grad_rows[...] = product
    payload[:, half:] = product
    payload[:, :half] = grads[:, pl.ds(pl.multiple_of((1 - place[0]) * half, half), half)]
    grads_half[...] = grads[:, pl.ds(pl.multiple_of(place[0] * half, half), half)]
    both_tiles(place, queries[...], queries_other[...], both_queries)


def both_tiles(place, mine, theirs, both):
    tile = mine.shape[0]
    both[pl.ds(pl.multiple_of(place[0] * tile, tile), tile), :] = mine
    both[pl.ds(pl.multiple_of((1 - place[0]) * tile, tile), tile), :] = theirs


def forward_kernel(inv_root, layout, carried, both_queries, *refs):
    groups, rest = split_groups(layout, refs)
    partial, scores = rest[-2:]
    dim = both_queries.shape[1]
    query_rows = both_queries[...]
    top, start, spans = None, 0, []
    if carried:
        top = rest[0][dim : dim + 1, :]
    for group in groups:
        keys = rows_of(group, 0)
        piece = lax.dot_general(
            keys, query_rows, (((1,), (1,)), ((), ())), preferred_element_type=jnp.float32
        )
        scores[start : start + keys.shape[0], :] = piece
        spans.append((start, keys.shape[0]))
        start += keys.shape[0]
        piece_top = jnp.max(piece, axis=0, keepdims=True) * inv_root
        top = piece_top if top is None else jnp.maximum(top, piece_top)
    if carried:
        share = jnp.exp(rest[0][dim : dim + 1, :] - top)
        total = rest[0][dim + 1 : dim + 2, :] * share
        mixed = rest[0][:dim, :] * share
    else:
        total = jnp.zeros_like(top)
        mixed = jnp.zeros((dim, query_rows.shape[0]), jnp.float32)
    for group, (start, count) in zip(groups, spans):
        weights = jnp.exp(scores[start : start + count, :] * inv_root - top)
        total = total + jnp.sum(weights, axis=0, keepdims=True)
        mixed = mixed + lax.dot_general(
            rows_of(group, 1),
            weights.astype(jnp.bfloat16),
            (((0,), (0,)), ((), ())),
            preferred_element_type=jnp.float32,
        )
    partial[:dim, :] = mixed
    row = lax.broadcasted_iota(jnp.int32, (STAT_ROWS, query_rows.shape[0]), 0)
    partial[dim:, :] = jnp.where(row == 0, top, total)


def merge_kernel(scale, plane, place, mine, theirs, payload, grads_half, grad_rows, *refs):
    stats, attended_own, terms, both_grads, both_attended, term_rows = (
        refs[0],
        refs[1],
        refs[2:-3],
        refs[-3],
        refs[-2],
        refs[-1],
    )
    tile, dim = grad_rows.shape
    half = grads_half.shape[1]
    top_a, top_b = mine[dim : dim + 1, :], theirs[dim : dim + 1, :]
    sum_a, sum_b = mine[dim + 1 : dim + 2, :], theirs[dim + 1 : dim + 2, :]
    top = jnp.maximum(top_a, top_b)
    share_a, share_b = jnp.exp(top_a - top), jnp.exp(top_b - top)
    total = share_a * sum_a + share_b * sum_b
    mixed = mine[:dim, :] * (share_a / total) + theirs[:dim, :] * (share_b / total)
    attended_t = mixed.astype(jnp.bfloat16).astype(jnp.float32)
    both_tiles(place, grad_rows[...], payload[:, half:], both_grads)
    row_dot = jnp.sum(both_grads[...].astype(jnp.float32).T * attended_t, axis=0, keepdims=True)
    row = lax.broadcasted_iota(jnp.int32, (STAT_ROWS, mixed.shape[1]), 0)
    stats[...] = jnp.where(row == 0, top + jnp.log(total), row_dot)
    both_attended[...] = attended_t.T.astype(jnp.bfloat16)
    rows_mine = both_attended[pl.ds(pl.multiple_of(place[0] * tile, tile), tile), :]
    rows_theirs = both_attended[pl.ds(pl.multiple_of((1 - place[0]) * tile, tile), tile), :]
    attended_own[...] = rows_mine
    if not terms:
        return
    contract = (((0,), (0,)), ((), ()))
    term = lax.dot_general(
        rows_mine, grads_half[...], contract, preferred_element_type=jnp.float32
    )
    term = term + lax.dot_general(
        rows_theirs, payload[:, :half], contract, preferred_element_type=jnp.float32
    )
    term_rows[...] = term * scale
    count = dim // plane
    for order, out in enumerate(terms):
        chunk = place[1] ^ order
        out[...] = term_rows[pl.ds(pl.multiple_of(chunk * count, count), count), :].astype(jnp.bfloat16)


def split_groups(layout, refs):
    groups, start = [], 0
    for count in layout:
        groups.append(refs[start : start + count])
        start += count
    return groups, refs[start:]


def backward_kernel(
    inv_root, layout, targets, place, stats, both_queries, payload, grad_rows, *refs
):
    groups, rest = split_groups(layout, refs)
    count = 1 + max(out for out, _ in targets)
    outs, rest = rest[:count], rest[count:]
    both_grads = rest[-1]
    tile, dim = grad_rows.shape
    columns = payload.shape[1]
    both_tiles(place, grad_rows[...], payload[:, columns - dim :], both_grads)
    query_rows, out_grads = both_queries[...], both_grads[...]
    level, row_dot = stats[0:1, :], stats[1:2, :]
    along = (((1,), (1,)), ((), ()))
    query_grad = jnp.zeros((dim, 2 * tile), jnp.float32)
    for group, (target, first) in zip(groups, targets):
        out, tiles = outs[target], group[0].shape[0]
        keys, values = rows_of(group, 0), rows_of(group, 1)
        scores = lax.dot_general(keys, query_rows, along, preferred_element_type=jnp.float32)
        probability = jnp.exp(scores * inv_root - level)
        prob_grad = lax.dot_general(values, out_grads, along, preferred_element_type=jnp.float32)
        score_grad = (probability * (prob_grad - row_dot)).astype(jnp.bfloat16)
        shape = (tiles,) + out.shape[2:]
        key_grad = jnp.dot(score_grad, query_rows, preferred_element_type=jnp.float32) * inv_root
        value_grad = jnp.dot(
            probability.astype(jnp.bfloat16), out_grads, preferred_element_type=jnp.float32
        )
        out[first : first + tiles, 0] = key_grad.reshape(shape).astype(out.dtype)
        out[first : first + tiles, 1] = value_grad.reshape(shape).astype(out.dtype)
        query_grad = query_grad + lax.dot_general(
            keys, score_grad, (((0,), (0,)), ((), ())), preferred_element_type=jnp.float32
        )
    rest[0][...] = query_grad


def query_kernel(inv_root, place, query_grad, query_own, query_other, both_out):
    tile, dim = query_own.shape
    both_out[...] = query_grad[...].T * inv_root
    query_own[...] = both_out[pl.ds(pl.multiple_of(place[0] * tile, tile), tile), :]
    other = both_out[pl.ds(pl.multiple_of((1 - place[0]) * tile, tile), tile), :]
    other = other.astype(jnp.bfloat16)
    rows = query_other.shape[0]
    for block in range(tile // rows):
        query_other[:, block * dim : (block + 1) * dim] = other[block * rows : (block + 1) * rows]


def assemble_kernel(flipped, rows, place, part, *refs):
    rows_ref, done = refs[-2:]
    count, width = rows_ref.shape
    copies = []
    if flipped:
        query_own, _, whole, grad_query, sums = refs[:-2]
        dim, step = query_own.shape[1], part.shape[0] - count
        for block in range(width // dim):
            piece = part[count:, block * dim : (block + 1) * dim].astype(jnp.float32)
            span = slice(block * step, (block + 1) * step)
            sums[span, :] = (query_own[span, :] + piece).astype(jnp.bfloat16)
        copies.append(pltpu.make_async_copy(sums, grad_query, done.at[count // rows]))
        copies[-1].start()
    else:
        whole = refs[0]
    core = 1 - place[0] if flipped else place[0]
    columns = pl.ds(pl.multiple_of(core * width, width), width)
    for order in range(count // rows):
        span = pl.ds(pl.multiple_of((place[1] ^ order) * rows, rows), rows)
        rows_ref[span, :] = part[order * rows : (order + 1) * rows, :].astype(jnp.float32)
        copies.append(
            pltpu.make_async_copy(rows_ref.at[span, :], whole.at[span, columns], done.at[order])
        )
        copies[-1].start()
    for copy in copies:
        copy.wait()


def assemble(flipped, place, part, rows, shape, whole=None, query_own=None):
    anywhere = pl.BlockSpec(memory_space=pl.ANY)
    outs, out_specs, operands, in_specs = shape, anywhere, (place, part), [SMEM, VMEM]
    scratch = [
        pltpu.VMEM((shape.shape[0], part.shape[1]), jnp.float32),
        pltpu.SemaphoreType.DMA((shape.shape[0] // rows + flipped,)),
    ]
    if flipped:
        outs, out_specs = (shape, shaped(*query_own.shape)), (anywhere, anywhere)
        operands, in_specs = operands + (query_own, whole), in_specs + [VMEM, anywhere]
        scratch = [pltpu.VMEM(query_own.shape, jnp.bfloat16)] + scratch
    return pl.pallas_call(
        functools.partial(assemble_kernel, flipped, rows),
        out_shape=outs,
        in_specs=in_specs,
        out_specs=out_specs,
        scratch_shapes=scratch,
        input_output_aliases={3: 0} if flipped else {},
        compiler_params=PARAMS,
        cost_estimate=cost_of(10**10, 10**8),
    )(*operands)


def owner_kernel(own_grad, *refs):
    for k, out in enumerate(refs[-2:]):
        total = own_grad[k]
        for block in refs[:-2]:
            total = total + block[k].astype(jnp.float32)
        out[...] = total.astype(jnp.bfloat16)


def pack_kernel(*refs):
    start = 0
    for piece in refs[:-1]:
        refs[-1][start : start + piece.shape[0], :] = piece[...]
        start += piece.shape[0]


def combine_kernel(column, *refs):
    arrived, pieces = refs[: -column.shape[0]], refs[-column.shape[0] :]
    for k, piece in enumerate(pieces):
        total = column[k]
        for block in arrived:
            total = total + block[k].astype(jnp.float32)
        piece[...] = total.astype(piece.dtype)


def shaped(*shape, kind=jnp.bfloat16):
    return jax.ShapeDtypeStruct(shape, kind)


def kernel_call(kernel, operands, outs, scratch=(), cost=None):
    many = isinstance(outs, (list, tuple))
    return pl.pallas_call(
        kernel,
        out_shape=outs,
        in_specs=[SMEM] + [VMEM] * (len(operands) - 1),
        out_specs=[VMEM] * len(outs) if many else VMEM,
        scratch_shapes=list(scratch),
        compiler_params=PARAMS,
        cost_estimate=cost,
    )(*operands)


def cost_of(flops, moved):
    return pl.CostEstimate(flops=int(flops), bytes_accessed=int(moved), transcendentals=0)


PLANE_BITS = ((0, 0), (0, 1), (2, 0), (2, 1))


def sum_over_plane(terms):
    summed = terms[0].astype(jnp.float32)
    for term, bit in zip(terms[1:], PLANE_BITS[1:]):
        summed = summed + flip(term, ("frame", "width"), bit).astype(jnp.float32)
    return summed.astype(jnp.bfloat16)


def join_sum(part, query_own, query_other, place):
    plane = len(part)
    pieces = part + [query_other]
    part = pl.pallas_call(
        pack_kernel,
        out_shape=shaped(sum(p.shape[0] for p in pieces), pieces[0].shape[1]),
        in_specs=[VMEM] * len(pieces),
        out_specs=VMEM,
        compiler_params=PARAMS,
    )(*pieces)
    other = flip(part, ("frame",), (1,))
    rows = (part.shape[0] - query_other.shape[0]) // plane
    shape = shaped(plane * rows, 2 * part.shape[1], kind=jnp.float32)
    whole = assemble(False, place, part, rows, shape)
    return whole, lambda whole: assemble(True, place, other, rows, shape, whole, query_own)


def body(queries, key_vectors, value_vectors, out_weight, projected_grad):
    head_dim = queries.shape[-1]
    model_dim = out_weight.shape[1]
    half = model_dim // 2
    inv_root = 1.0 / math.sqrt(head_dim)
    extents = tuple(lax.axis_size(axis) for axis in AXES)
    assert extents[0] == 4
    small = extents[1:] == (4, 2)
    frame, height, width = (lax.axis_index(axis) for axis in AXES)
    core = frame % 2
    place = jnp.stack([core, (frame // 2) * 2 + width, height]).astype(jnp.int32)
    query_rows = queries.reshape(-1, head_dim)
    grads = projected_grad.reshape(-1, model_dim)
    tile = query_rows.shape[0]

    own = jnp.stack((key_vectors.reshape(tile, head_dim), value_vectors.reshape(tile, head_dim)))
    cross = [(2 * s + y, 2 * p + 1 - y) for s, p in ((2, 0), (1, 3)) for y in (0, 1)]

    if small:
        swap = [(0, 1), (1, 0)]
        tiles = fetch(own, "height")
        own_beside = lax.ppermute(own[None], "width", swap)
        others = jnp.stack(tiles)
        column = jnp.stack([own] + tiles)
        others, column, own_beside, query_rows_late = lax.optimization_barrier(
            (others, column, own_beside, query_rows)
        )
        others_beside = lax.ppermute(others, "width", swap)
        far = [
            lax.ppermute(column, "frame", [(2, 1), (1, 2)]),
            lax.ppermute(column, ("frame", "width"), cross),
        ]
        blocks = [column, own_beside, others_beside, *far]
        layout = (1, 1, 1, 2)
        targets = ((0, 0), (1, 0), (1, 1), (2, 0))
        column_tiles, kinds = 1 + others.shape[0], 3
    else:
        query_rows_late = query_rows
        column = jnp.stack([own] + fetch(own, "height"))
        beside = fetch(column, "width")
        everything = jnp.concatenate([column] + beside, axis=0)
        far = [
            lax.ppermute(everything[:, :, : tile // 2], "frame", [(2, 0), (1, 3)]),
            lax.ppermute(everything[:, :, tile // 2 :], "frame", [(2, 1), (1, 2)]),
        ]
        blocks = [column] + beside + far
        layout = (1,) * (1 + len(beside)) + (2,)
        targets = tuple((k, 0) for k in range(len(layout)))
        column_tiles, kinds = column.shape[0], len(layout)
    queries_other = flip(query_rows_late, ("frame",), (1,))
    payload, grads_half, grad_rows, both_queries = kernel_call(
        token_kernel,
        (place, query_rows, queries_other, grads, out_weight),
        (
            shaped(tile, half + head_dim),
            shaped(tile, half),
            shaped(tile, head_dim),
            shaped(2 * tile, head_dim),
        ),
        cost=cost_of(2 * tile * head_dim * model_dim, 4 * tile * model_dim),
    )
    grad_shapes = [(column_tiles, 2, tile, head_dim)] * (kinds - 1)
    grad_shapes.append((column_tiles, 2, tile, head_dim) if small else far[0].shape)
    key_count = sum(shape[0] * shape[2] for shape in grad_shapes)
    product = 2 * key_count * 2 * tile * head_dim
    moved = sum(b.size * 2 for b in blocks)

    def forward(operands, groups, carried):
        keys, start = 0, 0
        for count in groups:
            keys += operands[start].shape[0] * operands[start].shape[2]
            start += count
        return pl.pallas_call(
            functools.partial(forward_kernel, inv_root, groups, bool(carried)),
            out_shape=shaped(head_dim + STAT_ROWS, 2 * tile, kind=jnp.float32),
            in_specs=[VMEM] * (1 + len(operands) + len(carried)),
            out_specs=VMEM,
            scratch_shapes=[pltpu.VMEM((keys, 2 * tile), jnp.float32)],
            compiler_params=PARAMS,
            cost_estimate=cost_of(5 * 10**9 if carried else 10**8, 10**6),
        )(both_queries, *operands, *carried)

    partial = forward(blocks[:1], (1,), ())
    payload, partial = lax.optimization_barrier((payload, partial))
    payload = flip(payload, ("frame",), (1,))
    partial = forward(blocks[1:], layout[1:], (partial,))
    partial_other = flip(partial, ("frame",), (1,))
    plane = 4
    chunks = plane if small else 0
    merged = kernel_call(
        functools.partial(merge_kernel, 1.0 / float(math.prod(extents)), plane),
        (place, partial, partial_other, payload, grads_half, grad_rows),
        (
            shaped(STAT_ROWS, 2 * tile, kind=jnp.float32),
            shaped(tile, head_dim),
            *[shaped(head_dim // plane, half)] * chunks,
        ),
        scratch=(
            pltpu.VMEM((2 * tile, head_dim), jnp.bfloat16),
            pltpu.VMEM((2 * tile, head_dim), jnp.bfloat16),
            pltpu.VMEM((head_dim, half), jnp.float32),
        ),
        cost=cost_of(4 * tile * head_dim * half, 4 * tile * model_dim),
    )
    stats, attended, *terms = merged
    *near_grads, far_grad, query_grad = kernel_call(
        functools.partial(backward_kernel, inv_root, layout, targets),
        (place, stats, both_queries, payload, grad_rows, *blocks),
        (
            shaped(*grad_shapes[0], kind=jnp.float32),
            *[shaped(*shape) for shape in grad_shapes[1:]],
            shaped(head_dim, 2 * tile, kind=jnp.float32),
        ),
        scratch=(pltpu.VMEM((2 * tile, head_dim), jnp.bfloat16),),
        cost=cost_of(5 * product, 2 * moved),
    )
    if small:
        terms[0], query_grad = lax.optimization_barrier((terms[0], query_grad))
        part = sum_over_plane(terms)
        part, query_grad = lax.optimization_barrier((part, query_grad))
    query_own, query_other = kernel_call(
        functools.partial(query_kernel, inv_root),
        (place, query_grad),
        (
            shaped(tile, head_dim, kind=jnp.float32),
            shaped(tile * head_dim // half, half),
        ),
        scratch=(pltpu.VMEM((2 * tile, head_dim), jnp.float32),),
        cost=cost_of(10**10, 10**8),
    )
    if small:
        far_grad, query_own = lax.optimization_barrier((far_grad, query_own))
    back = (*near_grads, far_grad, query_own, query_other)
    if small:
        other = flip(part, ("height",), (1,))
        part = (part.astype(jnp.float32) + other.astype(jnp.float32)).astype(jnp.bfloat16)
        part, attended = lax.optimization_barrier((part, attended))
        other = flip(part, ("height",), (2,))
    else:
        weight_term = jnp.einsum("td,tm->dm", attended, grads, preferred_element_type=jnp.float32)
        grad_out_weight = lax.psum(weight_term, AXES) / float(math.prod(extents))
    projected = (
        jnp.dot(attended, out_weight, preferred_element_type=jnp.float32)
        .astype(jnp.bfloat16)
        .reshape(projected_grad.shape)
    )
    column_grad, *beside_grads, far_grad, query_own, query_other = back
    if small:
        arrived = [
            lax.ppermute(beside_grads[0], "width", [(0, 1), (1, 0)]),
            lax.ppermute(far_grad, "frame", [(1, 2), (2, 1)]),
            lax.ppermute(far_grad, ("frame", "width"), [(p, s) for s, p in cross]),
        ]
        other, projected = lax.optimization_barrier((other, projected))
        part = (part.astype(jnp.float32) + other.astype(jnp.float32)).astype(jnp.bfloat16)
        part, column_grad = lax.optimization_barrier((part, column_grad))
        part = [part] + [flip(part, ("frame", "width"), bit) for bit in PLANE_BITS[1:]]
        shape = column_grad.shape[1:]
        pieces = pl.pallas_call(
            combine_kernel,
            out_shape=[shaped(*shape, kind=jnp.float32)] + [shaped(*shape)] * (column_tiles - 1),
            in_specs=[VMEM] * 4,
            out_specs=[VMEM] * column_tiles,
            compiler_params=PARAMS,
        )(column_grad, *arrived)
        pieces = list(pieces)
    else:
        arrived = jnp.concatenate(
            (
                lax.ppermute(far_grad, "frame", [(0, 2), (3, 1)]),
                lax.ppermute(far_grad, "frame", [(1, 2), (2, 1)]),
            ),
            axis=2,
        ).astype(jnp.float32)
        pieces = [column_grad] + [b.astype(jnp.float32) for b in beside_grads]
        span = column_tiles
        pieces = [p + arrived[i * span : (i + 1) * span] for i, p in enumerate(pieces)]
        column_grad = give_back(pieces, "width")
        pieces = [column_grad[k] for k in range(column_tiles)]
    if small:
        whole, finish = join_sum(part, query_own, query_other, place)
        grad_out_weight, grad_query = finish(whole)
        grad_out_weight, pieces[0] = lax.optimization_barrier((grad_out_weight, pieces[0]))
    else:
        query_other = flip(query_other, ("frame",), (1,)).reshape(-1, half // head_dim, head_dim)
        query_other = query_other.transpose(1, 0, 2).reshape(tile, head_dim)
        grad_query = (query_own + query_other.astype(jnp.float32)).astype(jnp.bfloat16)
    operands = (pieces[0], *returned(pieces[1:], "height"))
    grad_key, grad_value = pl.pallas_call(
        owner_kernel,
        out_shape=[shaped(tile, head_dim)] * 2,
        in_specs=[VMEM] * len(operands),
        out_specs=[VMEM] * 2,
        compiler_params=PARAMS,
        cost_estimate=cost_of(10**10, 10**8),
    )(*operands)
    grad_key = grad_key.reshape(key_vectors.shape)
    grad_value = grad_value.reshape(value_vectors.shape)
    grad_query = grad_query.reshape(queries.shape)
    return (projected, grad_query, grad_key, grad_value, grad_out_weight)


def solution(mesh):
    tokens = P("frame", "height", "width", None)
    return jax.shard_map(
        body,
        mesh=mesh,
        in_specs=(tokens, tokens, tokens, P(), tokens),
        out_specs=(tokens, tokens, tokens, tokens, P()),
        check_vma=False,
    )
```

```python
import functools
import math

import jax
import jax.numpy as jnp
from jax import lax
from jax.experimental import pallas as pl
from jax.experimental.pallas import tpu as pltpu
from jax.sharding import PartitionSpec as P

AXES = ("frame", "height", "width")
VMEM = pl.BlockSpec(memory_space=pltpu.VMEM)
SMEM = pl.BlockSpec(memory_space=pltpu.SMEM)
PARAMS = pltpu.CompilerParams(vmem_limit_bytes=24 * 1024 * 1024)
STAT_ROWS = 8
FREE = pl.CostEstimate(flops=0, bytes_accessed=0, transcendentals=0)


def window_of(position, extent):
    span = min(3, extent)
    start = max(0, min(position - 1, extent - 3))
    return range(start, start + span)


def routes_of(extent):
    first = [(p ^ 1, p) for p in range(extent) if (p ^ 1) in window_of(p, extent)]
    if extent > 4:
        first = [(p + 1, p) for p in range(extent - 1)]
    wanted = [(s, p) for p in range(extent) for s in window_of(p, extent) if s != p]
    wanted.sort(key=lambda pair: (pair[0] ^ pair[1], pair))
    routes = [first]
    for pair in wanted:
        if pair in first:
            continue
        for route in routes[1:]:
            if all(pair[0] != s and pair[1] != p for s, p in route):
                route.append(pair)
                break
        else:
            routes.append([pair])
    return [route for route in routes if route]


def slots_of(extent):
    routes = routes_of(extent)
    arrivals = [[c for c, r in enumerate(routes) if any(q == p for _, q in r)] for p in range(extent)]
    return [[arrivals[p][k] for p in range(extent)] for k in range(min(3, extent) - 1)]


def chosen(options, choice, axis):
    value = options[choice[0]]
    position = lax.axis_index(axis)
    for option in sorted(set(choice)):
        if option != choice[0]:
            here = functools.reduce(
                jnp.logical_or, [position == p for p, c in enumerate(choice) if c == option]
            )
            value = jnp.where(here, options[option], value)
    return value


def fetch(block, axis):
    extent = lax.axis_size(axis)
    routes = routes_of(extent)
    arrived = [lax.ppermute(block, axis, route) for route in routes]
    tiles = []
    for slot in slots_of(extent):
        used = sorted(set(slot))
        reached = sum(len(routes[c]) for c in used)
        if reached == extent:
            tiles.append(functools.reduce(jnp.add, [arrived[c] for c in used]))
        else:
            tiles.append(chosen(arrived, slot, axis))
    return tiles


def returned(pieces, axis):
    extent = lax.axis_size(axis)
    slots = slots_of(extent)
    arrived = []
    order = (0, 2, 1) if extent == 4 else range(len(routes_of(extent)))
    for c, route in ((c, routes_of(extent)[c]) for c in order):
        holders = [next((k for k in range(len(slots)) if slots[k][p] == c), None) for p in range(extent)]
        used = sorted({k for k in holders if k is not None})
        choice = [k if k is not None else used[0] for k in holders]
        outgoing = chosen({k: pieces[k] for k in used}, choice, axis).astype(jnp.bfloat16)
        arrived.append(lax.ppermute(outgoing, axis, [(p, s) for s, p in route]))
    return arrived


def give_back(pieces, axis):
    arrived = returned(pieces[1:], axis)
    return functools.reduce(jnp.add, [pieces[0]] + [a.astype(jnp.float32) for a in arrived])


def flip(block, axes, bits):
    sizes = [lax.axis_size(axis) for axis in axes]
    route = []
    for flat in range(math.prod(sizes)):
        rest, target, scale = flat, 0, 1
        for size, bit in zip(reversed(sizes), reversed(bits)):
            target += ((rest % size) ^ bit) * scale
            rest //= size
            scale *= size
        route.append((flat, target))
    return lax.ppermute(block, axes, route)


def rows_of(refs, part):
    block = refs[0][:, part]
    for ref in refs[1:]:
        block = block + ref[:, part]
    return block.reshape(-1, block.shape[-1])


def token_kernel(
    place, queries, queries_other, grads, weight, payload, grads_half, grad_rows, both_queries
):
    half = grads_half.shape[1]
    product = lax.dot_general(
        grads[...], weight[...], (((1,), (1,)), ((), ())), preferred_element_type=jnp.float32
    ).astype(jnp.bfloat16)
    grad_rows[...] = product
    payload[:, half:] = product
    payload[:, :half] = grads[:, pl.ds(pl.multiple_of((1 - place[0]) * half, half), half)]
    grads_half[...] = grads[:, pl.ds(pl.multiple_of(place[0] * half, half), half)]
    both_tiles(place, queries[...], queries_other[...], both_queries)


def both_tiles(place, mine, theirs, both):
    tile = mine.shape[0]
    both[pl.ds(pl.multiple_of(place[0] * tile, tile), tile), :] = mine
    both[pl.ds(pl.multiple_of((1 - place[0]) * tile, tile), tile), :] = theirs


def forward_kernel(inv_root, layout, carried, both_queries, *refs):
    groups, rest = split_groups(layout, refs)
    partial, scores = rest[-2:]
    dim = both_queries.shape[1]
    query_rows = both_queries[...]
    top, start, spans = None, 0, []
    if carried:
        top = rest[0][dim : dim + 1, :]
    for group in groups:
        keys = rows_of(group, 0)
        piece = lax.dot_general(
            keys, query_rows, (((1,), (1,)), ((), ())), preferred_element_type=jnp.float32
        )
        scores[start : start + keys.shape[0], :] = piece
        spans.append((start, keys.shape[0]))
        start += keys.shape[0]
        piece_top = jnp.max(piece, axis=0, keepdims=True) * inv_root
        top = piece_top if top is None else jnp.maximum(top, piece_top)
    if carried:
        share = jnp.exp(rest[0][dim : dim + 1, :] - top)
        total = rest[0][dim + 1 : dim + 2, :] * share
        mixed = rest[0][:dim, :] * share
    else:
        total = jnp.zeros_like(top)
        mixed = jnp.zeros((dim, query_rows.shape[0]), jnp.float32)
    for group, (start, count) in zip(groups, spans):
        weights = jnp.exp(scores[start : start + count, :] * inv_root - top)
        total = total + jnp.sum(weights, axis=0, keepdims=True)
        mixed = mixed + lax.dot_general(
            rows_of(group, 1),
            weights.astype(jnp.bfloat16),
            (((0,), (0,)), ((), ())),
            preferred_element_type=jnp.float32,
        )
    partial[:dim, :] = mixed
    row = lax.broadcasted_iota(jnp.int32, (STAT_ROWS, query_rows.shape[0]), 0)
    partial[dim:, :] = jnp.where(row == 0, top, total)


def merge_kernel(scale, plane, place, mine, theirs, payload, grads_half, grad_rows, *refs):
    stats, attended_own, terms, both_grads, both_attended, term_rows = (
        refs[0],
        refs[1],
        refs[2:-3],
        refs[-3],
        refs[-2],
        refs[-1],
    )
    tile, dim = grad_rows.shape
    half = grads_half.shape[1]
    top_a, top_b = mine[dim : dim + 1, :], theirs[dim : dim + 1, :]
    sum_a, sum_b = mine[dim + 1 : dim + 2, :], theirs[dim + 1 : dim + 2, :]
    top = jnp.maximum(top_a, top_b)
    share_a, share_b = jnp.exp(top_a - top), jnp.exp(top_b - top)
    total = share_a * sum_a + share_b * sum_b
    mixed = mine[:dim, :] * (share_a / total) + theirs[:dim, :] * (share_b / total)
    attended_t = mixed.astype(jnp.bfloat16).astype(jnp.float32)
    both_tiles(place, grad_rows[...], payload[:, half:], both_grads)
    row_dot = jnp.sum(both_grads[...].astype(jnp.float32).T * attended_t, axis=0, keepdims=True)
    row = lax.broadcasted_iota(jnp.int32, (STAT_ROWS, mixed.shape[1]), 0)
    stats[...] = jnp.where(row == 0, top + jnp.log(total), row_dot)
    both_attended[...] = attended_t.T.astype(jnp.bfloat16)
    rows_mine = both_attended[pl.ds(pl.multiple_of(place[0] * tile, tile), tile), :]
    rows_theirs = both_attended[pl.ds(pl.multiple_of((1 - place[0]) * tile, tile), tile), :]
    attended_own[...] = rows_mine
    if not terms:
        return
    contract = (((0,), (0,)), ((), ()))
    term = lax.dot_general(
        rows_mine, grads_half[...], contract, preferred_element_type=jnp.float32
    )
    term = term + lax.dot_general(
        rows_theirs, payload[:, :half], contract, preferred_element_type=jnp.float32
    )
    term_rows[...] = term * scale
    count = dim // plane
    for order, out in enumerate(terms):
        chunk = place[1] ^ order
        out[...] = term_rows[pl.ds(pl.multiple_of(chunk * count, count), count), :].astype(jnp.bfloat16)


def split_groups(layout, refs):
    groups, start = [], 0
    for count in layout:
        groups.append(refs[start : start + count])
        start += count
    return groups, refs[start:]


def backward_kernel(
    inv_root, layout, targets, place, stats, both_queries, payload, grad_rows, *refs
):
    groups, rest = split_groups(layout, refs)
    count = 1 + max(out for out, _ in targets)
    outs, rest = rest[:count], rest[count:]
    both_grads = rest[-1]
    tile, dim = grad_rows.shape
    columns = payload.shape[1]
    both_tiles(place, grad_rows[...], payload[:, columns - dim :], both_grads)
    query_rows, out_grads = both_queries[...], both_grads[...]
    level, row_dot = stats[0:1, :], stats[1:2, :]
    along = (((1,), (1,)), ((), ()))
    query_grad = jnp.zeros((dim, 2 * tile), jnp.float32)
    for group, (target, first) in zip(groups, targets):
        out, tiles = outs[target], group[0].shape[0]
        keys, values = rows_of(group, 0), rows_of(group, 1)
        scores = lax.dot_general(keys, query_rows, along, preferred_element_type=jnp.float32)
        probability = jnp.exp(scores * inv_root - level)
        prob_grad = lax.dot_general(values, out_grads, along, preferred_element_type=jnp.float32)
        score_grad = (probability * (prob_grad - row_dot)).astype(jnp.bfloat16)
        shape = (tiles,) + out.shape[2:]
        key_grad = jnp.dot(score_grad, query_rows, preferred_element_type=jnp.float32) * inv_root
        value_grad = jnp.dot(
            probability.astype(jnp.bfloat16), out_grads, preferred_element_type=jnp.float32
        )
        out[first : first + tiles, 0] = key_grad.reshape(shape).astype(out.dtype)
        out[first : first + tiles, 1] = value_grad.reshape(shape).astype(out.dtype)
        query_grad = query_grad + lax.dot_general(
            keys, score_grad, (((0,), (0,)), ((), ())), preferred_element_type=jnp.float32
        )
    rest[0][...] = query_grad


def query_kernel(inv_root, place, query_grad, query_own, query_other, both_out):
    tile, dim = query_own.shape
    both_out[...] = query_grad[...].T * inv_root
    query_own[...] = both_out[pl.ds(pl.multiple_of(place[0] * tile, tile), tile), :]
    other = both_out[pl.ds(pl.multiple_of((1 - place[0]) * tile, tile), tile), :]
    other = other.astype(jnp.bfloat16)
    rows = query_other.shape[0]
    for block in range(tile // rows):
        query_other[:, block * dim : (block + 1) * dim] = other[block * rows : (block + 1) * rows]


def assemble_kernel(flipped, rows, place, part, *refs):
    rows_ref, done = refs[-2:]
    count, width = rows_ref.shape
    copies = []
    if flipped:
        query_own, _, whole, grad_query, sums = refs[:-2]
        dim, step = query_own.shape[1], part.shape[0] - count
        for block in range(width // dim):
            piece = part[count:, block * dim : (block + 1) * dim].astype(jnp.float32)
            span = slice(block * step, (block + 1) * step)
            sums[span, :] = (query_own[span, :] + piece).astype(jnp.bfloat16)
        copies.append(pltpu.make_async_copy(sums, grad_query, done.at[count // rows]))
        copies[-1].start()
    else:
        whole = refs[0]
    core = 1 - place[0] if flipped else place[0]
    columns = pl.ds(pl.multiple_of(core * width, width), width)
    for order in range(count // rows):
        span = pl.ds(pl.multiple_of((place[1] ^ order) * rows, rows), rows)
        rows_ref[span, :] = part[order * rows : (order + 1) * rows, :].astype(jnp.float32)
        copies.append(
            pltpu.make_async_copy(rows_ref.at[span, :], whole.at[span, columns], done.at[order])
        )
        copies[-1].start()
    for copy in copies:
        copy.wait()


def assemble(flipped, place, part, rows, shape, whole=None, query_own=None):
    anywhere = pl.BlockSpec(memory_space=pl.ANY)
    outs, out_specs, operands, in_specs = shape, anywhere, (place, part), [SMEM, VMEM]
    scratch = [
        pltpu.VMEM((shape.shape[0], part.shape[1]), jnp.float32),
        pltpu.SemaphoreType.DMA((shape.shape[0] // rows + flipped,)),
    ]
    if flipped:
        outs, out_specs = (shape, shaped(*query_own.shape)), (anywhere, anywhere)
        operands, in_specs = operands + (query_own, whole), in_specs + [VMEM, anywhere]
        scratch = [pltpu.VMEM(query_own.shape, jnp.bfloat16)] + scratch
    return pl.pallas_call(
        functools.partial(assemble_kernel, flipped, rows),
        out_shape=outs,
        in_specs=in_specs,
        out_specs=out_specs,
        scratch_shapes=scratch,
        input_output_aliases={3: 0} if flipped else {},
        compiler_params=PARAMS,
        cost_estimate=cost_of(10**10, 10**8),
    )(*operands)


def owner_kernel(own_grad, *refs):
    arrived, (key_out, value_out, sums, done) = refs[:-4], refs[-4:]
    copies = []
    for k, out in enumerate((key_out, value_out)):
        total = own_grad[k]
        for block in arrived:
            total = total + block[k].astype(jnp.float32)
        sums[k] = total.astype(jnp.bfloat16)
        copies.append(pltpu.make_async_copy(sums.at[k], out, done.at[k]))
        copies[-1].start()
    for copy in copies:
        copy.wait()


def pack_kernel(*refs):
    start = 0
    for piece in refs[:-1]:
        refs[-1][start : start + piece.shape[0], :] = piece[...]
        start += piece.shape[0]


def combine_kernel(column, *refs):
    arrived, pieces = refs[: -column.shape[0]], refs[-column.shape[0] :]
    for k, piece in enumerate(pieces):
        total = column[k]
        for block in arrived:
            total = total + block[k].astype(jnp.float32)
        piece[...] = total.astype(piece.dtype)


def shaped(*shape, kind=jnp.bfloat16):
    return jax.ShapeDtypeStruct(shape, kind)


def kernel_call(kernel, operands, outs, scratch=(), cost=None):
    many = isinstance(outs, (list, tuple))
    return pl.pallas_call(
        kernel,
        out_shape=outs,
        in_specs=[SMEM] + [VMEM] * (len(operands) - 1),
        out_specs=[VMEM] * len(outs) if many else VMEM,
        scratch_shapes=list(scratch),
        compiler_params=PARAMS,
        cost_estimate=cost,
    )(*operands)


def cost_of(flops, moved):
    return pl.CostEstimate(flops=int(flops), bytes_accessed=int(moved), transcendentals=0)


PLANE_BITS = ((0, 0), (0, 1), (2, 0), (2, 1))


def sum_over_plane(terms):
    summed = terms[0].astype(jnp.float32)
    for term, bit in zip(terms[1:], PLANE_BITS[1:]):
        summed = summed + flip(term, ("frame", "width"), bit).astype(jnp.float32)
    return summed.astype(jnp.bfloat16)


def join_sum(part, query_own, query_other, place):
    plane = len(part)
    pieces = part + [query_other]
    part = pl.pallas_call(
        pack_kernel,
        out_shape=shaped(sum(p.shape[0] for p in pieces), pieces[0].shape[1]),
        in_specs=[VMEM] * len(pieces),
        out_specs=VMEM,
        compiler_params=PARAMS,
    )(*pieces)
    other = flip(part, ("frame",), (1,))
    rows = (part.shape[0] - query_other.shape[0]) // plane
    shape = shaped(plane * rows, 2 * part.shape[1], kind=jnp.float32)
    whole = assemble(False, place, part, rows, shape)
    return whole, lambda whole: assemble(True, place, other, rows, shape, whole, query_own)


def body(queries, key_vectors, value_vectors, out_weight, projected_grad):
    head_dim = queries.shape[-1]
    model_dim = out_weight.shape[1]
    half = model_dim // 2
    inv_root = 1.0 / math.sqrt(head_dim)
    extents = tuple(lax.axis_size(axis) for axis in AXES)
    assert extents[0] == 4
    small = extents[1:] == (4, 2)
    frame, height, width = (lax.axis_index(axis) for axis in AXES)
    core = frame % 2
    place = jnp.stack([core, (frame // 2) * 2 + width, height]).astype(jnp.int32)
    query_rows = queries.reshape(-1, head_dim)
    grads = projected_grad.reshape(-1, model_dim)
    tile = query_rows.shape[0]

    own = jnp.stack((key_vectors.reshape(tile, head_dim), value_vectors.reshape(tile, head_dim)))
    cross = [(2 * s + y, 2 * p + 1 - y) for s, p in ((2, 0), (1, 3)) for y in (0, 1)]

    if small:
        swap = [(0, 1), (1, 0)]
        tiles = fetch(own, "height")
        own_beside = lax.ppermute(own[None], "width", swap)
        others = jnp.stack(tiles)
        column = jnp.stack([own] + tiles)
        others, column, own_beside, query_rows_late = lax.optimization_barrier(
            (others, column, own_beside, query_rows)
        )
        others_beside = lax.ppermute(others, "width", swap)
        far = [
            lax.ppermute(column, "frame", [(2, 1), (1, 2)]),
            lax.ppermute(column, ("frame", "width"), cross),
        ]
        blocks = [column, own_beside, others_beside, *far]
        layout = (1, 1, 1, 2)
        targets = ((0, 0), (1, 0), (1, 1), (2, 0))
        column_tiles, kinds = 1 + others.shape[0], 3
    else:
        query_rows_late = query_rows
        column = jnp.stack([own] + fetch(own, "height"))
        beside = fetch(column, "width")
        everything = jnp.concatenate([column] + beside, axis=0)
        far = [
            lax.ppermute(everything[:, :, : tile // 2], "frame", [(2, 0), (1, 3)]),
            lax.ppermute(everything[:, :, tile // 2 :], "frame", [(2, 1), (1, 2)]),
        ]
        blocks = [column] + beside + far
        layout = (1,) * (1 + len(beside)) + (2,)
        targets = tuple((k, 0) for k in range(len(layout)))
        column_tiles, kinds = column.shape[0], len(layout)
    queries_other = flip(query_rows_late, ("frame",), (1,))
    payload, grads_half, grad_rows, both_queries = kernel_call(
        token_kernel,
        (place, query_rows, queries_other, grads, out_weight),
        (
            shaped(tile, half + head_dim),
            shaped(tile, half),
            shaped(tile, head_dim),
            shaped(2 * tile, head_dim),
        ),
        cost=cost_of(2 * tile * head_dim * model_dim, 4 * tile * model_dim),
    )
    grad_shapes = [(column_tiles, 2, tile, head_dim)] * (kinds - 1)
    grad_shapes.append((column_tiles, 2, tile, head_dim) if small else far[0].shape)
    key_count = sum(shape[0] * shape[2] for shape in grad_shapes)
    product = 2 * key_count * 2 * tile * head_dim
    moved = sum(b.size * 2 for b in blocks)

    def forward(operands, groups, carried):
        keys, start = 0, 0
        for count in groups:
            keys += operands[start].shape[0] * operands[start].shape[2]
            start += count
        return pl.pallas_call(
            functools.partial(forward_kernel, inv_root, groups, bool(carried)),
            out_shape=shaped(head_dim + STAT_ROWS, 2 * tile, kind=jnp.float32),
            in_specs=[VMEM] * (1 + len(operands) + len(carried)),
            out_specs=VMEM,
            scratch_shapes=[pltpu.VMEM((keys, 2 * tile), jnp.float32)],
            compiler_params=PARAMS,
            cost_estimate=cost_of(5 * 10**9 if carried else 10**8, 10**6),
        )(both_queries, *operands, *carried)

    partial = forward(blocks[:1], (1,), ())
    payload, partial = lax.optimization_barrier((payload, partial))
    payload = flip(payload, ("frame",), (1,))
    partial = forward(blocks[1:], layout[1:], (partial,))
    partial_other = flip(partial, ("frame",), (1,))
    plane = 4
    chunks = plane if small else 0
    merged = kernel_call(
        functools.partial(merge_kernel, 1.0 / float(math.prod(extents)), plane),
        (place, partial, partial_other, payload, grads_half, grad_rows),
        (
            shaped(STAT_ROWS, 2 * tile, kind=jnp.float32),
            shaped(tile, head_dim),
            *[shaped(head_dim // plane, half)] * chunks,
        ),
        scratch=(
            pltpu.VMEM((2 * tile, head_dim), jnp.bfloat16),
            pltpu.VMEM((2 * tile, head_dim), jnp.bfloat16),
            pltpu.VMEM((head_dim, half), jnp.float32),
        ),
        cost=cost_of(4 * tile * head_dim * half, 4 * tile * model_dim),
    )
    stats, attended, *terms = merged
    *near_grads, far_grad, query_grad = kernel_call(
        functools.partial(backward_kernel, inv_root, layout, targets),
        (place, stats, both_queries, payload, grad_rows, *blocks),
        (
            shaped(*grad_shapes[0], kind=jnp.float32),
            *[shaped(*shape) for shape in grad_shapes[1:]],
            shaped(head_dim, 2 * tile, kind=jnp.float32),
        ),
        scratch=(pltpu.VMEM((2 * tile, head_dim), jnp.bfloat16),),
        cost=cost_of(5 * product, 2 * moved),
    )
    if small:
        terms[0], query_grad = lax.optimization_barrier((terms[0], query_grad))
        part = sum_over_plane(terms)
        part, query_grad = lax.optimization_barrier((part, query_grad))
    query_own, query_other = kernel_call(
        functools.partial(query_kernel, inv_root),
        (place, query_grad),
        (
            shaped(tile, head_dim, kind=jnp.float32),
            shaped(tile * head_dim // half, half),
        ),
        scratch=(pltpu.VMEM((2 * tile, head_dim), jnp.float32),),
        cost=cost_of(10**10, 10**8),
    )
    if small:
        far_grad, query_own = lax.optimization_barrier((far_grad, query_own))
    back = (*near_grads, far_grad, query_own, query_other)
    if small:
        other = flip(part, ("height",), (1,))
        part = (part.astype(jnp.float32) + other.astype(jnp.float32)).astype(jnp.bfloat16)
        part, attended = lax.optimization_barrier((part, attended))
        other = flip(part, ("height",), (2,))
    else:
        weight_term = jnp.einsum("td,tm->dm", attended, grads, preferred_element_type=jnp.float32)
        grad_out_weight = lax.psum(weight_term, AXES) / float(math.prod(extents))
    projected = (
        jnp.dot(attended, out_weight, preferred_element_type=jnp.float32)
        .astype(jnp.bfloat16)
        .reshape(projected_grad.shape)
    )
    column_grad, *beside_grads, far_grad, query_own, query_other = back
    if small:
        arrived = [
            lax.ppermute(beside_grads[0], "width", [(0, 1), (1, 0)]),
            lax.ppermute(far_grad, "frame", [(1, 2), (2, 1)]),
            lax.ppermute(far_grad, ("frame", "width"), [(p, s) for s, p in cross]),
        ]
        other, projected = lax.optimization_barrier((other, projected))
        part = (part.astype(jnp.float32) + other.astype(jnp.float32)).astype(jnp.bfloat16)
        part, column_grad = lax.optimization_barrier((part, column_grad))
        part = [part] + [flip(part, ("frame", "width"), bit) for bit in PLANE_BITS[1:]]
        shape = column_grad.shape[1:]
        pieces = pl.pallas_call(
            combine_kernel,
            out_shape=[shaped(*shape, kind=jnp.float32)] + [shaped(*shape)] * (column_tiles - 1),
            in_specs=[VMEM] * 4,
            out_specs=[VMEM] * column_tiles,
            compiler_params=PARAMS,
        )(column_grad, *arrived)
        pieces = list(pieces)
    else:
        arrived = jnp.concatenate(
            (
                lax.ppermute(far_grad, "frame", [(0, 2), (3, 1)]),
                lax.ppermute(far_grad, "frame", [(1, 2), (2, 1)]),
            ),
            axis=2,
        ).astype(jnp.float32)
        pieces = [column_grad] + [b.astype(jnp.float32) for b in beside_grads]
        span = column_tiles
        pieces = [p + arrived[i * span : (i + 1) * span] for i, p in enumerate(pieces)]
        column_grad = give_back(pieces, "width")
        pieces = [column_grad[k] for k in range(column_tiles)]
    if small:
        whole, finish = join_sum(part, query_own, query_other, place)
        grad_out_weight, grad_query = finish(whole)
        grad_out_weight, pieces[0] = lax.optimization_barrier((grad_out_weight, pieces[0]))
    else:
        query_other = flip(query_other, ("frame",), (1,)).reshape(-1, half // head_dim, head_dim)
        query_other = query_other.transpose(1, 0, 2).reshape(tile, head_dim)
        grad_query = (query_own + query_other.astype(jnp.float32)).astype(jnp.bfloat16)
    operands = (pieces[0], *returned(pieces[1:], "height"))
    grad_key, grad_value = pl.pallas_call(
        owner_kernel,
        out_shape=[shaped(tile, head_dim)] * 2,
        in_specs=[VMEM] * len(operands),
        out_specs=[pl.BlockSpec(memory_space=pl.ANY)] * 2,
        scratch_shapes=[
            pltpu.VMEM((2, tile, head_dim), jnp.bfloat16),
            pltpu.SemaphoreType.DMA((2,)),
        ],
        compiler_params=PARAMS,
        cost_estimate=cost_of(10**10, 10**8),
    )(*operands)
    grad_key = grad_key.reshape(key_vectors.shape)
    grad_value = grad_value.reshape(value_vectors.shape)
    grad_query = grad_query.reshape(queries.shape)
    return (projected, grad_query, grad_key, grad_value, grad_out_weight)


def solution(mesh):
    tokens = P("frame", "height", "width", None)
    return jax.shard_map(
        body,
        mesh=mesh,
        in_specs=(tokens, tokens, tokens, P(), tokens),
        out_specs=(tokens, tokens, tokens, tokens, P()),
        check_vma=False,
    )
```
